32 devices in a mesh: dp: 16 (over z, y, core), tensor: 2 (over x).
Axes of the slice: x: 2, y: 2, z: 4, core: 2. Of those that a mesh axis runs over, the one named last changes fastest.
Arguments:
- tokens_in: bfloat16 [2, 16, 4, 512, 1024], P(None, 'dp', None, 'tensor'), may hold values from -6 to 6
- piece_starts: int32 [2, 16, 2], P(None, 'dp'), may hold values from 0 to 1792, as said below
- cotangent: bfloat16 [2, 16, 4, 512, 1024], P(None, 'dp', None, 'tensor'), may hold values from -6 to 6
- gain_tokens: bfloat16 [1024], P('dp'), may hold values from 0.099609375 to 1.8984375
- gain_mlp: bfloat16 [1024], P('dp'), may hold values from 0.099609375 to 1.8984375
- gain_state: bfloat16 [1024], P('dp'), may hold values from 0.099609375 to 1.8984375
- gate_bias: bfloat16 [1024], P('dp'), may hold values from -2 to 3
- w_query: bfloat16 [1024, 1024], P('dp', 'tensor'), may hold values from -0.1875 to 0.1875
- w_key: bfloat16 [1024, 1024], P('dp', 'tensor'), may hold values from -0.1875 to 0.1875
- w_value: bfloat16 [1024, 1024], P('dp', 'tensor'), may hold values from -0.1875 to 0.1875
- w_out: bfloat16 [1024, 1024], P('tensor', 'dp'), may hold values from -3 to 3
- w_state_query: bfloat16 [1024, 1024], P('dp', 'tensor'), may hold values from -0.1875 to 0.1875
- w_state_key: bfloat16 [1024, 1024], P('dp', 'tensor'), may hold values from -0.1875 to 0.1875
- w_state_value: bfloat16 [1024, 1024], P('dp', 'tensor'), may hold values from -0.1875 to 0.1875
- w_state_out: bfloat16 [1024, 1024], P('tensor', 'dp'), may hold values from -3 to 3
- w_gate: bfloat16 [1024, 1024], P('dp', 'tensor'), may hold values from -0.1875 to 0.1875
- w_up: bfloat16 [1024, 4096], P('dp', 'tensor'), may hold values from -0.1875 to 0.1875
- w_down: bfloat16 [4096, 1024], P('tensor', 'dp'), may hold values from -0.09375 to 0.09375
- state_init: bfloat16 [512, 1024], P('dp', 'tensor'), may hold values from -6 to 6
Outputs:
- output: bfloat16 [2, 16, 4, 512, 1024], P(None, 'dp', None, 'tensor')
- grad_tokens: bfloat16 [2, 16, 4, 512, 1024], P(None, 'dp', None, 'tensor')
- grad_gain_tokens: float32 [1024], P('dp')
- grad_gain_mlp: float32 [1024], P('dp')
- grad_gain_state: float32 [1024], P('dp')
- grad_gate_bias: float32 [1024], P('dp')
- grad_w_query: float32 [1024, 1024], P('dp', 'tensor')
- grad_w_key: float32 [1024, 1024], P('dp', 'tensor')
- grad_w_value: float32 [1024, 1024], P('dp', 'tensor')
- grad_w_out: float32 [1024, 1024], P('tensor', 'dp')
- grad_w_state_query: float32 [1024, 1024], P('dp', 'tensor')
- grad_w_state_key: float32 [1024, 1024], P('dp', 'tensor')
- grad_w_state_value: float32 [1024, 1024], P('dp', 'tensor')
- grad_w_state_out: float32 [1024, 1024], P('tensor', 'dp')
- grad_w_gate: float32 [1024, 1024], P('dp', 'tensor')
- grad_w_up: float32 [1024, 4096], P('dp', 'tensor')
- grad_w_down: float32 [4096, 1024], P('tensor', 'dp')
- grad_state_init: float32 [512, 1024], P('dp', 'tensor')
The draws below stay inside these ranges and needn't reach their ends.
Inputs may be any that keep to these rules, and one draw needn't show every extreme that they name: `piece_starts`: each sequence has 2 distinct picture pieces; every start is a multiple of 256.
All inputs are finite; a program needn't handle non-finite values.
Results may differ from the reference program's by a relative error of at most 0.025.
Values may be sent and summed in bfloat16 or wider, within the bound.
No kernel may reach another device: no remote copies, remote signals or barrier semaphores. Data moves between devices by JAX's collectives and lax.ppermute only.
A program may use at most 472 MiB of HBM per device.

```python
import math
import jax
import jax.numpy as jnp
from jax import lax

D = 1024
HEAD = 128
FF = 4096
W = 512
S = 512
PIECE = 256
NPIECE = 2
SEQ_LEN = 2048
MICRO = 2
NB = 4
SEQS = 16


def draw_piece_starts(key, part):
    slots = SEQ_LEN // PIECE
    count = MICRO * SEQS
    several = jax.random.split(key, count)

    def pick(one_key):
        return jax.random.permutation(one_key, slots)[:NPIECE].astype(jnp.int32)
    chosen = jax.vmap(pick)(several)
    first_key, second_key = jax.random.split(jax.random.fold_in(key, 7))
    with_end = jnp.concatenate([jnp.array([slots - 1], jnp.int32), jax.random.permutation(first_key, slots - 1)[:NPIECE - 1].astype(jnp.int32)])
    with_start = jnp.concatenate([jnp.array([0], jnp.int32), (1 + jax.random.permutation(second_key, slots - 1))[:NPIECE - 1].astype(jnp.int32)])
    chosen = chosen.at[0].set(with_end).at[count - 1].set(with_start)
    return (chosen * PIECE).reshape(MICRO, SEQS, NPIECE).astype(jnp.int32)


def levels(stream_key, extent, cuts, smallest, largest):
    def one(position, blocks):
        steps = jax.random.uniform(jax.random.fold_in(jax.random.fold_in(stream_key, 6), position), (blocks,), jnp.float32, smallest / len(cuts), largest / len(cuts))
        return jnp.repeat(jnp.exp(steps), extent[position] // blocks).reshape((-1,) + (1,) * (len(extent) - position - 1))

    loudness = one(*cuts[0])
    for cut in cuts[1:]:
        loudness = loudness * one(*cut)
    return loudness


def scatter_about(own_key, extent, width, limit, pieces=(), kind=jnp.bfloat16):
    drawn = width * jax.random.normal(own_key, extent, jnp.float32)
    if pieces:
        drawn = drawn * levels(own_key, extent, pieces, -0.22, 0.18)
    return jnp.clip(drawn, -limit, limit).astype(kind)


def setup_inputs(seed: int = 0) -> dict:
    splits = jax.random.split(jax.random.key(seed), 20)
    return {
        "tokens_in": scatter_about(splits[0], (MICRO, SEQS, NB, W, D), 1.0, 6.0, ((1, 16), (3, 2))),
        "piece_starts": draw_piece_starts(jax.random.fold_in(splits[19], 71), 0),
        "cotangent": scatter_about(splits[2], (MICRO, SEQS, NB, W, D), 1.0, 6.0, ((1, 16), (3, 2))),
        "gain_tokens": jnp.clip(1.0 + 0.18 * jax.random.normal(splits[3], (D,), jnp.float32), 0.099609375, 1.8984375).astype(jnp.bfloat16),
        "gain_mlp": jnp.clip(1.0 + 0.18 * jax.random.normal(splits[4], (D,), jnp.float32), 0.099609375, 1.8984375).astype(jnp.bfloat16),
        "gain_state": jnp.clip(1.0 + 0.18 * jax.random.normal(splits[5], (D,), jnp.float32), 0.099609375, 1.8984375).astype(jnp.bfloat16),
        "gate_bias": jnp.clip(-2.0 + 5.0 * jax.random.uniform(splits[6], (D,), jnp.float32) ** levels(splits[6], (D,), ((0, 16),), -0.2, 0.2), -2.0, 3.0).astype(jnp.bfloat16),
        "w_query": scatter_about(splits[7], (D, D), D ** -0.5, 0.1875, ((0, 16), (1, 2))),
        "w_key": scatter_about(splits[8], (D, D), D ** -0.5, 0.1875, ((0, 16), (1, 2))),
        "w_value": scatter_about(splits[9], (D, D), D ** -0.5, 0.1875, ((0, 16), (1, 2))),
        "w_out": scatter_about(splits[10], (D, D), (D // W * 2) ** -0.5, 3.0, ((0, 2), (1, 16))),
        "w_state_query": scatter_about(splits[11], (D, D), D ** -0.5, 0.1875, ((0, 16), (1, 2))),
        "w_state_key": scatter_about(splits[12], (D, D), D ** -0.5, 0.1875, ((0, 16), (1, 2))),
        "w_state_value": scatter_about(splits[13], (D, D), D ** -0.5, 0.1875, ((0, 16), (1, 2))),
        "w_state_out": scatter_about(splits[14], (D, D), (D // W * 2) ** -0.5, 3.0, ((0, 2), (1, 16))),
        "w_gate": scatter_about(splits[15], (D, D), D ** -0.5, 0.1875, ((0, 16), (1, 2))),
        "w_up": scatter_about(splits[16], (D, FF), D ** -0.5, 0.1875, ((0, 16), (1, 2))),
        "w_down": scatter_about(splits[17], (FF, D), FF ** -0.5, 0.09375, ((0, 2), (1, 16))),
        "state_init": scatter_about(splits[18], (S, D), 1.0, 6.0, ((0, 16), (1, 2))),
    }


@jax.custom_vjp
def low(v):
    return lax.optimization_barrier(v.astype(jnp.bfloat16)).astype(jnp.float32)

@jax.custom_vjp
def low_back(v):
    return v

def low_keep(v):
    return (low(v), None)

def low_pass(kept, grad):
    return (grad,)

def back_keep(v):
    return (v, None)

def back_low(kept, grad):
    return (low(grad),)
low.defvjp(low_keep, low_pass)
low_back.defvjp(back_keep, back_low)
epsilon = 1e-06
masked_score = -1e+30

def hdot(left, right):
    return jnp.dot(left, right, precision=lax.Precision.HIGHEST, preferred_element_type=jnp.float32)

def rms_scale(values):
    return values * lax.rsqrt(lax.optimization_barrier(jnp.mean(values * values, axis=-1, keepdims=True)) + epsilon)

def low_pair(values):
    return low_back(low(values))

def attend(query, keys, values, allowed):
    count = query.shape[0]
    heads = query.shape[1] // HEAD
    query_heads = query.reshape(count, heads, HEAD)
    key_heads = keys.reshape(keys.shape[0], heads, HEAD)
    value_heads = values.reshape(values.shape[0], heads, HEAD)
    scores = jnp.einsum('rhe,khe->hrk', query_heads, key_heads, precision=lax.Precision.HIGHEST) * (1.0 / math.sqrt(HEAD))
    scores = low_back(scores)
    scores = jnp.where(allowed, scores, masked_score)
    weights = low(jax.nn.softmax(scores, axis=-1))
    mixed = jnp.einsum('hrk,khe->rhe', weights, value_heads, precision=lax.Precision.HIGHEST)
    return low_pair(mixed.reshape(count, heads * HEAD))

def sequence_forward(params, rows, starts):
    gain_tokens, gain_mlp, gain_state, gate_bias, w_query, w_key, w_value, w_out, w_state_query, w_state_key, w_state_value, w_state_out, w_gate, w_up, w_down, state_init = params
    positions = jnp.arange(NB * W, dtype=jnp.int32)
    inside = (positions[None, :] >= starts[:, None]) & (positions[None, :] < starts[:, None] + PIECE)
    numbers = jnp.arange(1, NPIECE + 1, dtype=jnp.int32)
    labels = lax.optimization_barrier(jnp.sum(jnp.where(inside, numbers[:, None], 0), axis=0)).astype(jnp.int32)
    local = jnp.arange(W, dtype=jnp.int32)
    causal = local[None, :] <= local[:, None]
    state = state_init
    earlier = None
    results = []
    for block in range(NB):
        block_rows = rows[block]
        own = labels[block * W:(block + 1) * W]
        together = (own[:, None] == own[None, :]) & (own[:, None] > 0)
        current = causal | together
        normed = low(rms_scale(block_rows) * gain_tokens)
        state_normed = low(rms_scale(state) * gain_state)
        query = low_pair(hdot(normed, w_query))
        key = low_pair(hdot(normed, w_key))
        value = low_pair(hdot(normed, w_value))
        state_query = low_pair(hdot(state_normed, w_state_query))
        state_key = low_pair(hdot(state_normed, w_state_key))
        state_value = low_pair(hdot(state_normed, w_state_value))
        state_ones = jnp.ones((W, S), dtype=bool)
        if earlier is None:
            token_keys = jnp.concatenate([key, state_key], axis=0)
            token_values = jnp.concatenate([value, state_value], axis=0)
            allowed = jnp.concatenate([current, state_ones], axis=1)
        else:
            token_keys = jnp.concatenate([earlier[0], key, state_key], axis=0)
            token_values = jnp.concatenate([earlier[1], value, state_value], axis=0)
            allowed = jnp.concatenate([jnp.ones((W, W), dtype=bool), current, state_ones], axis=1)
        token_mixed = attend(query, token_keys, token_values, allowed[None])
        state_mixed = attend(state_query, jnp.concatenate([key, state_key], axis=0), jnp.concatenate([value, state_value], axis=0), True)
        middle = block_rows + low_back(hdot(token_mixed, w_out))
        forget = jax.nn.sigmoid(low_back(hdot(state_normed, w_gate) + gate_bias))
        state = forget * state + (1.0 - forget) * low_back(hdot(state_mixed, w_state_out))
        mlp_in = low(rms_scale(middle) * gain_mlp)
        hidden = low_back(hdot(mlp_in, w_up))
        active = low(jax.nn.gelu(hidden))
        results.append(middle + hdot(active, w_down))
        earlier = (key, value)
    return jnp.stack(results)

def reference(tokens_in, piece_starts, cotangent, gain_tokens, gain_mlp, gain_state, gate_bias, w_query, w_key, w_value, w_out, w_state_query, w_state_key, w_state_value, w_state_out, w_gate, w_up, w_down, state_init):
    params = tuple((weight.astype(jnp.float32) for weight in (gain_tokens, gain_mlp, gain_state, gate_bias, w_query, w_key, w_value, w_out, w_state_query, w_state_key, w_state_value, w_state_out, w_gate, w_up, w_down, state_init)))
    count = MICRO * SEQS
    rows_all = tokens_in.astype(jnp.float32).reshape(count, NB, W, D)
    starts_all = piece_starts.reshape(count, NPIECE).astype(jnp.int32)

    def run(weights, rows_value):

        def single(pair):
            return sequence_forward(weights, pair[0], pair[1])
        return lax.map(jax.checkpoint(single), (rows_value, starts_all))
    result, pullback = jax.vjp(run, params, rows_all)
    grads, grad_rows = pullback(cotangent.astype(jnp.float32).reshape(count, NB, W, D))
    full_shape = tokens_in.shape
    return (result.reshape(full_shape).astype(jnp.bfloat16), grad_rows.reshape(full_shape).astype(jnp.bfloat16), grads[0], grads[1], grads[2], grads[3], grads[4], grads[5], grads[6], grads[7], grads[8], grads[9], grads[10], grads[11], grads[12], grads[13], grads[14], grads[15])
```

```python
import math

import jax
import jax.numpy as jnp
from jax import lax
from jax.experimental import pallas as pl
from jax.experimental.pallas import tpu as pltpu
from jax.sharding import PartitionSpec as P

D = 1024
HEAD = 128
W = 512
S = 512
PIECE = 256
MICRO = 2
NB = 4


epsilon = 1e-06
masked_score = -1e30


def rms_scale(values):
    return values * lax.rsqrt(jnp.mean(values * values, axis=-1, keepdims=True) + epsilon)


def normed_rows(values, gain):
    return rms_scale(values) * gain


def matmul(left, right):
    return jnp.dot(left, right, preferred_element_type=jnp.float32)


def mlp_local(full_in, full_up, full_down):
    hidden = matmul(full_in, full_up)
    active = jax.nn.gelu(hidden).astype(jnp.bfloat16)
    return (hidden, active, matmul(active, full_down))


def mlp_back_local(full_grad, active, hidden, full_in, full_down, full_up):
    grad_down_w = jnp.einsum("...f,...d->fd", active, full_grad, preferred_element_type=jnp.float32)
    grad_active = jnp.einsum(
        "...d,fd->...f", full_grad, full_down, preferred_element_type=jnp.float32
    )
    unused_value, gelu_back = jax.vjp(jax.nn.gelu, hidden)
    grad_hidden = gelu_back(grad_active)[0].astype(jnp.bfloat16)
    grad_up_w = jnp.einsum(
        "...d,...f->df", full_in, grad_hidden, preferred_element_type=jnp.float32
    )
    mlp_part = jnp.einsum("...f,df->...d", grad_hidden, full_up, preferred_element_type=jnp.float32)
    return (grad_down_w, grad_up_w, mlp_part)


def piece_labels(starts):
    positions = jnp.arange(NB * W, dtype=jnp.int32)
    inside = (positions[None, None, :] >= starts[:, :, None]) & (
        positions[None, None, :] < starts[:, :, None] + PIECE
    )
    numbers = jnp.arange(1, starts.shape[1] + 1, dtype=jnp.int32)
    return jnp.sum(jnp.where(inside, numbers[None, :, None], 0), axis=1)


def token_mask(labels, block):
    batch = labels.shape[0]
    own = labels[:, block * W : (block + 1) * W]
    local = jnp.arange(W, dtype=jnp.int32)
    causal = (local[None, :] <= local[:, None])[None]
    together = (own[:, :, None] == own[:, None, :]) & (own[:, :, None] > 0)
    current = causal | together
    earlier = jnp.full((batch, W, W), block > 0)
    state_part = jnp.ones((batch, W, S), dtype=bool)
    return jnp.concatenate([earlier, current, state_part], axis=2)[:, None]


def split_heads(values):
    return values.reshape(values.shape[0], values.shape[1], values.shape[2] // HEAD, HEAD)


def scores_of(query, keys, allowed):
    scores = jnp.einsum(
        "brhe,bkhe->bhrk", split_heads(query), split_heads(keys), preferred_element_type=jnp.float32
    ) * (1.0 / math.sqrt(HEAD))
    return jnp.where(allowed, scores, masked_score)


def attend(query, keys, values, allowed):
    scores = scores_of(query, keys, allowed)
    top = jnp.max(scores, axis=-1, keepdims=True)
    total = top + jnp.log(jnp.sum(jnp.exp(scores - top), axis=-1, keepdims=True))
    weights = jnp.exp(scores - total).astype(jnp.bfloat16)
    mixed = jnp.einsum(
        "bhrk,bkhe->brhe", weights, split_heads(values), preferred_element_type=jnp.float32
    )
    return (mixed.reshape(query.shape).astype(jnp.bfloat16), total)


def attend_back(query, keys, values, allowed, total, grad_mixed):
    scale = 1.0 / math.sqrt(HEAD)
    weights = jnp.exp(scores_of(query, keys, allowed) - total)
    grad_heads = split_heads(grad_mixed)
    grad_weights = jnp.einsum(
        "brhe,bkhe->bhrk", grad_heads, split_heads(values), preferred_element_type=jnp.float32
    )
    grad_scores = (
        weights * (grad_weights - jnp.sum(weights * grad_weights, axis=-1, keepdims=True))
    ).astype(jnp.bfloat16)
    grad_query = (
        jnp.einsum(
            "bhrk,bkhe->brhe", grad_scores, split_heads(keys), preferred_element_type=jnp.float32
        )
        * scale
    )
    grad_keys = (
        jnp.einsum(
            "bhrk,brhe->bkhe", grad_scores, split_heads(query), preferred_element_type=jnp.float32
        )
        * scale
    )
    grad_values = jnp.einsum(
        "bhrk,brhe->bkhe",
        weights.astype(jnp.bfloat16),
        grad_heads,
        preferred_element_type=jnp.float32,
    )
    return (
        grad_query.reshape(query.shape),
        grad_keys.reshape(keys.shape),
        grad_values.reshape(values.shape),
    )


def generic_body(
    tokens_in,
    piece_starts,
    cotangent,
    gain_tokens,
    gain_mlp,
    gain_state,
    gate_bias,
    w_query,
    w_key,
    w_value,
    w_out,
    w_state_query,
    w_state_key,
    w_state_value,
    w_state_out,
    w_gate,
    w_up,
    w_down,
    state_init,
):
    width_local = w_query.shape[1]
    column_start = lax.axis_index("tensor") * width_local

    def collect():
        return (
            lax.all_gather(w_query, "dp", axis=0, tiled=True),
            lax.all_gather(w_key, "dp", axis=0, tiled=True),
            lax.all_gather(w_value, "dp", axis=0, tiled=True),
            lax.all_gather(w_state_query, "dp", axis=0, tiled=True),
            lax.all_gather(w_state_key, "dp", axis=0, tiled=True),
            lax.all_gather(w_state_value, "dp", axis=0, tiled=True),
            lax.all_gather(w_gate, "dp", axis=0, tiled=True),
            lax.all_gather(w_up, "dp", axis=0, tiled=True),
            lax.all_gather(state_init, "dp", axis=0, tiled=True),
            lax.all_gather(w_out, "dp", axis=1, tiled=True),
            lax.all_gather(w_state_out, "dp", axis=1, tiled=True),
            lax.all_gather(w_down, "dp", axis=1, tiled=True),
            lax.all_gather(gain_tokens, "dp", axis=0, tiled=True),
            lax.all_gather(gain_mlp, "dp", axis=0, tiled=True),
            lax.all_gather(gain_state, "dp", axis=0, tiled=True),
            lax.all_gather(gate_bias, "dp", axis=0, tiled=True),
        )

    def unpack_gains(weights):
        token_gain = weights[12].astype(jnp.float32)
        mlp_gain = weights[13].astype(jnp.float32)
        state_gain = lax.dynamic_slice_in_dim(
            weights[14].astype(jnp.float32), column_start, width_local
        )
        bias_columns = lax.dynamic_slice_in_dim(
            weights[15].astype(jnp.float32), column_start, width_local
        )
        return (token_gain, mlp_gain, state_gain, bias_columns)

    outputs = []
    input_grads = []
    totals = None
    for micro in range(MICRO):
        forward_weights = collect()
        forward_rows_in = tokens_in[micro]
        (
            forward_full_query,
            forward_full_key,
            forward_full_value,
            forward_full_state_query,
            forward_full_state_key,
            forward_full_state_value,
            forward_full_gate,
            forward_full_up,
            forward_full_init,
            forward_full_out,
            forward_full_state_out,
            forward_full_down,
        ) = forward_weights[:12]
        forward_token_gain, forward_mlp_gain, forward_state_gain, forward_bias_columns = (
            unpack_gains(forward_weights)
        )
        forward_batch = forward_rows_in.shape[0]
        forward_labels = piece_labels(piece_starts[micro])
        forward_state = jnp.broadcast_to(
            forward_full_init.astype(jnp.float32), (forward_batch, S, width_local)
        )
        zero_keys = jnp.zeros((forward_batch, W, width_local), jnp.bfloat16)
        forward_earlier_key = zero_keys
        forward_earlier_value = zero_keys
        forward_kept = []
        middles = []
        for forward_block in range(NB):
            forward_rows = forward_rows_in[:, forward_block].astype(jnp.float32)
            normed = normed_rows(forward_rows, forward_token_gain).astype(jnp.bfloat16)
            square_sum = lax.psum(jnp.sum(forward_state * forward_state, axis=-1), "tensor")
            forward_inverse = lax.rsqrt(square_sum / D + epsilon)[..., None]
            forward_scaled = forward_state * forward_inverse
            state_normed = (forward_scaled * forward_state_gain).astype(jnp.bfloat16)
            forward_full_normed, forward_full_state = (
                lax.all_gather(normed, "tensor", axis=1, tiled=True),
                lax.all_gather(state_normed, "tensor", axis=2, tiled=True),
            )
            forward_query = matmul(forward_full_normed, forward_full_query).astype(jnp.bfloat16)
            forward_key = matmul(forward_full_normed, forward_full_key).astype(jnp.bfloat16)
            forward_value = matmul(forward_full_normed, forward_full_value).astype(jnp.bfloat16)
            forward_state_query = matmul(forward_full_state, forward_full_state_query).astype(
                jnp.bfloat16
            )
            forward_state_key = matmul(forward_full_state, forward_full_state_key).astype(
                jnp.bfloat16
            )
            forward_state_value = matmul(forward_full_state, forward_full_state_value).astype(
                jnp.bfloat16
            )
            gate_pre = matmul(forward_full_state, forward_full_gate) + forward_bias_columns
            forward_allowed = token_mask(forward_labels, forward_block)
            forward_token_keys = jnp.concatenate(
                [forward_earlier_key, forward_key, forward_state_key], axis=1
            )
            forward_token_values = jnp.concatenate(
                [forward_earlier_value, forward_value, forward_state_value], axis=1
            )
            forward_token_mixed, forward_token_total = attend(
                forward_query, forward_token_keys, forward_token_values, forward_allowed
            )
            forward_cross_keys = jnp.concatenate([forward_key, forward_state_key], axis=1)
            forward_cross_values = jnp.concatenate([forward_value, forward_state_value], axis=1)
            forward_state_mixed, forward_state_total = attend(
                forward_state_query, forward_cross_keys, forward_cross_values, True
            )
            forward_row_part = matmul(forward_token_mixed, forward_full_out)
            forward_state_part = matmul(forward_state_mixed, forward_full_state_out)
            row_sum, forward_state_sum = (
                lax.psum_scatter(
                    forward_row_part.astype(jnp.bfloat16), "tensor", scatter_dimension=1, tiled=True
                ).astype(jnp.float32),
                lax.psum_scatter(
                    forward_state_part.astype(jnp.bfloat16),
                    "tensor",
                    scatter_dimension=2,
                    tiled=True,
                ).astype(jnp.float32),
            )
            forward_forget = jax.nn.sigmoid(gate_pre)
            forward_kept.append(
                (
                    forward_full_normed,
                    forward_full_state,
                    forward_query,
                    forward_key,
                    forward_value,
                    forward_state_query,
                    forward_state_key,
                    forward_state_value,
                    forward_token_mixed,
                    forward_state_mixed,
                    forward_token_total,
                    forward_state_total,
                    forward_state,
                    forward_scaled,
                    forward_inverse,
                    forward_forget,
                    forward_state_sum,
                    forward_earlier_key,
                    forward_earlier_value,
                )
            )
            middle_block = forward_rows + row_sum
            middles.append(middle_block)
            forward_state = (
                forward_forget * forward_state + (1.0 - forward_forget) * forward_state_sum
            )
            forward_earlier_key, forward_earlier_value = (forward_key, forward_value)
        forward_middle = jnp.stack(middles, axis=1)
        mlp_in = normed_rows(forward_middle, forward_mlp_gain).astype(jnp.bfloat16)
        forward_full_mlp_in = lax.all_gather(mlp_in, "tensor", axis=2, tiled=True)
        forward_hidden, forward_active, mlp_partial = mlp_local(
            forward_full_mlp_in, forward_full_up, forward_full_down
        )
        mlp_sum = lax.psum_scatter(
            mlp_partial.astype(jnp.bfloat16), "tensor", scatter_dimension=2, tiled=True
        ).astype(jnp.float32)
        output = (forward_middle + mlp_sum).astype(jnp.bfloat16)
        output, saved = (
            output,
            (
                forward_kept,
                forward_middle,
                forward_full_mlp_in,
                forward_hidden,
                forward_active,
                forward_labels,
            ),
        )
        outputs.append(output)
        backward_weights = collect()
        rows_in = tokens_in[micro]
        grad_rows_out = cotangent[micro]
        (
            full_query,
            full_key,
            full_value,
            full_state_query,
            full_state_key,
            full_state_value,
            full_gate,
            full_up,
            full_init,
            full_out,
            full_state_out,
            full_down,
        ) = backward_weights[:12]
        backward_token_gain, backward_mlp_gain, backward_state_gain, backward_bias_columns = (
            unpack_gains(backward_weights)
        )
        kept, middle, full_mlp_in, hidden, active, labels = saved
        batch = rows_in.shape[0]
        full_grad = lax.all_gather(grad_rows_out, "tensor", axis=2, tiled=True)
        grad_down_w, grad_up_w, mlp_part = mlp_back_local(
            full_grad, active, hidden, full_mlp_in, full_down, full_up
        )
        grad_mlp_in = lax.psum_scatter(
            mlp_part.astype(jnp.bfloat16), "tensor", scatter_dimension=2, tiled=True
        ).astype(jnp.float32)
        unused_norm, mlp_norm_back = jax.vjp(normed_rows, middle, backward_mlp_gain)
        grad_middle_norm, grad_mlp_gain = mlp_norm_back(grad_mlp_in)
        grad_middle = grad_rows_out.astype(jnp.float32) + grad_middle_norm
        grad_state = jnp.zeros((batch, S, width_local), jnp.float32)
        carry_key = jnp.zeros((batch, W, width_local), jnp.float32)
        carry_value = jnp.zeros((batch, W, width_local), jnp.float32)
        square_zero = jnp.zeros((D, width_local), jnp.float32)
        grad_query_w = square_zero
        grad_key_w = square_zero
        grad_value_w = square_zero
        grad_state_query_w = square_zero
        grad_state_key_w = square_zero
        grad_state_value_w = square_zero
        grad_gate_w = square_zero
        grad_out_w = jnp.zeros((width_local, D), jnp.float32)
        grad_state_out_w = jnp.zeros((width_local, D), jnp.float32)
        grad_token_gain = jnp.zeros((D,), jnp.float32)
        grad_state_gain = jnp.zeros((width_local,), jnp.float32)
        grad_bias = jnp.zeros((width_local,), jnp.float32)
        grad_rows = [None] * NB
        for block in reversed(range(NB)):
            (
                full_normed,
                full_state,
                query,
                key,
                value,
                state_query,
                state_key,
                state_value,
                token_mixed,
                state_mixed,
                token_total,
                state_total,
                state,
                scaled,
                inverse,
                forget,
                state_sum,
                earlier_key,
                earlier_value,
            ) = kept[block]
            grad_row_block = grad_middle[:, block]
            grad_branch_state = ((1.0 - forget) * grad_state).astype(jnp.bfloat16)
            grad_gate = (grad_state * (state - state_sum) * forget * (1.0 - forget)).astype(
                jnp.bfloat16
            )
            carried_state = grad_state * forget
            full_grad_rows, full_grad_state = (
                lax.all_gather(grad_row_block.astype(jnp.bfloat16), "tensor", axis=1, tiled=True),
                lax.all_gather(grad_branch_state, "tensor", axis=2, tiled=True),
            )
            grad_out_w = grad_out_w + jnp.einsum(
                "bwc,bwd->cd", token_mixed, full_grad_rows, preferred_element_type=jnp.float32
            )
            grad_state_out_w = grad_state_out_w + jnp.einsum(
                "bsc,bsd->cd", state_mixed, full_grad_state, preferred_element_type=jnp.float32
            )
            grad_token_mixed = jnp.einsum(
                "bwd,cd->bwc", full_grad_rows, full_out, preferred_element_type=jnp.float32
            ).astype(jnp.bfloat16)
            grad_state_mixed = jnp.einsum(
                "bsd,cd->bsc", full_grad_state, full_state_out, preferred_element_type=jnp.float32
            ).astype(jnp.bfloat16)
            allowed = token_mask(labels, block)
            token_keys = jnp.concatenate([earlier_key, key, state_key], axis=1)
            token_values = jnp.concatenate([earlier_value, value, state_value], axis=1)
            cross_keys = jnp.concatenate([key, state_key], axis=1)
            cross_values = jnp.concatenate([value, state_value], axis=1)
            token_grad_query, token_grad_keys, token_grad_values = attend_back(
                query, token_keys, token_values, allowed, token_total, grad_token_mixed
            )
            state_grad_query, cross_grad_keys, cross_grad_values = attend_back(
                state_query, cross_keys, cross_values, True, state_total, grad_state_mixed
            )
            grad_key = (token_grad_keys[:, W : 2 * W] + cross_grad_keys[:, :W] + carry_key).astype(
                jnp.bfloat16
            )
            grad_value = (
                token_grad_values[:, W : 2 * W] + cross_grad_values[:, :W] + carry_value
            ).astype(jnp.bfloat16)
            carry_key = token_grad_keys[:, :W]
            carry_value = token_grad_values[:, :W]
            grad_state_key = (token_grad_keys[:, 2 * W :] + cross_grad_keys[:, W:]).astype(
                jnp.bfloat16
            )
            grad_state_value = (token_grad_values[:, 2 * W :] + cross_grad_values[:, W:]).astype(
                jnp.bfloat16
            )
            grad_query = token_grad_query.astype(jnp.bfloat16)
            grad_state_query = state_grad_query.astype(jnp.bfloat16)
            grad_query_w = grad_query_w + jnp.einsum(
                "bwd,bwc->dc", full_normed, grad_query, preferred_element_type=jnp.float32
            )
            grad_key_w = grad_key_w + jnp.einsum(
                "bwd,bwc->dc", full_normed, grad_key, preferred_element_type=jnp.float32
            )
            grad_value_w = grad_value_w + jnp.einsum(
                "bwd,bwc->dc", full_normed, grad_value, preferred_element_type=jnp.float32
            )
            grad_state_query_w = grad_state_query_w + jnp.einsum(
                "bsd,bsc->dc", full_state, grad_state_query, preferred_element_type=jnp.float32
            )
            grad_state_key_w = grad_state_key_w + jnp.einsum(
                "bsd,bsc->dc", full_state, grad_state_key, preferred_element_type=jnp.float32
            )
            grad_state_value_w = grad_state_value_w + jnp.einsum(
                "bsd,bsc->dc", full_state, grad_state_value, preferred_element_type=jnp.float32
            )
            grad_gate_w = grad_gate_w + jnp.einsum(
                "bsd,bsc->dc", full_state, grad_gate, preferred_element_type=jnp.float32
            )
            grad_bias = grad_bias + jnp.sum(grad_gate.astype(jnp.float32), axis=(0, 1))
            row_part = jnp.einsum(
                "bwc,dc->bwd", grad_query, full_query, preferred_element_type=jnp.float32
            )
            row_part = row_part + jnp.einsum(
                "bwc,dc->bwd", grad_key, full_key, preferred_element_type=jnp.float32
            )
            row_part = row_part + jnp.einsum(
                "bwc,dc->bwd", grad_value, full_value, preferred_element_type=jnp.float32
            )
            state_part = jnp.einsum(
                "bsc,dc->bsd",
                grad_state_query,
                full_state_query,
                preferred_element_type=jnp.float32,
            )
            state_part = state_part + jnp.einsum(
                "bsc,dc->bsd", grad_state_key, full_state_key, preferred_element_type=jnp.float32
            )
            state_part = state_part + jnp.einsum(
                "bsc,dc->bsd",
                grad_state_value,
                full_state_value,
                preferred_element_type=jnp.float32,
            )
            state_part = state_part + jnp.einsum(
                "bsc,dc->bsd", grad_gate, full_gate, preferred_element_type=jnp.float32
            )
            grad_normed, grad_state_normed = (
                lax.psum_scatter(
                    row_part.astype(jnp.bfloat16), "tensor", scatter_dimension=1, tiled=True
                ).astype(jnp.float32),
                lax.psum_scatter(
                    state_part.astype(jnp.bfloat16), "tensor", scatter_dimension=2, tiled=True
                ).astype(jnp.float32),
            )
            rows = rows_in[:, block].astype(jnp.float32)
            unused_rows, token_norm_back = jax.vjp(normed_rows, rows, backward_token_gain)
            grad_rows_norm, grad_gain_part = token_norm_back(grad_normed)
            grad_token_gain = grad_token_gain + grad_gain_part
            grad_rows[block] = (grad_row_block + grad_rows_norm).astype(jnp.bfloat16)
            grad_scaled = grad_state_normed * backward_state_gain
            grad_state_gain = grad_state_gain + jnp.sum(grad_state_normed * scaled, axis=(0, 1))
            dot_sum = lax.psum(jnp.sum(grad_scaled * scaled, axis=-1), "tensor")
            grad_state = carried_state + inverse * (grad_scaled - scaled * (dot_sum / D)[..., None])
        grad_init = jnp.sum(grad_state, axis=0)
        state_gain_full = lax.dynamic_update_slice_in_dim(
            jnp.zeros((D,), jnp.float32), grad_state_gain, column_start, 0
        )
        bias_full = lax.dynamic_update_slice_in_dim(
            jnp.zeros((D,), jnp.float32), grad_bias, column_start, 0
        )
        grads = (
            grad_query_w,
            grad_key_w,
            grad_value_w,
            grad_state_query_w,
            grad_state_key_w,
            grad_state_value_w,
            grad_gate_w,
            grad_up_w,
            grad_init,
            grad_out_w,
            grad_state_out_w,
            grad_down_w,
            grad_token_gain,
            grad_mlp_gain,
            state_gain_full,
            bias_full,
        )
        grads, grad_in = (grads, jnp.stack(grad_rows, axis=1))
        input_grads.append(grad_in)
        if totals is None:
            totals = grads
        else:
            totals = tuple((first + second for first, second in zip(totals, grads)))
    reduced = (
        lax.psum_scatter(
            totals[0].astype(jnp.bfloat16), "dp", scatter_dimension=0, tiled=True
        ).astype(jnp.float32),
        lax.psum_scatter(
            totals[1].astype(jnp.bfloat16), "dp", scatter_dimension=0, tiled=True
        ).astype(jnp.float32),
        lax.psum_scatter(
            totals[2].astype(jnp.bfloat16), "dp", scatter_dimension=0, tiled=True
        ).astype(jnp.float32),
        lax.psum_scatter(
            totals[3].astype(jnp.bfloat16), "dp", scatter_dimension=0, tiled=True
        ).astype(jnp.float32),
        lax.psum_scatter(
            totals[4].astype(jnp.bfloat16), "dp", scatter_dimension=0, tiled=True
        ).astype(jnp.float32),
        lax.psum_scatter(
            totals[5].astype(jnp.bfloat16), "dp", scatter_dimension=0, tiled=True
        ).astype(jnp.float32),
        lax.psum_scatter(
            totals[6].astype(jnp.bfloat16), "dp", scatter_dimension=0, tiled=True
        ).astype(jnp.float32),
        lax.psum_scatter(
            totals[7].astype(jnp.bfloat16), "dp", scatter_dimension=0, tiled=True
        ).astype(jnp.float32),
        lax.psum_scatter(
            totals[8].astype(jnp.bfloat16), "dp", scatter_dimension=0, tiled=True
        ).astype(jnp.float32),
        lax.psum_scatter(
            totals[9].astype(jnp.bfloat16), "dp", scatter_dimension=1, tiled=True
        ).astype(jnp.float32),
        lax.psum_scatter(
            totals[10].astype(jnp.bfloat16), "dp", scatter_dimension=1, tiled=True
        ).astype(jnp.float32),
        lax.psum_scatter(
            totals[11].astype(jnp.bfloat16), "dp", scatter_dimension=1, tiled=True
        ).astype(jnp.float32),
        lax.psum_scatter(
            totals[12].astype(jnp.bfloat16), "dp", scatter_dimension=0, tiled=True
        ).astype(jnp.float32),
        lax.psum_scatter(
            totals[13].astype(jnp.bfloat16), "dp", scatter_dimension=0, tiled=True
        ).astype(jnp.float32),
        lax.psum_scatter(
            totals[14].astype(jnp.bfloat16), "dp", scatter_dimension=0, tiled=True
        ).astype(jnp.float32),
        lax.psum_scatter(
            totals[15].astype(jnp.bfloat16), "dp", scatter_dimension=0, tiled=True
        ).astype(jnp.float32),
    )
    gain_totals = lax.psum((reduced[12], reduced[13], reduced[14], reduced[15]), "tensor")
    return (
        jnp.stack(outputs, axis=0),
        jnp.stack(input_grads, axis=0),
        gain_totals[0],
        gain_totals[1],
        gain_totals[2],
        gain_totals[3],
        reduced[0],
        reduced[1],
        reduced[2],
        reduced[9],
        reduced[3],
        reduced[4],
        reduced[5],
        reduced[10],
        reduced[6],
        reduced[7],
        reduced[11],
        reduced[8],
    )


BF = jnp.bfloat16
F32 = jnp.float32
HALF = 256
VMEM_BYTES = 60 * 1024 * 1024
EXP2_SCALE = math.log2(math.e) / math.sqrt(HEAD)
SCORE_SCALE = 1.0 / math.sqrt(HEAD)


def nn(left, right):
    return lax.dot_general(left, right, (((1,), (0,)), ((), ())), preferred_element_type=F32)


def nt(left, right):
    return lax.dot_general(left, right, (((1,), (1,)), ((), ())), preferred_element_type=F32)


def tn(left, right):
    return lax.dot_general(left, right, (((0,), (0,)), ((), ())), preferred_element_type=F32)


def inverse_rms(values):
    return lax.rsqrt(jnp.mean(values * values, axis=-1, keepdims=True) + epsilon)


def rms_back(scaled, inverse, grad):
    return (grad - scaled * jnp.mean(grad * scaled, axis=-1, keepdims=True)) * inverse


def params(semantics=("arbitrary",)):
    return pltpu.CompilerParams(dimension_semantics=semantics, vmem_limit_bytes=VMEM_BYTES)


def cost(flops, moved, transcendentals=0):
    return pl.CostEstimate(
        flops=int(flops), bytes_accessed=int(moved), transcendentals=int(transcendentals)
    )


def once(shape, index):
    return pl.BlockSpec(shape, index, pipeline_mode=pl.Buffered(1))


def project_kernel(rows, gain, w0, w1, normed, query, key, value):
    width = w0.shape[1] // 3
    wide = rows[...].astype(F32)
    normed[...] = (wide * inverse_rms(wide) * gain[...]).astype(BF)
    for half, weight in enumerate((w0, w1)):
        for which, out in enumerate((query, key, value)):
            out[:, half * width : (half + 1) * width] = nn(
                normed[...], weight[:, which * width : (which + 1) * width]
            ).astype(BF)


def project(rows, gain, weights):
    tokens = rows.shape[0]
    width = weights.shape[1]
    out = jax.ShapeDtypeStruct((tokens, D), BF)
    block = pl.BlockSpec((W, D), lambda b: (b, 0))
    return pl.pallas_call(
        project_kernel,
        grid=(tokens // W,),
        in_specs=[
            block,
            once((1, D), lambda b: (0, 0)),
            once((D, width), lambda b: (0, 0)),
            once((D, width), lambda b: (1, 0)),
        ],
        out_specs=[block] * 4,
        out_shape=[out] * 4,
        compiler_params=params(),
        cost_estimate=cost(2 * tokens * D * 3 * D, 2 * (5 * tokens * D + 3 * D * D)),
        name="project",
    )(rows, gain, weights, weights)


def softmax_parts(parts):
    top = parts[0][0].max(axis=1, keepdims=True)
    for scores, unused in parts[1:]:
        top = jnp.maximum(top, scores.max(axis=1, keepdims=True))
    total = None
    mixed = None
    for scores, values in parts:
        weights = jnp.exp2((scores - top) * EXP2_SCALE)
        part_total = weights.sum(axis=1, keepdims=True)
        part_mixed = nn(weights.astype(BF), values)
        total = part_total if total is None else total + part_total
        mixed = part_mixed if mixed is None else mixed + part_mixed
    return (mixed / total).astype(BF), top * EXP2_SCALE + jnp.log2(total)


def allowed_in_half(flag):
    row = lax.broadcasted_iota(jnp.int32, (HALF, HALF), 0)
    column = lax.broadcasted_iota(jnp.int32, (HALF, HALF), 1)
    return row, column


def forward_kernel(
    flags,
    query,
    key,
    value,
    key_before,
    value_before,
    init,
    gain,
    bias,
    wst0,
    wst1,
    wso0,
    wso1,
    token_mixed,
    state_mixed,
    state_normed,
    state_query,
    state_key,
    state_value,
    state_in,
    forget,
    apart,
    totals,
    state,
    token_totals,
    state_totals,
):
    block = pl.program_id(0)
    width = wso0.shape[1]

    @pl.when(block == 0)
    def start():
        state[...] = init[...].astype(F32)

    now = state[...]
    state_in[...] = now
    state_normed[...] = (now * inverse_rms(now) * gain[...]).astype(BF)
    for half, weight in enumerate((wst0, wst1)):
        columns = slice(half * width, (half + 1) * width)
        for which, out in enumerate((state_query, state_key, state_value)):
            out[:, columns] = nn(
                state_normed[...], weight[:, which * width : (which + 1) * width]
            ).astype(BF)
        gate = nn(state_normed[...], weight[:, 3 * width :]) + bias[:, columns]
        forget[:, columns] = jax.nn.sigmoid(gate)

    def heads(with_before):
        def head(index, carry):
            columns = pl.ds(pl.multiple_of(index * HEAD, HEAD), HEAD)
            lane = lax.broadcasted_iota(jnp.int32, (HALF, HEAD), 1) == index
            for half in range(2):
                rows = slice(half * HALF, (half + 1) * HALF)
                own = query[rows, columns]
                parts = []
                if with_before:
                    parts.append((nt(own, key_before[:, columns]), value_before[:, columns]))
                if half == 1:
                    parts.append((nt(own, key[:HALF, columns]), value[:HALF, columns]))
                row = lax.broadcasted_iota(jnp.int32, (HALF, HALF), 0)
                column = lax.broadcasted_iota(jnp.int32, (HALF, HALF), 1)
                reach = row + flags[2 * block + half] * HALF
                near = jnp.where(column <= reach, nt(own, key[rows, columns]), masked_score)
                parts.append((near, value[rows, columns]))
                parts.append((nt(own, state_key[:, columns]), state_value[:, columns]))
                mixed, total = softmax_parts(parts)
                token_mixed[rows, columns] = mixed
                token_totals[rows, :] = jnp.where(lane, total, token_totals[rows, :])
                own = state_query[rows, columns]
                mixed, total = softmax_parts(
                    [
                        (nt(own, key[:, columns]), value[:, columns]),
                        (nt(own, state_key[:, columns]), state_value[:, columns]),
                    ]
                )
                state_mixed[rows, columns] = mixed
                state_totals[rows, :] = jnp.where(lane, total, state_totals[rows, :])
            return carry

        lax.fori_loop(0, D // HEAD, head, 0)

    @pl.when(block == 0)
    def first():
        heads(False)

    @pl.when(block > 0)
    def later():
        heads(True)

    count = D // HEAD
    totals[0, :count, :] = token_totals[...].T[:count]
    totals[0, count:, :] = state_totals[...].T[:count]
    new = nt(state_mixed[:, :width], wso0[...]) + nt(state_mixed[:, width:], wso1[...])
    apart[...] = (now - new).astype(BF)
    state[...] = new + forget[...] * (now - new)


def forward(flags, query, key, value, init, gain, bias, weights, out_weights):
    blocks = query.shape[0] // W
    heads = D // HEAD
    width = weights.shape[1]
    own = pl.BlockSpec((W, D), lambda b, s: (b, 0))
    before = pl.BlockSpec((W, D), lambda b, s: (jnp.maximum(b - 1, 0), 0))
    low = jax.ShapeDtypeStruct((blocks * W, D), BF)
    wide = jax.ShapeDtypeStruct((blocks * W, D), F32)
    return pl.pallas_call(
        forward_kernel,
        grid_spec=pltpu.PrefetchScalarGridSpec(
            num_scalar_prefetch=1,
            grid=(blocks,),
            in_specs=[
                own,
                own,
                own,
                before,
                before,
                once((S, D), lambda b, s: (0, 0)),
                once((1, D), lambda b, s: (0, 0)),
                once((1, D), lambda b, s: (0, 0)),
                once((D, width), lambda b, s: (0, 0)),
                once((D, width), lambda b, s: (1, 0)),
                once((D, width // 4), lambda b, s: (0, 0)),
                once((D, width // 4), lambda b, s: (1, 0)),
            ],
            out_specs=[own] * 9 + [pl.BlockSpec((1, 2 * heads, W), lambda b, s: (b, 0, 0))],
            scratch_shapes=[
                pltpu.VMEM((S, D), F32),
                pltpu.VMEM((W, HEAD), F32),
                pltpu.VMEM((S, HEAD), F32),
            ],
        ),
        out_shape=[low] * 6 + [wide, wide, low, jax.ShapeDtypeStruct((blocks, 2 * heads, W), F32)],
        compiler_params=params(),
        cost_estimate=cost(42e9, 100e6, 40e6),
        name="forward",
    )(
        flags,
        query,
        key,
        value,
        key,
        value,
        init,
        gain,
        bias,
        weights,
        weights,
        out_weights,
        out_weights,
    )


def middle_kernel(rows, mixed, w0, w1, gain, cotangent, middle, mlp_in, mlp_turned, cot_turned):
    width = w0.shape[1]
    here = (
        rows[...].astype(F32) + nt(mixed[:, :width], w0[...]) + nt(mixed[:, width:], w1[...])
    )
    middle[...] = here
    low = (here * inverse_rms(here) * gain[...]).astype(BF)
    mlp_in[...] = low
    mlp_turned[...] = low.T
    cot_turned[...] = cotangent[...].T


def middle_rows(rows, mixed, weights, gain, cotangent):
    tokens = rows.shape[0]
    width = weights.shape[1]
    block = pl.BlockSpec((W, D), lambda b: (b, 0))
    turned = pl.BlockSpec((D, W), lambda b: (0, b))
    low = jax.ShapeDtypeStruct((tokens, D), BF)
    return pl.pallas_call(
        middle_kernel,
        grid=(tokens // W,),
        in_specs=[
            block,
            block,
            once((D, width), lambda b: (0, 0)),
            once((D, width), lambda b: (1, 0)),
            once((1, D), lambda b: (0, 0)),
            block,
        ],
        out_specs=[block, block, turned, turned],
        out_shape=[
            jax.ShapeDtypeStruct((tokens, D), F32),
            low,
            jax.ShapeDtypeStruct((D, tokens), BF),
            jax.ShapeDtypeStruct((D, tokens), BF),
        ],
        compiler_params=params(),
        cost_estimate=cost(2 * tokens * D * D, 2 * 8 * tokens * D),
        name="middle",
    )(rows, mixed, weights, weights, gain, cotangent)


def mlp_kernel(
    mlp_in, mlp_turned, cot, cot_turned, weights, out, grad_in, grads, out_sum, grad_sum, act, gh
):
    step = pl.program_id(0)
    units = weights.shape[1] // 2
    tokens = mlp_in.shape[0]

    @pl.when(step == 0)
    def start():
        out_sum[...] = jnp.zeros_like(out_sum)
        grad_sum[...] = jnp.zeros_like(grad_sum)

    slope = math.sqrt(2.0 / math.pi)

    def chunk(index, carry):
        rows = pl.ds(pl.multiple_of(index * W, W), W)
        hidden = nn(mlp_in[rows, :], weights[:, :units])
        back = nn(cot[rows, :], weights[:, units:])
        square = hidden * hidden
        bent = jnp.tanh(slope * hidden * (1.0 + 0.044715 * square))
        open_part = 0.5 * (1.0 + bent)
        active = (hidden * open_part).astype(BF)
        steep = open_part + (0.5 * slope) * hidden * (1.0 - bent * bent) * (
            1.0 + (3 * 0.044715) * square
        )
        grad = (steep * back).astype(BF)
        act[rows, :] = active
        gh[rows, :] = grad
        out_sum[rows, :] += nt(active, weights[:, units:])
        grad_sum[rows, :] += nt(grad, weights[:, :units])
        return carry

    lax.fori_loop(0, tokens // W, chunk, 0)
    grads[:, :units] = nn(mlp_turned[...], gh[...]).astype(BF)
    grads[:, units:] = nn(cot_turned[...], act[...]).astype(BF)

    @pl.when(step == pl.num_programs(0) - 1)
    def end():
        out[...] = out_sum[...].astype(BF)
        grad_in[...] = grad_sum[...].astype(BF)


def mlp(mlp_in, mlp_turned, cot, cot_turned, weights):
    tokens = mlp_in.shape[0]
    units = 512
    across = weights.shape[1] // (2 * units)
    low = jax.ShapeDtypeStruct((tokens, D), BF)
    rows = once((tokens, D), lambda f: (0, 0))
    turned = once((D, tokens), lambda f: (0, 0))
    tile = pl.BlockSpec((D, 2 * units), lambda f: (f // across, f % across))
    return pl.pallas_call(
        mlp_kernel,
        grid=(2 * across,),
        in_specs=[rows, turned, rows, turned, tile],
        out_specs=[rows, rows, tile],
        out_shape=[low, low, jax.ShapeDtypeStruct(weights.shape, BF)],
        scratch_shapes=[
            pltpu.VMEM((tokens, D), F32),
            pltpu.VMEM((tokens, D), F32),
            pltpu.VMEM((tokens, units), BF),
            pltpu.VMEM((tokens, units), BF),
        ],
        compiler_params=params(),
        cost_estimate=cost(103e9, 60e6, 8e6),
        name="mlp",
    )(mlp_in, mlp_turned, cot, cot_turned, weights)


def after_mlp_kernel(
    middle, mlp_out, grad_in, cot, gain, w0, w1, output, grad_middle, grad_mixed, grad_gain
):
    width = w0.shape[1]
    here = middle[...]
    inverse = inverse_rms(here)
    scaled = here * inverse
    grad = grad_in[...].astype(F32)
    output[...] = (here + mlp_out[...].astype(F32)).astype(BF)
    low = (cot[...].astype(F32) + rms_back(scaled, inverse, gain[...] * grad)).astype(BF)
    grad_middle[...] = low
    grad_mixed[:, :width] = nn(low, w0[...]).astype(BF)
    grad_mixed[:, width:] = nn(low, w1[...]).astype(BF)
    part = jnp.sum(grad * scaled, axis=0, keepdims=True)

    @pl.when(pl.program_id(0) == 0)
    def first():
        grad_gain[...] = part

    @pl.when(pl.program_id(0) > 0)
    def later():
        grad_gain[...] += part


def after_mlp(middle, mlp_out, grad_in, cot, gain, weights):
    tokens = middle.shape[0]
    width = weights.shape[1]
    block = pl.BlockSpec((W, D), lambda b: (b, 0))
    low = jax.ShapeDtypeStruct((tokens, D), BF)
    return pl.pallas_call(
        after_mlp_kernel,
        grid=(tokens // W,),
        in_specs=[
            block,
            block,
            block,
            block,
            once((1, D), lambda b: (0, 0)),
            once((D, width), lambda b: (0, 0)),
            once((D, width), lambda b: (1, 0)),
        ],
        out_specs=[block, block, block, pl.BlockSpec((1, D), lambda b: (0, 0))],
        out_shape=[low, low, low, jax.ShapeDtypeStruct((1, D), F32)],
        compiler_params=params(),
        cost_estimate=cost(2 * tokens * D * D, 2 * 8 * tokens * D),
        name="after_mlp",
    )(middle, mlp_out, grad_in, cot, gain, weights, weights)


def backward_kernel(
    flags,
    query,
    key,
    value,
    key_before,
    value_before,
    state_query,
    state_key,
    state_value,
    token_mixed,
    state_mixed,
    grad_mixed,
    totals,
    forget,
    state_in,
    apart,
    gain,
    weight,
    wso0,
    wso1,
    grad_tokens,
    grad_states,
    branch,
    grad_init,
    grad_gain,
    grad_bias,
    grad_state,
    grad_state_mixed,
    grad_normed,
    gate_part,
    carry_key,
    carry_value,
    grad_query_sum,
    deltas,
    queries,
    grads_out,
):
    step = pl.program_id(0)
    half = pl.program_id(1)
    block = pl.num_programs(0) - 1 - step
    width = wso0.shape[1]
    local = width // HEAD
    count = D // HEAD

    @pl.when((step == 0) & (half == 0))
    def start():
        grad_state[...] = jnp.zeros_like(grad_state)
        carry_key[...] = jnp.zeros_like(carry_key)
        carry_value[...] = jnp.zeros_like(carry_value)
        grad_gain[...] = jnp.zeros_like(grad_gain)
        grad_bias[...] = jnp.zeros_like(grad_bias)

    @pl.when(half == 0)
    def begin():
        coming = grad_state[...]
        keep = forget[...]
        low = ((1.0 - keep) * coming).astype(BF)
        branch[...] = low
        gate = (coming * apart[...].astype(F32) * keep * (1.0 - keep)).astype(BF)
        gate_part[0] = gate[:, :width]
        gate_part[1] = gate[:, width:]
        grad_bias[...] += jnp.sum(gate.astype(F32), axis=0, keepdims=True)
        grad_state_mixed[0] = nn(low, wso0[...]).astype(BF)
        grad_state_mixed[1] = nn(low, wso1[...]).astype(BF)
        grad_normed[...] = jnp.zeros_like(grad_normed)

    grad_states[3] = gate_part[half]

    def head(index, carry):
        columns = pl.ds(pl.multiple_of(index * HEAD, HEAD), HEAD)
        at = half * local + index
        queries[:W] = query[:, columns]
        queries[W:] = state_query[:, columns]
        grads_out[:W] = grad_mixed[:, columns]
        grads_out[W:] = grad_state_mixed[half, :, columns]
        for first, mixed in ((0, token_mixed), (W, state_mixed)):
            product = grads_out[first : first + W].astype(F32) * mixed[:, columns].astype(F32)
            deltas[:, first : first + W] = jnp.sum(product.T, axis=0, keepdims=True)
        token_total = totals[0, pl.ds(at, 1), :]
        state_total = totals[0, pl.ds(count + at, 1), :]
        total = jnp.concatenate([token_total, state_total], axis=1)

        def chunk(keys, values, first, last, mask, fresh):
            some = queries[first:last]
            some_grads = grads_out[first:last]
            scores = nt(keys, some)
            if mask is not None:
                size = mask.shape[1]
                scores = jnp.concatenate(
                    [jnp.where(mask, scores[:, :size], masked_score), scores[:, size:]], axis=1
                )
            weights = jnp.exp2(scores * EXP2_SCALE - total[:, first:last])
            back = nt(values, some_grads) - deltas[:, first:last]
            grad_scores = (weights * back).astype(BF)
            grad_values = nn(weights.astype(BF), some_grads)
            grad_keys = nn(grad_scores, some)
            turned = tn(keys, grad_scores)
            if fresh:
                grad_query_sum[:, first:last] = turned
            else:
                grad_query_sum[:, first:last] += turned
            return grad_keys * SCORE_SCALE, grad_values

        for part in range(2):
            rows = slice(part * HALF, (part + 1) * HALF)
            grad_keys, grad_values = chunk(
                state_key[rows, columns], state_value[rows, columns], 0, W + S, None, part == 0
            )
            grad_states[1, rows, columns] = grad_keys.astype(BF)
            grad_states[2, rows, columns] = grad_values.astype(BF)
        for part in range(2):
            rows = slice(part * HALF, (part + 1) * HALF)
            row = lax.broadcasted_iota(jnp.int32, (HALF, HALF), 0)
            column = lax.broadcasted_iota(jnp.int32, (HALF, HALF), 1)
            mask = row <= column + flags[2 * block + part] * HALF
            grad_keys, grad_values = chunk(
                key[rows, columns], value[rows, columns], part * HALF, W + S, mask, False
            )
            grad_tokens[1, rows, columns] = (grad_keys + carry_key[half, rows, columns]).astype(BF)
            grad_tokens[2, rows, columns] = (
                grad_values + carry_value[half, rows, columns]
            ).astype(BF)

        @pl.when(block > 0)
        def before():
            for part in range(2):
                rows = slice(part * HALF, (part + 1) * HALF)
                grad_keys, grad_values = chunk(
                    key_before[rows, columns], value_before[rows, columns], 0, W, None, False
                )
                carry_key[half, rows, columns] = grad_keys
                carry_value[half, rows, columns] = grad_values

        grad_query = (grad_query_sum[...] * SCORE_SCALE).T
        grad_tokens[0, :, columns] = grad_query[:W].astype(BF)
        grad_states[0, :, columns] = grad_query[W:].astype(BF)
        return carry

    lax.fori_loop(0, local, head, 0)
    for which in range(4):
        grad_normed[...] += nt(
            grad_states[which], weight[:, which * width : (which + 1) * width]
        )

    @pl.when(half == 1)
    def finish():
        here = state_in[...]
        inverse = inverse_rms(here)
        scaled = here * inverse
        grad = grad_normed[...]
        grad_gain[...] += jnp.sum(grad * scaled, axis=0, keepdims=True)
        grad_state[...] = forget[...] * grad_state[...] + rms_back(
            scaled, inverse, gain[...] * grad
        )

    @pl.when((half == 1) & (block == 0))
    def end():
        grad_init[...] = grad_state[...].astype(BF)


def backward(
    flags,
    query,
    key,
    value,
    state_query,
    state_key,
    state_value,
    token_mixed,
    state_mixed,
    grad_mixed,
    totals,
    forget,
    state_in,
    apart,
    gain,
    weights,
    out_weights,
):
    blocks = query.shape[0] // W
    heads = D // HEAD
    width = weights.shape[1]
    half_width = width // 4

    def rev(b):
        return blocks - 1 - b

    own = pl.BlockSpec((W, half_width), lambda b, t, s: (rev(b), t))
    before = pl.BlockSpec((W, half_width), lambda b, t, s: (jnp.maximum(rev(b) - 1, 0), t))
    whole = pl.BlockSpec((S, D), lambda b, t, s: (rev(b), 0))
    fixed_row = pl.BlockSpec((1, D), lambda b, t, s: (0, 0))
    return pl.pallas_call(
        backward_kernel,
        grid_spec=pltpu.PrefetchScalarGridSpec(
            num_scalar_prefetch=1,
            grid=(blocks, 2),
            in_specs=[own, own, own, before, before]
            + [own] * 6
            + [pl.BlockSpec((1, 2 * heads, W), lambda b, t, s: (rev(b), 0, 0))]
            + [whole] * 3
            + [
                once((1, D), lambda b, t, s: (0, 0)),
                pl.BlockSpec((D, width), lambda b, t, s: (t, 0)),
                once((D, half_width), lambda b, t, s: (0, 0)),
                once((D, half_width), lambda b, t, s: (1, 0)),
            ],
            out_specs=[
                pl.BlockSpec((3, W, half_width), lambda b, t, s: (0, rev(b), t)),
                pl.BlockSpec((4, S, half_width), lambda b, t, s: (0, rev(b), t)),
                whole,
                pl.BlockSpec((S, D), lambda b, t, s: (0, 0)),
                fixed_row,
                fixed_row,
            ],
            scratch_shapes=[
                pltpu.VMEM((S, D), F32),
                pltpu.VMEM((2, S, half_width), BF),
                pltpu.VMEM((S, D), F32),
                pltpu.VMEM((2, S, half_width), BF),
                pltpu.VMEM((2, W, half_width), F32),
                pltpu.VMEM((2, W, half_width), F32),
                pltpu.VMEM((HEAD, W + S), F32),
                pltpu.VMEM((1, W + S), F32),
                pltpu.VMEM((W + S, HEAD), BF),
                pltpu.VMEM((W + S, HEAD), BF),
            ],
        ),
        out_shape=[
            jax.ShapeDtypeStruct((3, blocks * W, D), BF),
            jax.ShapeDtypeStruct((4, blocks * W, D), BF),
            jax.ShapeDtypeStruct((blocks * W, D), BF),
            jax.ShapeDtypeStruct((S, D), BF),
            jax.ShapeDtypeStruct((1, D), F32),
            jax.ShapeDtypeStruct((1, D), F32),
        ],
        compiler_params=params(("arbitrary", "arbitrary")),
        cost_estimate=cost(70e9, 100e6, 40e6),
        name="backward",
    )(
        flags,
        query,
        key,
        value,
        key,
        value,
        state_query,
        state_key,
        state_value,
        token_mixed,
        state_mixed,
        grad_mixed,
        totals,
        forget,
        state_in,
        apart,
        gain,
        weights,
        out_weights,
        out_weights,
    )


def weight_grad_kernel(left, right, out, turned):
    @pl.when(pl.program_id(0) == 0)
    def start():
        turned[...] = left[...].T

    out[...] = nn(turned[...], right[0]).astype(BF)


def weight_grads(left, rights):
    many, tokens, unused = rights.shape
    width = D // 2
    return pl.pallas_call(
        weight_grad_kernel,
        grid=(2 * many,),
        in_specs=[
            once((tokens, D), lambda g: (0, 0)),
            pl.BlockSpec((1, tokens, width), lambda g: (g // 2, 0, g % 2)),
        ],
        out_specs=pl.BlockSpec((D, width), lambda g: (g % 2, g // 2)),
        out_shape=jax.ShapeDtypeStruct((2 * D, many * width), BF),
        scratch_shapes=[pltpu.VMEM((D, tokens), BF)],
        compiler_params=params(),
        cost_estimate=cost(2 * tokens * D * D * many, 2 * (tokens * D + 2 * many * D * D)),
        name="weight_grads",
    )(left, rights)


def token_grad_kernel(grads, w0, w1, rows, grad_middle, gain, out, grad_gain):
    width = w0.shape[1] // 3
    total = None
    for which in range(3):
        for half, weight in enumerate((w0, w1)):
            part = nt(
                grads[which, :, half * width : (half + 1) * width],
                weight[:, which * width : (which + 1) * width],
            )
            total = part if total is None else total + part
    here = rows[...].astype(F32)
    inverse = inverse_rms(here)
    scaled = here * inverse
    out[...] = (
        grad_middle[...].astype(F32) + rms_back(scaled, inverse, gain[...] * total)
    ).astype(BF)
    part = jnp.sum(total * scaled, axis=0, keepdims=True)

    @pl.when(pl.program_id(0) == 0)
    def first():
        grad_gain[...] = part

    @pl.when(pl.program_id(0) > 0)
    def later():
        grad_gain[...] += part


def token_grad(grads, weights, rows, grad_middle, gain):
    tokens = rows.shape[0]
    width = weights.shape[1]
    block = pl.BlockSpec((W, D), lambda b: (b, 0))
    return pl.pallas_call(
        token_grad_kernel,
        grid=(tokens // W,),
        in_specs=[
            pl.BlockSpec((3, W, D), lambda b: (0, b, 0)),
            once((D, width), lambda b: (0, 0)),
            once((D, width), lambda b: (1, 0)),
            block,
            block,
            once((1, D), lambda b: (0, 0)),
        ],
        out_specs=[block, pl.BlockSpec((1, D), lambda b: (0, 0))],
        out_shape=[jax.ShapeDtypeStruct((tokens, D), BF), jax.ShapeDtypeStruct((1, D), F32)],
        compiler_params=params(),
        cost_estimate=cost(2 * tokens * 3 * D * D, 2 * 6 * tokens * D),
        name="token_grad",
    )(grads, weights, weights, rows, grad_middle, gain)


def gather(local):
    return lax.all_gather(local, ("tensor", "dp"), axis=0, tiled=True)


def scatter(total):
    return lax.psum_scatter(total, ("tensor", "dp"), scatter_dimension=0, tiled=True)


def whole_sequence_body(
    tokens_in,
    piece_starts,
    cotangent,
    gain_tokens,
    gain_mlp,
    gain_state,
    gate_bias,
    w_query,
    w_key,
    w_value,
    w_out,
    w_state_query,
    w_state_key,
    w_state_value,
    w_state_out,
    w_gate,
    w_up,
    w_down,
    state_init,
):
    mine = lax.axis_index("tensor")
    first = mine == 0
    local_rows = w_query.shape[0]
    dp = D // local_rows
    width = w_query.shape[1]
    units = 512
    across = w_up.shape[1] // units
    swap = [(0, 1), (1, 0)]

    def bring(pair):
        keep = jnp.where(first, pair[0, 0], pair[1, 0])
        send = jnp.where(first, pair[1, 0], pair[0, 0])
        come = lax.ppermute(send, "tensor", swap)
        top = jnp.where(first, keep, come)
        low = jnp.where(first, come, keep)
        return jnp.concatenate([top, low], axis=1).reshape(NB * W, D)

    def give(rows):
        halves = rows.reshape(NB, 2, HALF, D)
        keep = jnp.where(first, halves[:, 0], halves[:, 1])
        send = jnp.where(first, halves[:, 1], halves[:, 0])
        come = lax.ppermute(send, "tensor", swap)
        return jnp.stack([jnp.where(first, keep, come), jnp.where(first, come, keep)])[:, None]

    def split_init(values):
        side = values.shape[1] // 2
        return jnp.concatenate([values[:, :side], values[:, side:]], axis=0)

    gains = jnp.stack([gain_tokens, gain_mlp, gain_state, gate_bias])
    small = jnp.concatenate(
        [split_init(state_init), jnp.pad(gains, ((0, local_rows - 4), (0, 128 - local_rows)))],
        axis=1,
    )
    full_qkv = gather(jnp.concatenate([w_query, w_key, w_value, small], axis=1))
    full_small = full_qkv[:, 3 * width :]
    full_state = gather(
        jnp.concatenate([w_state_query, w_state_key, w_state_value, w_gate], axis=1)
    )
    full_outs = gather(jnp.concatenate([w_state_out.T, w_out.T], axis=1))
    up_parts = w_up.reshape(local_rows, across, 1, units)
    down_parts = w_down.T.reshape(local_rows, across, 1, units)
    full_mlp = gather(
        jnp.concatenate([up_parts, down_parts], axis=2).reshape(local_rows, 2 * across * units)
    )
    side = width // 2
    init = full_small[:, :side].reshape(2, dp, 2, local_rows // 2, side)
    init = jnp.transpose(init, (1, 3, 0, 2, 4)).reshape(S, D)
    gains = full_small[:D, side:].reshape(dp, local_rows, 128)[:, :4, :local_rows]
    gains = jnp.transpose(gains, (1, 0, 2)).reshape(4, 1, D).astype(F32)

    rows = bring(tokens_in)
    cot = bring(cotangent)
    starts = jnp.where(first, piece_starts[0, 0], piece_starts[1, 0])
    flags = jnp.any(
        starts[:, None] == PIECE * jnp.arange(NB * W // PIECE, dtype=jnp.int32)[None], axis=0
    ).astype(jnp.int32)

    weights_qkv = full_qkv[:, : 3 * width]
    weights_so = full_outs[:, :width]
    weights_out = full_outs[:, width:]
    normed, query, key, value = project(rows, gains[0], weights_qkv)
    (
        token_mixed,
        state_mixed,
        state_normed,
        state_query,
        state_key,
        state_value,
        state_in,
        forget,
        apart,
        totals,
    ) = forward(flags, query, key, value, init, gains[2], gains[3], full_state, weights_so)
    middle, mlp_in, mlp_turned, cot_turned = middle_rows(
        rows, token_mixed, weights_out, gains[1], cot
    )
    mlp_out, grad_mlp_in, grad_mlp_w = mlp(mlp_in, mlp_turned, cot, cot_turned, full_mlp)
    output, grad_middle, grad_mixed, grad_gain_mlp = after_mlp(
        middle, mlp_out, grad_mlp_in, cot, gains[1], weights_out
    )
    part_mlp = scatter(grad_mlp_w)
    grad_tok, grad_sta, branch, grad_init, grad_gain_state, grad_bias = backward(
        flags,
        query,
        key,
        value,
        state_query,
        state_key,
        state_value,
        token_mixed,
        state_mixed,
        grad_mixed,
        totals,
        forget,
        state_in,
        apart,
        gains[2],
        full_state,
        weights_so,
    )
    part_out = scatter(weight_grads(grad_middle, token_mixed[None]))
    part_so = scatter(weight_grads(branch, state_mixed[None]))
    part_state = scatter(weight_grads(state_normed, grad_sta))
    part_qkv = scatter(weight_grads(normed, grad_tok))
    grad_in, grad_gain_tokens = token_grad(grad_tok, weights_qkv, rows, grad_middle, gains[0])

    init_parts = jnp.transpose(
        grad_init.reshape(dp, local_rows // 2, 2, 2, side), (2, 0, 3, 1, 4)
    ).reshape(2 * D, side)
    gain_parts = jnp.stack(
        [grad_gain_tokens[0], grad_gain_mlp[0], grad_gain_state[0], grad_bias[0]]
    ).reshape(4, dp, local_rows)
    gain_parts = jnp.pad(
        jnp.transpose(gain_parts, (1, 0, 2)),
        ((0, 0), (0, local_rows - 4), (0, 128 - local_rows)),
    ).reshape(D, 128)
    gain_parts = jnp.concatenate([gain_parts, gain_parts], axis=0).astype(BF)
    part_small = scatter(jnp.concatenate([init_parts, gain_parts], axis=1)).astype(F32)

    part_init = part_small[:, :side]
    part_init = jnp.concatenate(
        [part_init[: local_rows // 2], part_init[local_rows // 2 :]], axis=1
    )
    part_gains = part_small[:4, side : side + local_rows]
    part_mlp = part_mlp.astype(F32).reshape(local_rows, across, 2, units)
    part_qkv = part_qkv.astype(F32)
    part_state = part_state.astype(F32)
    return (
        give(output),
        give(grad_in),
        part_gains[0],
        part_gains[1],
        part_gains[2],
        part_gains[3],
        part_qkv[:, :width],
        part_qkv[:, width : 2 * width],
        part_qkv[:, 2 * width :],
        part_out.astype(F32).T,
        part_state[:, :width],
        part_state[:, width : 2 * width],
        part_state[:, 2 * width : 3 * width],
        part_so.astype(F32).T,
        part_state[:, 3 * width :],
        part_mlp[:, :, 0].reshape(local_rows, across * units),
        part_mlp[:, :, 1].reshape(local_rows, across * units).T,
        part_init,
    )


def solution(mesh):
    one_each = mesh.shape["tensor"] == MICRO
    return jax.shard_map(
        whole_sequence_body if one_each else generic_body,
        mesh=mesh,
        in_specs=(
            P(None, "dp", None, "tensor", None),
            P(None, "dp", None),
            P(None, "dp", None, "tensor", None),
            P("dp"),
            P("dp"),
            P("dp"),
            P("dp"),
            P("dp", "tensor"),
            P("dp", "tensor"),
            P("dp", "tensor"),
            P("tensor", "dp"),
            P("dp", "tensor"),
            P("dp", "tensor"),
            P("dp", "tensor"),
            P("tensor", "dp"),
            P("dp", "tensor"),
            P("dp", "tensor"),
            P("tensor", "dp"),
            P("dp", "tensor"),
        ),
        out_specs=(
            P(None, "dp", None, "tensor", None),
            P(None, "dp", None, "tensor", None),
            P("dp"),
            P("dp"),
            P("dp"),
            P("dp"),
            P("dp", "tensor"),
            P("dp", "tensor"),
            P("dp", "tensor"),
            P("tensor", "dp"),
            P("dp", "tensor"),
            P("dp", "tensor"),
            P("dp", "tensor"),
            P("tensor", "dp"),
            P("dp", "tensor"),
            P("dp", "tensor"),
            P("tensor", "dp"),
            P("dp", "tensor"),
        ),
        check_vma=False,
    )
```

```python
import functools
import math

import jax
import jax.numpy as jnp
from jax import lax
from jax.experimental import pallas as pl
from jax.experimental.pallas import tpu as pltpu
from jax.sharding import PartitionSpec as P

D = 1024
HEAD = 128
W = 512
S = 512
PIECE = 256
MICRO = 2
NB = 4


epsilon = 1e-06
masked_score = -1e30


def rms_scale(values):
    return values * lax.rsqrt(jnp.mean(values * values, axis=-1, keepdims=True) + epsilon)


def normed_rows(values, gain):
    return rms_scale(values) * gain


def matmul(left, right):
    return jnp.dot(left, right, preferred_element_type=jnp.float32)


def mlp_local(full_in, full_up, full_down):
    hidden = matmul(full_in, full_up)
    active = jax.nn.gelu(hidden).astype(jnp.bfloat16)
    return (hidden, active, matmul(active, full_down))


def mlp_back_local(full_grad, active, hidden, full_in, full_down, full_up):
    grad_down_w = jnp.einsum("...f,...d->fd", active, full_grad, preferred_element_type=jnp.float32)
    grad_active = jnp.einsum(
        "...d,fd->...f", full_grad, full_down, preferred_element_type=jnp.float32
    )
    unused_value, gelu_back = jax.vjp(jax.nn.gelu, hidden)
    grad_hidden = gelu_back(grad_active)[0].astype(jnp.bfloat16)
    grad_up_w = jnp.einsum(
        "...d,...f->df", full_in, grad_hidden, preferred_element_type=jnp.float32
    )
    mlp_part = jnp.einsum("...f,df->...d", grad_hidden, full_up, preferred_element_type=jnp.float32)
    return (grad_down_w, grad_up_w, mlp_part)


def piece_labels(starts):
    positions = jnp.arange(NB * W, dtype=jnp.int32)
    inside = (positions[None, None, :] >= starts[:, :, None]) & (
        positions[None, None, :] < starts[:, :, None] + PIECE
    )
    numbers = jnp.arange(1, starts.shape[1] + 1, dtype=jnp.int32)
    return jnp.sum(jnp.where(inside, numbers[None, :, None], 0), axis=1)


def token_mask(labels, block):
    batch = labels.shape[0]
    own = labels[:, block * W : (block + 1) * W]
    local = jnp.arange(W, dtype=jnp.int32)
    causal = (local[None, :] <= local[:, None])[None]
    together = (own[:, :, None] == own[:, None, :]) & (own[:, :, None] > 0)
    current = causal | together
    earlier = jnp.full((batch, W, W), block > 0)
    state_part = jnp.ones((batch, W, S), dtype=bool)
    return jnp.concatenate([earlier, current, state_part], axis=2)[:, None]


def split_heads(values):
    return values.reshape(values.shape[0], values.shape[1], values.shape[2] // HEAD, HEAD)


def scores_of(query, keys, allowed):
    scores = jnp.einsum(
        "brhe,bkhe->bhrk", split_heads(query), split_heads(keys), preferred_element_type=jnp.float32
    ) * (1.0 / math.sqrt(HEAD))
    return jnp.where(allowed, scores, masked_score)


def attend(query, keys, values, allowed):
    scores = scores_of(query, keys, allowed)
    top = jnp.max(scores, axis=-1, keepdims=True)
    total = top + jnp.log(jnp.sum(jnp.exp(scores - top), axis=-1, keepdims=True))
    weights = jnp.exp(scores - total).astype(jnp.bfloat16)
    mixed = jnp.einsum(
        "bhrk,bkhe->brhe", weights, split_heads(values), preferred_element_type=jnp.float32
    )
    return (mixed.reshape(query.shape).astype(jnp.bfloat16), total)


def attend_back(query, keys, values, allowed, total, grad_mixed):
    scale = 1.0 / math.sqrt(HEAD)
    weights = jnp.exp(scores_of(query, keys, allowed) - total)
    grad_heads = split_heads(grad_mixed)
    grad_weights = jnp.einsum(
        "brhe,bkhe->bhrk", grad_heads, split_heads(values), preferred_element_type=jnp.float32
    )
    grad_scores = (
        weights * (grad_weights - jnp.sum(weights * grad_weights, axis=-1, keepdims=True))
    ).astype(jnp.bfloat16)
    grad_query = (
        jnp.einsum(
            "bhrk,bkhe->brhe", grad_scores, split_heads(keys), preferred_element_type=jnp.float32
        )
        * scale
    )
    grad_keys = (
        jnp.einsum(
            "bhrk,brhe->bkhe", grad_scores, split_heads(query), preferred_element_type=jnp.float32
        )
        * scale
    )
    grad_values = jnp.einsum(
        "bhrk,brhe->bkhe",
        weights.astype(jnp.bfloat16),
        grad_heads,
        preferred_element_type=jnp.float32,
    )
    return (
        grad_query.reshape(query.shape),
        grad_keys.reshape(keys.shape),
        grad_values.reshape(values.shape),
    )


def generic_body(
    tokens_in,
    piece_starts,
    cotangent,
    gain_tokens,
    gain_mlp,
    gain_state,
    gate_bias,
    w_query,
    w_key,
    w_value,
    w_out,
    w_state_query,
    w_state_key,
    w_state_value,
    w_state_out,
    w_gate,
    w_up,
    w_down,
    state_init,
):
    width_local = w_query.shape[1]
    column_start = lax.axis_index("tensor") * width_local

    def collect():
        return (
            lax.all_gather(w_query, "dp", axis=0, tiled=True),
            lax.all_gather(w_key, "dp", axis=0, tiled=True),
            lax.all_gather(w_value, "dp", axis=0, tiled=True),
            lax.all_gather(w_state_query, "dp", axis=0, tiled=True),
            lax.all_gather(w_state_key, "dp", axis=0, tiled=True),
            lax.all_gather(w_state_value, "dp", axis=0, tiled=True),
            lax.all_gather(w_gate, "dp", axis=0, tiled=True),
            lax.all_gather(w_up, "dp", axis=0, tiled=True),
            lax.all_gather(state_init, "dp", axis=0, tiled=True),
            lax.all_gather(w_out, "dp", axis=1, tiled=True),
            lax.all_gather(w_state_out, "dp", axis=1, tiled=True),
            lax.all_gather(w_down, "dp", axis=1, tiled=True),
            lax.all_gather(gain_tokens, "dp", axis=0, tiled=True),
            lax.all_gather(gain_mlp, "dp", axis=0, tiled=True),
            lax.all_gather(gain_state, "dp", axis=0, tiled=True),
            lax.all_gather(gate_bias, "dp", axis=0, tiled=True),
        )

    def unpack_gains(weights):
        token_gain = weights[12].astype(jnp.float32)
        mlp_gain = weights[13].astype(jnp.float32)
        state_gain = lax.dynamic_slice_in_dim(
            weights[14].astype(jnp.float32), column_start, width_local
        )
        bias_columns = lax.dynamic_slice_in_dim(
            weights[15].astype(jnp.float32), column_start, width_local
        )
        return (token_gain, mlp_gain, state_gain, bias_columns)

    outputs = []
    input_grads = []
    totals = None
    for micro in range(MICRO):
        forward_weights = collect()
        forward_rows_in = tokens_in[micro]
        (
            forward_full_query,
            forward_full_key,
            forward_full_value,
            forward_full_state_query,
            forward_full_state_key,
            forward_full_state_value,
            forward_full_gate,
            forward_full_up,
            forward_full_init,
            forward_full_out,
            forward_full_state_out,
            forward_full_down,
        ) = forward_weights[:12]
        forward_token_gain, forward_mlp_gain, forward_state_gain, forward_bias_columns = (
            unpack_gains(forward_weights)
        )
        forward_batch = forward_rows_in.shape[0]
        forward_labels = piece_labels(piece_starts[micro])
        forward_state = jnp.broadcast_to(
            forward_full_init.astype(jnp.float32), (forward_batch, S, width_local)
        )
        zero_keys = jnp.zeros((forward_batch, W, width_local), jnp.bfloat16)
        forward_earlier_key = zero_keys
        forward_earlier_value = zero_keys
        forward_kept = []
        middles = []
        for forward_block in range(NB):
            forward_rows = forward_rows_in[:, forward_block].astype(jnp.float32)
            normed = normed_rows(forward_rows, forward_token_gain).astype(jnp.bfloat16)
            square_sum = lax.psum(jnp.sum(forward_state * forward_state, axis=-1), "tensor")
            forward_inverse = lax.rsqrt(square_sum / D + epsilon)[..., None]
            forward_scaled = forward_state * forward_inverse
            state_normed = (forward_scaled * forward_state_gain).astype(jnp.bfloat16)
            forward_full_normed, forward_full_state = (
                lax.all_gather(normed, "tensor", axis=1, tiled=True),
                lax.all_gather(state_normed, "tensor", axis=2, tiled=True),
            )
            forward_query = matmul(forward_full_normed, forward_full_query).astype(jnp.bfloat16)
            forward_key = matmul(forward_full_normed, forward_full_key).astype(jnp.bfloat16)
            forward_value = matmul(forward_full_normed, forward_full_value).astype(jnp.bfloat16)
            forward_state_query = matmul(forward_full_state, forward_full_state_query).astype(
                jnp.bfloat16
            )
            forward_state_key = matmul(forward_full_state, forward_full_state_key).astype(
                jnp.bfloat16
            )
            forward_state_value = matmul(forward_full_state, forward_full_state_value).astype(
                jnp.bfloat16
            )
            gate_pre = matmul(forward_full_state, forward_full_gate) + forward_bias_columns
            forward_allowed = token_mask(forward_labels, forward_block)
            forward_token_keys = jnp.concatenate(
                [forward_earlier_key, forward_key, forward_state_key], axis=1
            )
            forward_token_values = jnp.concatenate(
                [forward_earlier_value, forward_value, forward_state_value], axis=1
            )
            forward_token_mixed, forward_token_total = attend(
                forward_query, forward_token_keys, forward_token_values, forward_allowed
            )
            forward_cross_keys = jnp.concatenate([forward_key, forward_state_key], axis=1)
            forward_cross_values = jnp.concatenate([forward_value, forward_state_value], axis=1)
            forward_state_mixed, forward_state_total = attend(
                forward_state_query, forward_cross_keys, forward_cross_values, True
            )
            forward_row_part = matmul(forward_token_mixed, forward_full_out)
            forward_state_part = matmul(forward_state_mixed, forward_full_state_out)
            row_sum, forward_state_sum = (
                lax.psum_scatter(
                    forward_row_part.astype(jnp.bfloat16), "tensor", scatter_dimension=1, tiled=True
                ).astype(jnp.float32),
                lax.psum_scatter(
                    forward_state_part.astype(jnp.bfloat16),
                    "tensor",
                    scatter_dimension=2,
                    tiled=True,
                ).astype(jnp.float32),
            )
            forward_forget = jax.nn.sigmoid(gate_pre)
            forward_kept.append(
                (
                    forward_full_normed,
                    forward_full_state,
                    forward_query,
                    forward_key,
                    forward_value,
                    forward_state_query,
                    forward_state_key,
                    forward_state_value,
                    forward_token_mixed,
                    forward_state_mixed,
                    forward_token_total,
                    forward_state_total,
                    forward_state,
                    forward_scaled,
                    forward_inverse,
                    forward_forget,
                    forward_state_sum,
                    forward_earlier_key,
                    forward_earlier_value,
                )
            )
            middle_block = forward_rows + row_sum
            middles.append(middle_block)
            forward_state = (
                forward_forget * forward_state + (1.0 - forward_forget) * forward_state_sum
            )
            forward_earlier_key, forward_earlier_value = (forward_key, forward_value)
        forward_middle = jnp.stack(middles, axis=1)
        mlp_in = normed_rows(forward_middle, forward_mlp_gain).astype(jnp.bfloat16)
        forward_full_mlp_in = lax.all_gather(mlp_in, "tensor", axis=2, tiled=True)
        forward_hidden, forward_active, mlp_partial = mlp_local(
            forward_full_mlp_in, forward_full_up, forward_full_down
        )
        mlp_sum = lax.psum_scatter(
            mlp_partial.astype(jnp.bfloat16), "tensor", scatter_dimension=2, tiled=True
        ).astype(jnp.float32)
        output = (forward_middle + mlp_sum).astype(jnp.bfloat16)
        output, saved = (
            output,
            (
                forward_kept,
                forward_middle,
                forward_full_mlp_in,
                forward_hidden,
                forward_active,
                forward_labels,
            ),
        )
        outputs.append(output)
        backward_weights = collect()
        rows_in = tokens_in[micro]
        grad_rows_out = cotangent[micro]
        (
            full_query,
            full_key,
            full_value,
            full_state_query,
            full_state_key,
            full_state_value,
            full_gate,
            full_up,
            full_init,
            full_out,
            full_state_out,
            full_down,
        ) = backward_weights[:12]
        backward_token_gain, backward_mlp_gain, backward_state_gain, backward_bias_columns = (
            unpack_gains(backward_weights)
        )
        kept, middle, full_mlp_in, hidden, active, labels = saved
        batch = rows_in.shape[0]
        full_grad = lax.all_gather(grad_rows_out, "tensor", axis=2, tiled=True)
        grad_down_w, grad_up_w, mlp_part = mlp_back_local(
            full_grad, active, hidden, full_mlp_in, full_down, full_up
        )
        grad_mlp_in = lax.psum_scatter(
            mlp_part.astype(jnp.bfloat16), "tensor", scatter_dimension=2, tiled=True
        ).astype(jnp.float32)
        unused_norm, mlp_norm_back = jax.vjp(normed_rows, middle, backward_mlp_gain)
        grad_middle_norm, grad_mlp_gain = mlp_norm_back(grad_mlp_in)
        grad_middle = grad_rows_out.astype(jnp.float32) + grad_middle_norm
        grad_state = jnp.zeros((batch, S, width_local), jnp.float32)
        carry_key = jnp.zeros((batch, W, width_local), jnp.float32)
        carry_value = jnp.zeros((batch, W, width_local), jnp.float32)
        square_zero = jnp.zeros((D, width_local), jnp.float32)
        grad_query_w = square_zero
        grad_key_w = square_zero
        grad_value_w = square_zero
        grad_state_query_w = square_zero
        grad_state_key_w = square_zero
        grad_state_value_w = square_zero
        grad_gate_w = square_zero
        grad_out_w = jnp.zeros((width_local, D), jnp.float32)
        grad_state_out_w = jnp.zeros((width_local, D), jnp.float32)
        grad_token_gain = jnp.zeros((D,), jnp.float32)
        grad_state_gain = jnp.zeros((width_local,), jnp.float32)
        grad_bias = jnp.zeros((width_local,), jnp.float32)
        grad_rows = [None] * NB
        for block in reversed(range(NB)):
            (
                full_normed,
                full_state,
                query,
                key,
                value,
                state_query,
                state_key,
                state_value,
                token_mixed,
                state_mixed,
                token_total,
                state_total,
                state,
                scaled,
                inverse,
                forget,
                state_sum,
                earlier_key,
                earlier_value,
            ) = kept[block]
            grad_row_block = grad_middle[:, block]
            grad_branch_state = ((1.0 - forget) * grad_state).astype(jnp.bfloat16)
            grad_gate = (grad_state * (state - state_sum) * forget * (1.0 - forget)).astype(
                jnp.bfloat16
            )
            carried_state = grad_state * forget
            full_grad_rows, full_grad_state = (
                lax.all_gather(grad_row_block.astype(jnp.bfloat16), "tensor", axis=1, tiled=True),
                lax.all_gather(grad_branch_state, "tensor", axis=2, tiled=True),
            )
            grad_out_w = grad_out_w + jnp.einsum(
                "bwc,bwd->cd", token_mixed, full_grad_rows, preferred_element_type=jnp.float32
            )
            grad_state_out_w = grad_state_out_w + jnp.einsum(
                "bsc,bsd->cd", state_mixed, full_grad_state, preferred_element_type=jnp.float32
            )
            grad_token_mixed = jnp.einsum(
                "bwd,cd->bwc", full_grad_rows, full_out, preferred_element_type=jnp.float32
            ).astype(jnp.bfloat16)
            grad_state_mixed = jnp.einsum(
                "bsd,cd->bsc", full_grad_state, full_state_out, preferred_element_type=jnp.float32
            ).astype(jnp.bfloat16)
            allowed = token_mask(labels, block)
            token_keys = jnp.concatenate([earlier_key, key, state_key], axis=1)
            token_values = jnp.concatenate([earlier_value, value, state_value], axis=1)
            cross_keys = jnp.concatenate([key, state_key], axis=1)
            cross_values = jnp.concatenate([value, state_value], axis=1)
            token_grad_query, token_grad_keys, token_grad_values = attend_back(
                query, token_keys, token_values, allowed, token_total, grad_token_mixed
            )
            state_grad_query, cross_grad_keys, cross_grad_values = attend_back(
                state_query, cross_keys, cross_values, True, state_total, grad_state_mixed
            )
            grad_key = (token_grad_keys[:, W : 2 * W] + cross_grad_keys[:, :W] + carry_key).astype(
                jnp.bfloat16
            )
            grad_value = (
                token_grad_values[:, W : 2 * W] + cross_grad_values[:, :W] + carry_value
            ).astype(jnp.bfloat16)
            carry_key = token_grad_keys[:, :W]
            carry_value = token_grad_values[:, :W]
            grad_state_key = (token_grad_keys[:, 2 * W :] + cross_grad_keys[:, W:]).astype(
                jnp.bfloat16
            )
            grad_state_value = (token_grad_values[:, 2 * W :] + cross_grad_values[:, W:]).astype(
                jnp.bfloat16
            )
            grad_query = token_grad_query.astype(jnp.bfloat16)
            grad_state_query = state_grad_query.astype(jnp.bfloat16)
            grad_query_w = grad_query_w + jnp.einsum(
                "bwd,bwc->dc", full_normed, grad_query, preferred_element_type=jnp.float32
            )
            grad_key_w = grad_key_w + jnp.einsum(
                "bwd,bwc->dc", full_normed, grad_key, preferred_element_type=jnp.float32
            )
            grad_value_w = grad_value_w + jnp.einsum(
                "bwd,bwc->dc", full_normed, grad_value, preferred_element_type=jnp.float32
            )
            grad_state_query_w = grad_state_query_w + jnp.einsum(
                "bsd,bsc->dc", full_state, grad_state_query, preferred_element_type=jnp.float32
            )
            grad_state_key_w = grad_state_key_w + jnp.einsum(
                "bsd,bsc->dc", full_state, grad_state_key, preferred_element_type=jnp.float32
            )
            grad_state_value_w = grad_state_value_w + jnp.einsum(
                "bsd,bsc->dc", full_state, grad_state_value, preferred_element_type=jnp.float32
            )
            grad_gate_w = grad_gate_w + jnp.einsum(
                "bsd,bsc->dc", full_state, grad_gate, preferred_element_type=jnp.float32
            )
            grad_bias = grad_bias + jnp.sum(grad_gate.astype(jnp.float32), axis=(0, 1))
            row_part = jnp.einsum(
                "bwc,dc->bwd", grad_query, full_query, preferred_element_type=jnp.float32
            )
            row_part = row_part + jnp.einsum(
                "bwc,dc->bwd", grad_key, full_key, preferred_element_type=jnp.float32
            )
            row_part = row_part + jnp.einsum(
                "bwc,dc->bwd", grad_value, full_value, preferred_element_type=jnp.float32
            )
            state_part = jnp.einsum(
                "bsc,dc->bsd",
                grad_state_query,
                full_state_query,
                preferred_element_type=jnp.float32,
            )
            state_part = state_part + jnp.einsum(
                "bsc,dc->bsd", grad_state_key, full_state_key, preferred_element_type=jnp.float32
            )
            state_part = state_part + jnp.einsum(
                "bsc,dc->bsd",
                grad_state_value,
                full_state_value,
                preferred_element_type=jnp.float32,
            )
            state_part = state_part + jnp.einsum(
                "bsc,dc->bsd", grad_gate, full_gate, preferred_element_type=jnp.float32
            )
            grad_normed, grad_state_normed = (
                lax.psum_scatter(
                    row_part.astype(jnp.bfloat16), "tensor", scatter_dimension=1, tiled=True
                ).astype(jnp.float32),
                lax.psum_scatter(
                    state_part.astype(jnp.bfloat16), "tensor", scatter_dimension=2, tiled=True
                ).astype(jnp.float32),
            )
            rows = rows_in[:, block].astype(jnp.float32)
            unused_rows, token_norm_back = jax.vjp(normed_rows, rows, backward_token_gain)
            grad_rows_norm, grad_gain_part = token_norm_back(grad_normed)
            grad_token_gain = grad_token_gain + grad_gain_part
            grad_rows[block] = (grad_row_block + grad_rows_norm).astype(jnp.bfloat16)
            grad_scaled = grad_state_normed * backward_state_gain
            grad_state_gain = grad_state_gain + jnp.sum(grad_state_normed * scaled, axis=(0, 1))
            dot_sum = lax.psum(jnp.sum(grad_scaled * scaled, axis=-1), "tensor")
            grad_state = carried_state + inverse * (grad_scaled - scaled * (dot_sum / D)[..., None])
        grad_init = jnp.sum(grad_state, axis=0)
        state_gain_full = lax.dynamic_update_slice_in_dim(
            jnp.zeros((D,), jnp.float32), grad_state_gain, column_start, 0
        )
        bias_full = lax.dynamic_update_slice_in_dim(
            jnp.zeros((D,), jnp.float32), grad_bias, column_start, 0
        )
        grads = (
            grad_query_w,
            grad_key_w,
            grad_value_w,
            grad_state_query_w,
            grad_state_key_w,
            grad_state_value_w,
            grad_gate_w,
            grad_up_w,
            grad_init,
            grad_out_w,
            grad_state_out_w,
            grad_down_w,
            grad_token_gain,
            grad_mlp_gain,
            state_gain_full,
            bias_full,
        )
        grads, grad_in = (grads, jnp.stack(grad_rows, axis=1))
        input_grads.append(grad_in)
        if totals is None:
            totals = grads
        else:
            totals = tuple((first + second for first, second in zip(totals, grads)))
    reduced = (
        lax.psum_scatter(
            totals[0].astype(jnp.bfloat16), "dp", scatter_dimension=0, tiled=True
        ).astype(jnp.float32),
        lax.psum_scatter(
            totals[1].astype(jnp.bfloat16), "dp", scatter_dimension=0, tiled=True
        ).astype(jnp.float32),
        lax.psum_scatter(
            totals[2].astype(jnp.bfloat16), "dp", scatter_dimension=0, tiled=True
        ).astype(jnp.float32),
        lax.psum_scatter(
            totals[3].astype(jnp.bfloat16), "dp", scatter_dimension=0, tiled=True
        ).astype(jnp.float32),
        lax.psum_scatter(
            totals[4].astype(jnp.bfloat16), "dp", scatter_dimension=0, tiled=True
        ).astype(jnp.float32),
        lax.psum_scatter(
            totals[5].astype(jnp.bfloat16), "dp", scatter_dimension=0, tiled=True
        ).astype(jnp.float32),
        lax.psum_scatter(
            totals[6].astype(jnp.bfloat16), "dp", scatter_dimension=0, tiled=True
        ).astype(jnp.float32),
        lax.psum_scatter(
            totals[7].astype(jnp.bfloat16), "dp", scatter_dimension=0, tiled=True
        ).astype(jnp.float32),
        lax.psum_scatter(
            totals[8].astype(jnp.bfloat16), "dp", scatter_dimension=0, tiled=True
        ).astype(jnp.float32),
        lax.psum_scatter(
            totals[9].astype(jnp.bfloat16), "dp", scatter_dimension=1, tiled=True
        ).astype(jnp.float32),
        lax.psum_scatter(
            totals[10].astype(jnp.bfloat16), "dp", scatter_dimension=1, tiled=True
        ).astype(jnp.float32),
        lax.psum_scatter(
            totals[11].astype(jnp.bfloat16), "dp", scatter_dimension=1, tiled=True
        ).astype(jnp.float32),
        lax.psum_scatter(
            totals[12].astype(jnp.bfloat16), "dp", scatter_dimension=0, tiled=True
        ).astype(jnp.float32),
        lax.psum_scatter(
            totals[13].astype(jnp.bfloat16), "dp", scatter_dimension=0, tiled=True
        ).astype(jnp.float32),
        lax.psum_scatter(
            totals[14].astype(jnp.bfloat16), "dp", scatter_dimension=0, tiled=True
        ).astype(jnp.float32),
        lax.psum_scatter(
            totals[15].astype(jnp.bfloat16), "dp", scatter_dimension=0, tiled=True
        ).astype(jnp.float32),
    )
    gain_totals = lax.psum((reduced[12], reduced[13], reduced[14], reduced[15]), "tensor")
    return (
        jnp.stack(outputs, axis=0),
        jnp.stack(input_grads, axis=0),
        gain_totals[0],
        gain_totals[1],
        gain_totals[2],
        gain_totals[3],
        reduced[0],
        reduced[1],
        reduced[2],
        reduced[9],
        reduced[3],
        reduced[4],
        reduced[5],
        reduced[10],
        reduced[6],
        reduced[7],
        reduced[11],
        reduced[8],
    )


BF = jnp.bfloat16
F32 = jnp.float32
HALF = 256
VMEM_BYTES = 60 * 1024 * 1024
EXP2_SCALE = math.log2(math.e) / math.sqrt(HEAD)
SCORE_SCALE = 1.0 / math.sqrt(HEAD)


def nn(left, right):
    return lax.dot_general(left, right, (((1,), (0,)), ((), ())), preferred_element_type=F32)


def nt(left, right):
    return lax.dot_general(left, right, (((1,), (1,)), ((), ())), preferred_element_type=F32)


def tn(left, right):
    return lax.dot_general(left, right, (((0,), (0,)), ((), ())), preferred_element_type=F32)


def inverse_rms(values):
    return lax.rsqrt(jnp.mean(values * values, axis=-1, keepdims=True) + epsilon)


def rms_back(scaled, inverse, grad):
    return (grad - scaled * jnp.mean(grad * scaled, axis=-1, keepdims=True)) * inverse


def params(semantics=("arbitrary",)):
    return pltpu.CompilerParams(dimension_semantics=semantics, vmem_limit_bytes=VMEM_BYTES)


def cost(flops, moved, transcendentals=0):
    return pl.CostEstimate(
        flops=int(flops), bytes_accessed=int(moved), transcendentals=int(transcendentals)
    )


def once(shape, index):
    return pl.BlockSpec(shape, index, pipeline_mode=pl.Buffered(1))


def project_kernel(rows, gain, w0, w1, turned, query, key, value):
    width = w0.shape[1] // 3
    wide = rows[...].astype(F32)
    normed = (wide * inverse_rms(wide) * gain[...]).astype(BF)
    turned[...] = normed.T
    for half, weight in enumerate((w0, w1)):
        for which, out in enumerate((query, key, value)):
            out[:, half * width : (half + 1) * width] = nn(
                normed, weight[:, which * width : (which + 1) * width]
            ).astype(BF)


def project(rows, gain, weights):
    tokens = rows.shape[0]
    width = 3 * D // 2
    out = jax.ShapeDtypeStruct((tokens, D), BF)
    block = pl.BlockSpec((W, D), lambda b: (b, 0))
    return pl.pallas_call(
        project_kernel,
        grid=(tokens // W,),
        in_specs=[
            block,
            once((1, D), lambda b: (0, 0)),
            once((D, width), lambda b: (0, 0)),
            once((D, width), lambda b: (1, 0)),
        ],
        out_specs=[pl.BlockSpec((D, W), lambda b: (0, b))] + [block] * 3,
        out_shape=[jax.ShapeDtypeStruct((D, tokens), BF)] + [out] * 3,
        compiler_params=params(),
        cost_estimate=cost(2 * tokens * D * 3 * D, 2 * (5 * tokens * D + 3 * D * D)),
        name="project",
    )(rows, gain, weights, weights)


def softmax_parts(parts):
    top = parts[0][0].max(axis=1, keepdims=True)
    for scores, unused in parts[1:]:
        top = jnp.maximum(top, scores.max(axis=1, keepdims=True))
    total = None
    mixed = None
    for scores, values in parts:
        weights = jnp.exp2((scores - top) * EXP2_SCALE)
        part_total = weights.sum(axis=1, keepdims=True)
        part_mixed = nn(weights.astype(BF), values)
        total = part_total if total is None else total + part_total
        mixed = part_mixed if mixed is None else mixed + part_mixed
    return (mixed / total).astype(BF), top * EXP2_SCALE + jnp.log2(total)


def forward_kernel(
    flags,
    query,
    key,
    value,
    key_before,
    value_before,
    init,
    gain,
    bias,
    query0,
    query1,
    key0,
    key1,
    second0,
    second1,
    token_mixed,
    state_mixed,
    turned,
    state_query,
    state_key,
    state_value,
    state_in,
    forget,
    apart,
    totals,
    state,
    token_totals,
    state_totals,
):
    block = pl.program_id(0)
    width = query0.shape[1]

    @pl.when(block == 0)
    def start():
        state[...] = init[...].astype(F32)

    now = state[...]
    state_in[...] = now
    state_normed = (now * inverse_rms(now) * gain[...]).astype(BF)
    turned[...] = state_normed.T
    for half, (one, other, two) in enumerate(((query0, key0, second0), (query1, key1, second1))):
        columns = slice(half * width, (half + 1) * width)
        state_query[:, columns] = nn(state_normed, one[...]).astype(BF)
        state_key[:, columns] = nn(state_normed, other[...]).astype(BF)
        state_value[:, columns] = nn(state_normed, two[:, :width]).astype(BF)
        gate = nn(state_normed, two[:, width : 2 * width]) + bias[:, columns]
        forget[:, columns] = jax.nn.sigmoid(gate)

    def heads(with_before):
        def head(index, carry):
            columns = pl.ds(pl.multiple_of(index * HEAD, HEAD), HEAD)
            lane = lax.broadcasted_iota(jnp.int32, (HALF, HEAD), 1) == index
            for half in range(2):
                rows = slice(half * HALF, (half + 1) * HALF)
                own = query[rows, columns]
                parts = []
                if with_before:
                    parts.append((nt(own, key_before[:, columns]), value_before[:, columns]))
                if half == 1:
                    parts.append((nt(own, key[:HALF, columns]), value[:HALF, columns]))
                row = lax.broadcasted_iota(jnp.int32, (HALF, HALF), 0)
                column = lax.broadcasted_iota(jnp.int32, (HALF, HALF), 1)
                reach = row + flags[2 * block + half] * HALF
                near = jnp.where(column <= reach, nt(own, key[rows, columns]), masked_score)
                parts.append((near, value[rows, columns]))
                parts.append((nt(own, state_key[:, columns]), state_value[:, columns]))
                mixed, total = softmax_parts(parts)
                token_mixed[rows, columns] = mixed
                token_totals[rows, :] = jnp.where(lane, total, token_totals[rows, :])
                own = state_query[rows, columns]
                mixed, total = softmax_parts(
                    [
                        (nt(own, key[:, columns]), value[:, columns]),
                        (nt(own, state_key[:, columns]), state_value[:, columns]),
                    ]
                )
                state_mixed[rows, columns] = mixed
                state_totals[rows, :] = jnp.where(lane, total, state_totals[rows, :])
            return carry

        lax.fori_loop(0, D // HEAD, head, 0)

    @pl.when(block == 0)
    def first():
        heads(False)

    @pl.when(block > 0)
    def later():
        heads(True)

    count = D // HEAD
    totals[0, :count, :] = token_totals[...].T[:count]
    totals[0, count:, :] = state_totals[...].T[:count]
    new = nt(state_mixed[:, :width], second0[:, 2 * width :]) + nt(
        state_mixed[:, width:], second1[:, 2 * width :]
    )
    apart[...] = (now - new).astype(BF)
    state[...] = new + forget[...] * (now - new)


def forward(flags, query, key, value, init, gain, bias, weights, more_weights):
    blocks = query.shape[0] // W
    heads = D // HEAD
    own = pl.BlockSpec((W, D), lambda b, s: (b, 0))
    before = pl.BlockSpec((W, D), lambda b, s: (jnp.maximum(b - 1, 0), 0))
    low = jax.ShapeDtypeStruct((blocks * W, D), BF)
    wide = jax.ShapeDtypeStruct((blocks * W, D), F32)
    return pl.pallas_call(
        forward_kernel,
        grid_spec=pltpu.PrefetchScalarGridSpec(
            num_scalar_prefetch=1,
            grid=(blocks,),
            in_specs=[
                own,
                own,
                own,
                before,
                before,
                once((S, D), lambda b, s: (0, 0)),
                once((1, D), lambda b, s: (0, 0)),
                once((1, D), lambda b, s: (0, 0)),
                once((D, D // 2), lambda b, s: (0, 3)),
                once((D, D // 2), lambda b, s: (1, 3)),
                once((D, D // 2), lambda b, s: (0, 4)),
                once((D, D // 2), lambda b, s: (1, 4)),
                once((D, more_weights.shape[1]), lambda b, s: (0, 0)),
                once((D, more_weights.shape[1]), lambda b, s: (1, 0)),
            ],
            out_specs=[own] * 2
            + [pl.BlockSpec((D, S), lambda b, s: (0, b))]
            + [own] * 6
            + [pl.BlockSpec((1, 2 * heads, W), lambda b, s: (b, 0, 0))],
            scratch_shapes=[
                pltpu.VMEM((S, D), F32),
                pltpu.VMEM((W, HEAD), F32),
                pltpu.VMEM((S, HEAD), F32),
            ],
        ),
        out_shape=[low] * 2
        + [jax.ShapeDtypeStruct((D, blocks * S), BF)]
        + [low] * 3
        + [wide, wide, low, jax.ShapeDtypeStruct((blocks, 2 * heads, W), F32)],
        compiler_params=params(),
        cost_estimate=cost(42e9, 100e6, 40e6),
        name="forward",
    )(
        flags,
        query,
        key,
        value,
        key,
        value,
        init,
        gain,
        bias,
        weights,
        weights,
        weights,
        weights,
        more_weights,
        more_weights,
    )


def middle_kernel(rows, mixed, w0, w1, gain, cotangent, middle, mlp_in, mlp_turned, cot_turned):
    width = w0.shape[1]
    here = (
        rows[...].astype(F32) + nt(mixed[:, :width], w0[...]) + nt(mixed[:, width:], w1[...])
    )
    middle[...] = here
    low = (here * inverse_rms(here) * gain[...]).astype(BF)
    mlp_in[...] = low
    mlp_turned[...] = low.T
    cot_turned[...] = cotangent[...].T


def middle_rows(rows, mixed, weights, gain, cotangent):
    tokens = rows.shape[0]
    width = D // 2
    last = weights.shape[1] // width - 1
    block = pl.BlockSpec((W, D), lambda b: (b, 0))
    turned = pl.BlockSpec((D, W), lambda b: (0, b))
    low = jax.ShapeDtypeStruct((tokens, D), BF)
    return pl.pallas_call(
        middle_kernel,
        grid=(tokens // W,),
        in_specs=[
            block,
            block,
            once((D, width), lambda b: (0, last)),
            once((D, width), lambda b: (1, last)),
            once((1, D), lambda b: (0, 0)),
            block,
        ],
        out_specs=[block, block, turned, turned],
        out_shape=[
            jax.ShapeDtypeStruct((tokens, D), F32),
            low,
            jax.ShapeDtypeStruct((D, tokens), BF),
            jax.ShapeDtypeStruct((D, tokens), BF),
        ],
        compiler_params=params(),
        cost_estimate=cost(2 * tokens * D * D, 2 * 8 * tokens * D),
        name="middle",
    )(rows, mixed, weights, weights, gain, cotangent)


def mlp_kernel(
    mlp_in, mlp_turned, cot, cot_turned, weights, out, grad_in, grads, out_sum, grad_sum, act, gh
):
    step = pl.program_id(0)
    units = weights.shape[1] // 2
    tokens = mlp_in.shape[0]

    @pl.when(step == 0)
    def start():
        out_sum[...] = jnp.zeros_like(out_sum)
        grad_sum[...] = jnp.zeros_like(grad_sum)

    slope = math.sqrt(2.0 / math.pi)

    def chunk(index, carry):
        rows = pl.ds(pl.multiple_of(index * W, W), W)
        hidden = nn(mlp_in[rows, :], weights[:, :units])
        back = nn(cot[rows, :], weights[:, units:])
        square = hidden * hidden
        bent = jnp.tanh(slope * hidden * (1.0 + 0.044715 * square))
        open_part = 0.5 * (1.0 + bent)
        active = (hidden * open_part).astype(BF)
        steep = open_part + (0.5 * slope) * hidden * (1.0 - bent * bent) * (
            1.0 + (3 * 0.044715) * square
        )
        grad = (steep * back).astype(BF)
        act[rows, :] = active
        gh[rows, :] = grad
        out_sum[rows, :] += nt(active, weights[:, units:])
        grad_sum[rows, :] += nt(grad, weights[:, :units])
        return carry

    lax.fori_loop(0, tokens // W, chunk, 0)
    grads[:, :units] = nn(mlp_turned[...], gh[...]).astype(BF)
    grads[:, units:] = nn(cot_turned[...], act[...]).astype(BF)

    @pl.when(step == pl.num_programs(0) - 1)
    def end():
        out[...] = out_sum[...].astype(BF)
        grad_in[...] = grad_sum[...].astype(BF)


def mlp(mlp_in, mlp_turned, cot, cot_turned, weights):
    tokens = mlp_in.shape[0]
    units = 512
    across = (weights.shape[1] - D // 2) // (2 * units)
    low = jax.ShapeDtypeStruct((tokens, D), BF)
    rows = once((tokens, D), lambda f: (0, 0))
    turned = once((D, tokens), lambda f: (0, 0))
    tile = pl.BlockSpec((D, 2 * units), lambda f: (f // across, f % across))
    return pl.pallas_call(
        mlp_kernel,
        grid=(2 * across,),
        in_specs=[rows, turned, rows, turned, tile],
        out_specs=[rows, rows, tile],
        out_shape=[low, low, jax.ShapeDtypeStruct(weights.shape, BF)],
        scratch_shapes=[
            pltpu.VMEM((tokens, D), F32),
            pltpu.VMEM((tokens, D), F32),
            pltpu.VMEM((tokens, units), BF),
            pltpu.VMEM((tokens, units), BF),
        ],
        compiler_params=params(),
        cost_estimate=cost(103e9, 60e6, 8e6),
        name="mlp",
    )(mlp_in, mlp_turned, cot, cot_turned, weights)


def after_mlp_kernel(
    middle, mlp_out, grad_in, cot, gain, w0, w1, output, grad_middle, turned, grad_mixed, grad_gain
):
    width = w0.shape[1]
    here = middle[...]
    inverse = inverse_rms(here)
    scaled = here * inverse
    grad = grad_in[...].astype(F32)
    output[...] = (here + mlp_out[...].astype(F32)).astype(BF)
    low = (cot[...].astype(F32) + rms_back(scaled, inverse, gain[...] * grad)).astype(BF)
    grad_middle[...] = low
    turned[...] = low.T
    grad_mixed[:, :width] = nn(low, w0[...]).astype(BF)
    grad_mixed[:, width:] = nn(low, w1[...]).astype(BF)
    part = jnp.sum(grad * scaled, axis=0, keepdims=True)

    @pl.when(pl.program_id(0) == 0)
    def first():
        grad_gain[...] = part

    @pl.when(pl.program_id(0) > 0)
    def later():
        grad_gain[...] += part


def after_mlp(middle, mlp_out, grad_in, cot, gain, weights):
    tokens = middle.shape[0]
    width = D // 2
    last = weights.shape[1] // width - 1
    block = pl.BlockSpec((W, D), lambda b: (b, 0))
    low = jax.ShapeDtypeStruct((tokens, D), BF)
    return pl.pallas_call(
        after_mlp_kernel,
        grid=(tokens // W,),
        in_specs=[
            block,
            block,
            block,
            block,
            once((1, D), lambda b: (0, 0)),
            once((D, width), lambda b: (0, last)),
            once((D, width), lambda b: (1, last)),
        ],
        out_specs=[
            block,
            block,
            pl.BlockSpec((D, W), lambda b: (0, b)),
            block,
            pl.BlockSpec((1, D), lambda b: (0, 0)),
        ],
        out_shape=[
            low,
            low,
            jax.ShapeDtypeStruct((D, tokens), BF),
            low,
            jax.ShapeDtypeStruct((1, D), F32),
        ],
        compiler_params=params(),
        cost_estimate=cost(2 * tokens * D * D, 2 * 8 * tokens * D),
        name="after_mlp",
    )(middle, mlp_out, grad_in, cot, gain, weights, weights)


def backward_kernel(
    flags,
    query,
    key,
    value,
    key_before,
    value_before,
    state_query,
    state_key,
    state_value,
    token_mixed,
    state_mixed,
    grad_mixed,
    totals,
    forget,
    state_in,
    apart,
    gain,
    weight_query,
    weight_key,
    more_weight,
    wso0,
    wso1,
    grad_tokens,
    grad_states,
    branch,
    grad_init,
    grad_gain,
    grad_bias,
    grad_state,
    grad_state_mixed,
    grad_normed,
    gate_part,
    carry_key,
    carry_value,
    grad_query_sum,
    deltas,
    queries,
    grads_out,
):
    step = pl.program_id(0)
    half = pl.program_id(1)
    block = pl.num_programs(0) - 1 - step
    width = wso0.shape[1]
    local = width // HEAD
    count = D // HEAD

    @pl.when((step == 0) & (half == 0))
    def start():
        grad_state[...] = jnp.zeros_like(grad_state)
        carry_key[...] = jnp.zeros_like(carry_key)
        carry_value[...] = jnp.zeros_like(carry_value)
        grad_gain[...] = jnp.zeros_like(grad_gain)
        grad_bias[...] = jnp.zeros_like(grad_bias)

    @pl.when(half == 0)
    def begin():
        coming = grad_state[...]
        keep = forget[...]
        low = ((1.0 - keep) * coming).astype(BF)
        branch[...] = low.T
        gate = (coming * apart[...].astype(F32) * keep * (1.0 - keep)).astype(BF)
        gate_part[0] = gate[:, :width]
        gate_part[1] = gate[:, width:]
        grad_bias[...] += jnp.sum(gate.astype(F32), axis=0, keepdims=True)
        grad_state_mixed[0] = nn(low, wso0[...]).astype(BF)
        grad_state_mixed[1] = nn(low, wso1[...]).astype(BF)
        grad_normed[...] = jnp.zeros_like(grad_normed)

    grad_states[3] = gate_part[half]

    def head(index, carry):
        columns = pl.ds(pl.multiple_of(index * HEAD, HEAD), HEAD)
        at = half * local + index
        queries[:W] = query[:, columns]
        queries[W:] = state_query[:, columns]
        grads_out[:W] = grad_mixed[:, columns]
        grads_out[W:] = grad_state_mixed[half, :, columns]
        for first, mixed in ((0, token_mixed), (W, state_mixed)):
            product = grads_out[first : first + W].astype(F32) * mixed[:, columns].astype(F32)
            deltas[:, first : first + W] = jnp.sum(product.T, axis=0, keepdims=True)
        token_total = totals[0, pl.ds(at, 1), :]
        state_total = totals[0, pl.ds(count + at, 1), :]
        total = jnp.concatenate([token_total, state_total], axis=1)

        def chunk(keys, values, first, last, mask, fresh):
            some = queries[first:last]
            some_grads = grads_out[first:last]
            scores = nt(keys, some)
            if mask is not None:
                size = mask.shape[1]
                scores = jnp.concatenate(
                    [jnp.where(mask, scores[:, :size], masked_score), scores[:, size:]], axis=1
                )
            weights = jnp.exp2(scores * EXP2_SCALE - total[:, first:last])
            back = nt(values, some_grads) - deltas[:, first:last]
            grad_scores = (weights * back).astype(BF)
            grad_values = nn(weights.astype(BF), some_grads)
            grad_keys = nn(grad_scores, some)
            turned = tn(keys, grad_scores)
            if fresh:
                grad_query_sum[:, first:last] = turned
            else:
                grad_query_sum[:, first:last] += turned
            return grad_keys * SCORE_SCALE, grad_values

        for part in range(2):
            rows = slice(part * HALF, (part + 1) * HALF)
            grad_keys, grad_values = chunk(
                state_key[rows, columns], state_value[rows, columns], 0, W + S, None, part == 0
            )
            grad_states[1, rows, columns] = grad_keys.astype(BF)
            grad_states[2, rows, columns] = grad_values.astype(BF)
        for part in range(2):
            rows = slice(part * HALF, (part + 1) * HALF)
            row = lax.broadcasted_iota(jnp.int32, (HALF, HALF), 0)
            column = lax.broadcasted_iota(jnp.int32, (HALF, HALF), 1)
            mask = row <= column + flags[2 * block + part] * HALF
            grad_keys, grad_values = chunk(
                key[rows, columns], value[rows, columns], part * HALF, W + S, mask, False
            )
            grad_tokens[1, rows, columns] = (grad_keys + carry_key[half, rows, columns]).astype(BF)
            grad_tokens[2, rows, columns] = (
                grad_values + carry_value[half, rows, columns]
            ).astype(BF)

        @pl.when(block > 0)
        def before():
            for part in range(2):
                rows = slice(part * HALF, (part + 1) * HALF)
                grad_keys, grad_values = chunk(
                    key_before[rows, columns], value_before[rows, columns], 0, W, None, False
                )
                carry_key[half, rows, columns] = grad_keys
                carry_value[half, rows, columns] = grad_values

        grad_query = (grad_query_sum[...] * SCORE_SCALE).T
        grad_tokens[0, :, columns] = grad_query[:W].astype(BF)
        grad_states[0, :, columns] = grad_query[W:].astype(BF)
        return carry

    lax.fori_loop(0, local, head, 0)
    grad_normed[...] += (
        nt(grad_states[0], weight_query[...])
        + nt(grad_states[1], weight_key[...])
        + nt(grad_states[2], more_weight[:, :width])
        + nt(grad_states[3], more_weight[:, width:])
    )

    @pl.when(half == 1)
    def finish():
        here = state_in[...]
        inverse = inverse_rms(here)
        scaled = here * inverse
        grad = grad_normed[...]
        grad_gain[...] += jnp.sum(grad * scaled, axis=0, keepdims=True)
        grad_state[...] = forget[...] * grad_state[...] + rms_back(
            scaled, inverse, gain[...] * grad
        )

    @pl.when((half == 1) & (block == 0))
    def end():
        grad_init[...] = grad_state[...].astype(BF)


def backward(
    flags,
    query,
    key,
    value,
    state_query,
    state_key,
    state_value,
    token_mixed,
    state_mixed,
    grad_mixed,
    totals,
    forget,
    state_in,
    apart,
    gain,
    weights,
    more_weights,
):
    blocks = query.shape[0] // W
    heads = D // HEAD
    half_width = D // 2

    def rev(b):
        return blocks - 1 - b

    own = pl.BlockSpec((W, half_width), lambda b, t, s: (rev(b), t))
    before = pl.BlockSpec((W, half_width), lambda b, t, s: (jnp.maximum(rev(b) - 1, 0), t))
    whole = pl.BlockSpec((S, D), lambda b, t, s: (rev(b), 0))
    fixed_row = pl.BlockSpec((1, D), lambda b, t, s: (0, 0))
    return pl.pallas_call(
        backward_kernel,
        grid_spec=pltpu.PrefetchScalarGridSpec(
            num_scalar_prefetch=1,
            grid=(blocks, 2),
            in_specs=[own, own, own, before, before]
            + [own] * 6
            + [pl.BlockSpec((1, 2 * heads, W), lambda b, t, s: (rev(b), 0, 0))]
            + [whole] * 3
            + [
                once((1, D), lambda b, t, s: (0, 0)),
                pl.BlockSpec((D, half_width), lambda b, t, s: (t, 3)),
                pl.BlockSpec((D, half_width), lambda b, t, s: (t, 4)),
                pl.BlockSpec((D, 2 * half_width), lambda b, t, s: (t, 0)),
                once((D, half_width), lambda b, t, s: (0, 2)),
                once((D, half_width), lambda b, t, s: (1, 2)),
            ],
            out_specs=[
                pl.BlockSpec((3, W, half_width), lambda b, t, s: (0, rev(b), t)),
                pl.BlockSpec((4, S, half_width), lambda b, t, s: (0, rev(b), t)),
                pl.BlockSpec((D, S), lambda b, t, s: (0, rev(b))),
                pl.BlockSpec((S, D), lambda b, t, s: (0, 0)),
                fixed_row,
                fixed_row,
            ],
            scratch_shapes=[
                pltpu.VMEM((S, D), F32),
                pltpu.VMEM((2, S, half_width), BF),
                pltpu.VMEM((S, D), F32),
                pltpu.VMEM((2, S, half_width), BF),
                pltpu.VMEM((2, W, half_width), F32),
                pltpu.VMEM((2, W, half_width), F32),
                pltpu.VMEM((HEAD, W + S), F32),
                pltpu.VMEM((1, W + S), F32),
                pltpu.VMEM((W + S, HEAD), BF),
                pltpu.VMEM((W + S, HEAD), BF),
            ],
        ),
        out_shape=[
            jax.ShapeDtypeStruct((3, blocks * W, D), BF),
            jax.ShapeDtypeStruct((4, blocks * W, D), BF),
            jax.ShapeDtypeStruct((D, blocks * W), BF),
            jax.ShapeDtypeStruct((S, D), BF),
            jax.ShapeDtypeStruct((1, D), F32),
            jax.ShapeDtypeStruct((1, D), F32),
        ],
        compiler_params=params(("arbitrary", "arbitrary")),
        cost_estimate=cost(70e9, 100e6, 40e6),
        name="backward",
    )(
        flags,
        query,
        key,
        value,
        key,
        value,
        state_query,
        state_key,
        state_value,
        token_mixed,
        state_mixed,
        grad_mixed,
        totals,
        forget,
        state_in,
        apart,
        gain,
        weights,
        weights,
        more_weights,
        more_weights,
        more_weights,
    )


def whole_grad_kernel(turned, right, into, out):
    out[...] = nn(turned[...], right[...]).astype(BF)


def whole_weight_grad(turned, right, into):
    tokens = right.shape[0]
    width = D // 2
    last = into.shape[1] // width - 1
    return pl.pallas_call(
        whole_grad_kernel,
        grid=(2,),
        in_specs=[
            once((D, tokens), lambda g: (0, 0)),
            pl.BlockSpec((tokens, width), lambda g: (0, g)),
            pl.BlockSpec(memory_space=pl.ANY),
        ],
        out_specs=pl.BlockSpec((D, width), lambda g: (g, last)),
        out_shape=jax.ShapeDtypeStruct(into.shape, BF),
        input_output_aliases={2: 0},
        compiler_params=params(),
        cost_estimate=cost(2 * tokens * D * D, 2 * (tokens * D + 2 * D * D)),
        name="whole_weight_grad",
    )(turned, right, into)


def weight_grad_kernel(groups, core, turned, right, *rest):
    keep, send = rest[-2:]
    grads = nn(turned[...], right[0]).astype(BF)
    group = turned.shape[0] // groups
    grads = grads.reshape(groups // 2, 2, group, grads.shape[1])
    shape = keep.shape
    low = grads[:, 0].reshape(shape)
    high = grads[:, 1].reshape(shape)
    mine = core[0] == 0
    keep[...] = jnp.where(mine, low, high)
    send[...] = jnp.where(mine, high, low)


def weight_grads(dp, core, turned, rights, first=0, many=1, across=0, at=0, into=None):
    tokens = rights.shape[1]
    width = D // 2
    across = across or many
    out = jax.ShapeDtypeStruct((D, across * width), BF)
    tile = pl.BlockSpec((D // 2, width), lambda g, s: (g % 2, at + g // 2))
    into = into or ()
    return pl.pallas_call(
        functools.partial(weight_grad_kernel, dp),
        grid_spec=pltpu.PrefetchScalarGridSpec(
            num_scalar_prefetch=1,
            grid=(2 * many,),
            in_specs=[
                once((D, tokens), lambda g, s: (0, 0)),
                pl.BlockSpec((1, tokens, width), lambda g, s: (first + g // 2, 0, g % 2)),
            ]
            + [pl.BlockSpec(memory_space=pl.ANY)] * len(into),
            out_specs=[tile, tile],
        ),
        out_shape=[out, out],
        input_output_aliases={3 + i: i for i in range(len(into))},
        compiler_params=params(),
        cost_estimate=cost(2 * tokens * D * D * many, 2 * (tokens * D + 2 * many * D * D)),
        name="weight_grads",
    )(core, turned, rights, *into)


def token_grad_kernel(grads, w0, w1, rows, grad_middle, gain, out, grad_gain):
    width = w0.shape[1] // 3
    total = None
    for which in range(3):
        for half, weight in enumerate((w0, w1)):
            part = nt(
                grads[which, :, half * width : (half + 1) * width],
                weight[:, which * width : (which + 1) * width],
            )
            total = part if total is None else total + part
    here = rows[...].astype(F32)
    inverse = inverse_rms(here)
    scaled = here * inverse
    out[...] = (
        grad_middle[...].astype(F32) + rms_back(scaled, inverse, gain[...] * total)
    ).astype(BF)
    part = jnp.sum(total * scaled, axis=0, keepdims=True)

    @pl.when(pl.program_id(0) == 0)
    def first():
        grad_gain[...] = part

    @pl.when(pl.program_id(0) > 0)
    def later():
        grad_gain[...] += part


def token_grad(grads, weights, rows, grad_middle, gain):
    tokens = rows.shape[0]
    width = 3 * D // 2
    block = pl.BlockSpec((W, D), lambda b: (b, 0))
    return pl.pallas_call(
        token_grad_kernel,
        grid=(tokens // W,),
        in_specs=[
            pl.BlockSpec((3, W, D), lambda b: (0, b, 0)),
            once((D, width), lambda b: (0, 0)),
            once((D, width), lambda b: (1, 0)),
            block,
            block,
            once((1, D), lambda b: (0, 0)),
        ],
        out_specs=[block, pl.BlockSpec((1, D), lambda b: (0, 0))],
        out_shape=[jax.ShapeDtypeStruct((tokens, D), BF), jax.ShapeDtypeStruct((1, D), F32)],
        compiler_params=params(),
        cost_estimate=cost(2 * tokens * 3 * D * D, 2 * 6 * tokens * D),
        name="token_grad",
    )(grads, weights, weights, rows, grad_middle, gain)


def gather(local):
    return lax.all_gather(local, ("tensor", "dp"), axis=0, tiled=True)


def scatter(total):
    return lax.psum_scatter(total, ("tensor", "dp"), scatter_dimension=0, tiled=True)


def axes_of(dp):
    return ["tensor"] + list(reversed(range(dp.bit_length() - 1)))


def side_of(axis):
    if axis == "tensor":
        return lax.axis_index("tensor")
    return (lax.axis_index("dp") >> axis) & 1


def trade(values, axis, dp):
    if axis == "tensor":
        return lax.ppermute(values, "tensor", [(0, 1), (1, 0)])
    return lax.ppermute(values, "dp", [(i, i ^ (1 << axis)) for i in range(dp)])


def order_of(dp, turn):
    bits = dp.bit_length() - 1
    middle = ["tensor"] + ([1] if bits > 1 else [])
    if turn:
        middle = middle[::-1]
    return ([0] if bits else []) + middle + list(reversed(range(2, bits)))


class Halving:
    def __init__(self, keep, send, dp, turn):
        self.dp = dp
        self.axes = axes_of(dp)
        self.left = order_of(dp, turn)
        self.rest = 2 * keep.shape[0] >> len(self.axes)
        self.keep = keep
        self.sent = send

    def send(self):
        axis = self.left[0]
        where = self.axes.index(axis)
        columns = self.part.shape[1]
        many = len(self.axes) - where - 1
        pairs = self.part.reshape(1 << where, 2, self.rest << many, columns)
        side = side_of(axis)
        self.sent = lax.dynamic_index_in_dim(pairs, 1 - side, 1, keepdims=False)
        self.keep = lax.dynamic_index_in_dim(pairs, side, 1, keepdims=False)
        return self.sent

    def go(self):
        self.come = trade(self.sent, self.left[0], self.dp)

    def add(self, earlier=None):
        come = self.come if earlier is None else after(self.come, earlier)
        total = (self.keep.astype(F32) + come.astype(F32)).astype(BF)
        self.part = total.reshape(-1, total.shape[-1])
        self.axes.remove(self.left.pop(0))
        if self.left:
            self.send()


def finish(many):
    while any(one.left for one in many):
        active = [one for one in many if one.left]
        for one in active:
            one.go()
        for one, come in zip(active, lax.optimization_barrier([one.come for one in active])):
            one.come = come
            one.add()
    return [one.part for one in many]


def split_core(total, dp):
    groups = total.reshape(dp, 2, total.shape[0] // (2 * dp), total.shape[1])
    side = side_of(0)
    keep = lax.dynamic_index_in_dim(groups, side, 1, keepdims=False)
    send = lax.dynamic_index_in_dim(groups, 1 - side, 1, keepdims=False)
    return [one.reshape(total.shape[0] // 2, total.shape[1]) for one in (keep, send)]


def gather_steps(local, dp, turn, earlier):
    axes = axes_of(dp)
    done = []
    part = local
    for axis in reversed(order_of(dp, turn)):
        if axis == "tensor":
            part = after(part, earlier)
        come = trade(part, axis, dp)
        low = side_of(axis) == 0
        done = [one for one in axes if one == axis or one in done]
        lead = 1 << done.index(axis)
        pair = [jnp.where(low, part, come), jnp.where(low, come, part)]
        pair = [one.reshape(lead, part.shape[0] // lead, part.shape[1]) for one in pair]
        part = jnp.stack(pair, axis=1).reshape(2 * part.shape[0], part.shape[1])
    return part


def after(values, earlier):
    return lax.optimization_barrier((values, earlier))[0]


def whole_sequence_body(
    tokens_in,
    piece_starts,
    cotangent,
    gain_tokens,
    gain_mlp,
    gain_state,
    gate_bias,
    w_query,
    w_key,
    w_value,
    w_out,
    w_state_query,
    w_state_key,
    w_state_value,
    w_state_out,
    w_gate,
    w_up,
    w_down,
    state_init,
):
    mine = lax.axis_index("tensor")
    first = mine == 0
    local_rows = w_query.shape[0]
    dp = D // local_rows
    width = w_query.shape[1]
    units = 512
    across = w_up.shape[1] // units
    swap = [(0, 1), (1, 0)]

    def other_half(pair):
        return lax.ppermute(jnp.where(first, pair[1, 0], pair[0, 0]), "tensor", swap)

    def bring(pair, come):
        keep = jnp.where(first, pair[0, 0], pair[1, 0])
        top = jnp.where(first, keep, come)
        low = jnp.where(first, come, keep)
        return jnp.concatenate([top, low], axis=1).reshape(NB * W, D)

    def give(rows, later=None):
        halves = rows.reshape(NB, 2, HALF, D)
        keep = jnp.where(first, halves[:, 0], halves[:, 1])
        send = jnp.where(first, halves[:, 1], halves[:, 0])
        come = lax.ppermute(send, "tensor", swap)
        if later is not None:
            come = after(come, later)
        return jnp.stack([jnp.where(first, keep, come), jnp.where(first, come, keep)])[:, None]

    def split_init(values):
        side = values.shape[1] // 2
        return jnp.concatenate([values[:, :side], values[:, side:]], axis=0)

    gains = jnp.stack([gain_tokens, gain_mlp, gain_state, gate_bias])
    small = jnp.concatenate(
        [split_init(state_init), jnp.pad(gains, ((0, local_rows - 4), (0, 128 - local_rows)))],
        axis=1,
    )
    full_qkv = gather(
        jnp.concatenate([w_query, w_key, w_value, w_state_query, w_state_key, small], axis=1)
    )
    full_small = full_qkv[:, 5 * width :]
    turned_down = w_down.T
    late = []
    for unit in range(0, across * units, units):
        late += [w_up[:, unit : unit + units], turned_down[:, unit : unit + units]]
    late = jnp.concatenate(late + [w_out.T], axis=1)
    rows = bring(tokens_in, other_half(tokens_in))
    full_state1 = gather_steps(
        jnp.concatenate([w_state_value, w_gate, w_state_out.T], axis=1), dp, False, (rows, late)
    )
    full_late = gather(after(late, (full_qkv, full_state1)))
    side = width // 2
    init = full_small[:, :side].reshape(2, dp, 2, local_rows // 2, side)
    init = jnp.transpose(init, (1, 3, 0, 2, 4)).reshape(S, D)
    gains = full_small[:D, side:].reshape(dp, local_rows, 128)[:, :4, :local_rows]
    gains = jnp.transpose(gains, (1, 0, 2)).reshape(4, 1, D).astype(F32)

    cot_half = other_half(after(cotangent, rows))
    starts = jnp.where(first, piece_starts[0, 0], piece_starts[1, 0])
    flags = jnp.any(
        starts[:, None] == PIECE * jnp.arange(NB * W // PIECE, dtype=jnp.int32)[None], axis=0
    ).astype(jnp.int32)

    turned, query, key, value = project(rows, gains[0], full_qkv)
    (
        token_mixed,
        state_mixed,
        state_turned,
        state_query,
        state_key,
        state_value,
        state_in,
        forget,
        apart,
        totals,
    ) = forward(flags, query, key, value, init, gains[2], gains[3], full_qkv, full_state1)
    cot = bring(cotangent, after(cot_half, token_mixed))
    middle, mlp_in, mlp_turned, cot_turned = middle_rows(
        rows, token_mixed, full_late, gains[1], cot
    )
    mlp_out, grad_mlp_in, grad_mlp_w = mlp(mlp_in, mlp_turned, cot, cot_turned, full_late)
    output, grad_middle, middle_turned, grad_mixed, grad_gain_mlp = after_mlp(
        middle, mlp_out, grad_mlp_in, cot, gains[1], full_late
    )
    grads_late = whole_weight_grad(middle_turned, token_mixed, grad_mlp_w)
    part_late = scatter(grads_late)
    core = (side_of(0) & 1).astype(jnp.int32).reshape(1)
    grad_tok, grad_sta, branch, grad_init, grad_gain_state, grad_bias = backward(
        flags,
        query,
        key,
        value,
        state_query,
        state_key,
        state_value,
        token_mixed,
        state_mixed,
        after(grad_mixed, grads_late),
        totals,
        forget,
        state_in,
        apart,
        gains[2],
        full_qkv,
        full_state1,
    )
    given_output = give(output, grad_tok)

    a = Halving(*weight_grads(dp, core, state_turned, after(grad_sta, given_output), 0, 2), dp, False)
    a.go()
    b = Halving(*weight_grads(dp, core, state_turned, after(grad_sta, a.sent), 2, 2), dp, True)
    a.add(b.keep)
    a.go()
    b.go()
    c = Halving(*weight_grads(dp, core, turned, after(grad_tok, (a.sent, b.sent)), 1, 2), dp, False)
    b.add(c.keep)
    b.go()
    c.go()
    grads_q = weight_grads(dp, core, turned, after(grad_tok, (b.sent, c.sent)), 0, 1, 2, 0)
    c.add(grads_q)
    c.go()
    d = Halving(
        *weight_grads(dp, core, after(branch, c.sent), state_mixed[None], 0, 1, 2, 1, grads_q),
        dp,
        True,
    )
    d.go()
    grad_in, grad_gain_tokens = token_grad(
        after(grad_tok, (d.sent, part_late)), full_qkv, rows, grad_middle, gains[0]
    )
    a.add(grad_in)
    d.add(grad_in)
    b.add(grad_in)
    init_parts = jnp.transpose(
        grad_init.reshape(dp, local_rows // 2, 2, 2, side), (2, 0, 3, 1, 4)
    ).reshape(2 * D, side)
    gain_parts = jnp.stack(
        [grad_gain_tokens[0], grad_gain_mlp[0], grad_gain_state[0], grad_bias[0]]
    ).reshape(4, dp, local_rows)
    gain_parts = jnp.pad(
        jnp.transpose(gain_parts, (1, 0, 2)),
        ((0, 0), (0, local_rows - 4), (0, 128 - local_rows)),
    ).reshape(D, 128)
    gain_parts = jnp.concatenate([gain_parts, gain_parts], axis=0).astype(BF)
    e = Halving(*split_core(jnp.concatenate([init_parts, gain_parts], axis=1), dp), dp, True)
    given_grad = give(grad_in)
    part_rest, part_kv, part_sqk, part_svg, part_small = [
        one.astype(F32) for one in finish([d, c, a, b, e])
    ]
    part_so = part_rest[:, width:]
    part_init = part_small[:, :side]
    part_init = jnp.concatenate(
        [part_init[: local_rows // 2], part_init[local_rows // 2 :]], axis=1
    )
    part_gains = part_small[:4, side : side + local_rows]
    part_late = part_late.astype(F32)
    part_up = [part_late[:, 2 * i * units : (2 * i + 1) * units] for i in range(across)]
    part_down = [part_late[:, (2 * i + 1) * units : (2 * i + 2) * units] for i in range(across)]
    part_sqk = part_sqk.astype(F32)
    part_svg = part_svg.astype(F32)
    return (
        given_output,
        given_grad,
        part_gains[0],
        part_gains[1],
        part_gains[2],
        part_gains[3],
        part_rest[:, :width],
        part_kv[:, :width],
        part_kv[:, width:],
        part_late[:, 2 * across * units :].T,
        part_sqk[:, :width],
        part_sqk[:, width:],
        part_svg[:, :width],
        part_so.T,
        part_svg[:, width:],
        jnp.concatenate(part_up, axis=1),
        jnp.concatenate([one.T for one in part_down], axis=0),
        part_init,
    )


def solution(mesh):
    dp = mesh.shape["dp"]
    one_each = mesh.shape["tensor"] == MICRO and dp > 1 and dp & (dp - 1) == 0
    return jax.shard_map(
        whole_sequence_body if one_each else generic_body,
        mesh=mesh,
        in_specs=(
            P(None, "dp", None, "tensor", None),
            P(None, "dp", None),
            P(None, "dp", None, "tensor", None),
            P("dp"),
            P("dp"),
            P("dp"),
            P("dp"),
            P("dp", "tensor"),
            P("dp", "tensor"),
            P("dp", "tensor"),
            P("tensor", "dp"),
            P("dp", "tensor"),
            P("dp", "tensor"),
            P("dp", "tensor"),
            P("tensor", "dp"),
            P("dp", "tensor"),
            P("dp", "tensor"),
            P("tensor", "dp"),
            P("dp", "tensor"),
        ),
        out_specs=(
            P(None, "dp", None, "tensor", None),
            P(None, "dp", None, "tensor", None),
            P("dp"),
            P("dp"),
            P("dp"),
            P("dp"),
            P("dp", "tensor"),
            P("dp", "tensor"),
            P("dp", "tensor"),
            P("tensor", "dp"),
            P("dp", "tensor"),
            P("dp", "tensor"),
            P("dp", "tensor"),
            P("tensor", "dp"),
            P("dp", "tensor"),
            P("dp", "tensor"),
            P("tensor", "dp"),
            P("dp", "tensor"),
        ),
        check_vma=False,
    )
```

```python
import functools
import math

import jax
import jax.numpy as jnp
from jax import lax
from jax.experimental import pallas as pl
from jax.experimental.pallas import tpu as pltpu
from jax.sharding import PartitionSpec as P

D = 1024
HEAD = 128
W = 512
S = 512
PIECE = 256
MICRO = 2
NB = 4


epsilon = 1e-06
masked_score = -1e30


def rms_scale(values):
    return values * lax.rsqrt(jnp.mean(values * values, axis=-1, keepdims=True) + epsilon)


def normed_rows(values, gain):
    return rms_scale(values) * gain


def matmul(left, right):
    return jnp.dot(left, right, preferred_element_type=jnp.float32)


def mlp_local(full_in, full_up, full_down):
    hidden = matmul(full_in, full_up)
    active = jax.nn.gelu(hidden).astype(jnp.bfloat16)
    return (hidden, active, matmul(active, full_down))


def mlp_back_local(full_grad, active, hidden, full_in, full_down, full_up):
    grad_down_w = jnp.einsum("...f,...d->fd", active, full_grad, preferred_element_type=jnp.float32)
    grad_active = jnp.einsum(
        "...d,fd->...f", full_grad, full_down, preferred_element_type=jnp.float32
    )
    unused_value, gelu_back = jax.vjp(jax.nn.gelu, hidden)
    grad_hidden = gelu_back(grad_active)[0].astype(jnp.bfloat16)
    grad_up_w = jnp.einsum(
        "...d,...f->df", full_in, grad_hidden, preferred_element_type=jnp.float32
    )
    mlp_part = jnp.einsum("...f,df->...d", grad_hidden, full_up, preferred_element_type=jnp.float32)
    return (grad_down_w, grad_up_w, mlp_part)


def piece_labels(starts):
    positions = jnp.arange(NB * W, dtype=jnp.int32)
    inside = (positions[None, None, :] >= starts[:, :, None]) & (
        positions[None, None, :] < starts[:, :, None] + PIECE
    )
    numbers = jnp.arange(1, starts.shape[1] + 1, dtype=jnp.int32)
    return jnp.sum(jnp.where(inside, numbers[None, :, None], 0), axis=1)


def token_mask(labels, block):
    batch = labels.shape[0]
    own = labels[:, block * W : (block + 1) * W]
    local = jnp.arange(W, dtype=jnp.int32)
    causal = (local[None, :] <= local[:, None])[None]
    together = (own[:, :, None] == own[:, None, :]) & (own[:, :, None] > 0)
    current = causal | together
    earlier = jnp.full((batch, W, W), block > 0)
    state_part = jnp.ones((batch, W, S), dtype=bool)
    return jnp.concatenate([earlier, current, state_part], axis=2)[:, None]


def split_heads(values):
    return values.reshape(values.shape[0], values.shape[1], values.shape[2] // HEAD, HEAD)


def scores_of(query, keys, allowed):
    scores = jnp.einsum(
        "brhe,bkhe->bhrk", split_heads(query), split_heads(keys), preferred_element_type=jnp.float32
    ) * (1.0 / math.sqrt(HEAD))
    return jnp.where(allowed, scores, masked_score)


def attend(query, keys, values, allowed):
    scores = scores_of(query, keys, allowed)
    top = jnp.max(scores, axis=-1, keepdims=True)
    total = top + jnp.log(jnp.sum(jnp.exp(scores - top), axis=-1, keepdims=True))
    weights = jnp.exp(scores - total).astype(jnp.bfloat16)
    mixed = jnp.einsum(
        "bhrk,bkhe->brhe", weights, split_heads(values), preferred_element_type=jnp.float32
    )
    return (mixed.reshape(query.shape).astype(jnp.bfloat16), total)


def attend_back(query, keys, values, allowed, total, grad_mixed):
    scale = 1.0 / math.sqrt(HEAD)
    weights = jnp.exp(scores_of(query, keys, allowed) - total)
    grad_heads = split_heads(grad_mixed)
    grad_weights = jnp.einsum(
        "brhe,bkhe->bhrk", grad_heads, split_heads(values), preferred_element_type=jnp.float32
    )
    grad_scores = (
        weights * (grad_weights - jnp.sum(weights * grad_weights, axis=-1, keepdims=True))
    ).astype(jnp.bfloat16)
    grad_query = (
        jnp.einsum(
            "bhrk,bkhe->brhe", grad_scores, split_heads(keys), preferred_element_type=jnp.float32
        )
        * scale
    )
    grad_keys = (
        jnp.einsum(
            "bhrk,brhe->bkhe", grad_scores, split_heads(query), preferred_element_type=jnp.float32
        )
        * scale
    )
    grad_values = jnp.einsum(
        "bhrk,brhe->bkhe",
        weights.astype(jnp.bfloat16),
        grad_heads,
        preferred_element_type=jnp.float32,
    )
    return (
        grad_query.reshape(query.shape),
        grad_keys.reshape(keys.shape),
        grad_values.reshape(values.shape),
    )


def generic_body(
    tokens_in,
    piece_starts,
    cotangent,
    gain_tokens,
    gain_mlp,
    gain_state,
    gate_bias,
    w_query,
    w_key,
    w_value,
    w_out,
    w_state_query,
    w_state_key,
    w_state_value,
    w_state_out,
    w_gate,
    w_up,
    w_down,
    state_init,
):
    width_local = w_query.shape[1]
    column_start = lax.axis_index("tensor") * width_local

    def collect():
        return (
            lax.all_gather(w_query, "dp", axis=0, tiled=True),
            lax.all_gather(w_key, "dp", axis=0, tiled=True),
            lax.all_gather(w_value, "dp", axis=0, tiled=True),
            lax.all_gather(w_state_query, "dp", axis=0, tiled=True),
            lax.all_gather(w_state_key, "dp", axis=0, tiled=True),
            lax.all_gather(w_state_value, "dp", axis=0, tiled=True),
            lax.all_gather(w_gate, "dp", axis=0, tiled=True),
            lax.all_gather(w_up, "dp", axis=0, tiled=True),
            lax.all_gather(state_init, "dp", axis=0, tiled=True),
            lax.all_gather(w_out, "dp", axis=1, tiled=True),
            lax.all_gather(w_state_out, "dp", axis=1, tiled=True),
            lax.all_gather(w_down, "dp", axis=1, tiled=True),
            lax.all_gather(gain_tokens, "dp", axis=0, tiled=True),
            lax.all_gather(gain_mlp, "dp", axis=0, tiled=True),
            lax.all_gather(gain_state, "dp", axis=0, tiled=True),
            lax.all_gather(gate_bias, "dp", axis=0, tiled=True),
        )

    def unpack_gains(weights):
        token_gain = weights[12].astype(jnp.float32)
        mlp_gain = weights[13].astype(jnp.float32)
        state_gain = lax.dynamic_slice_in_dim(
            weights[14].astype(jnp.float32), column_start, width_local
        )
        bias_columns = lax.dynamic_slice_in_dim(
            weights[15].astype(jnp.float32), column_start, width_local
        )
        return (token_gain, mlp_gain, state_gain, bias_columns)

    outputs = []
    input_grads = []
    totals = None
    for micro in range(MICRO):
        forward_weights = collect()
        forward_rows_in = tokens_in[micro]
        (
            forward_full_query,
            forward_full_key,
            forward_full_value,
            forward_full_state_query,
            forward_full_state_key,
            forward_full_state_value,
            forward_full_gate,
            forward_full_up,
            forward_full_init,
            forward_full_out,
            forward_full_state_out,
            forward_full_down,
        ) = forward_weights[:12]
        forward_token_gain, forward_mlp_gain, forward_state_gain, forward_bias_columns = (
            unpack_gains(forward_weights)
        )
        forward_batch = forward_rows_in.shape[0]
        forward_labels = piece_labels(piece_starts[micro])
        forward_state = jnp.broadcast_to(
            forward_full_init.astype(jnp.float32), (forward_batch, S, width_local)
        )
        zero_keys = jnp.zeros((forward_batch, W, width_local), jnp.bfloat16)
        forward_earlier_key = zero_keys
        forward_earlier_value = zero_keys
        forward_kept = []
        middles = []
        for forward_block in range(NB):
            forward_rows = forward_rows_in[:, forward_block].astype(jnp.float32)
            normed = normed_rows(forward_rows, forward_token_gain).astype(jnp.bfloat16)
            square_sum = lax.psum(jnp.sum(forward_state * forward_state, axis=-1), "tensor")
            forward_inverse = lax.rsqrt(square_sum / D + epsilon)[..., None]
            forward_scaled = forward_state * forward_inverse
            state_normed = (forward_scaled * forward_state_gain).astype(jnp.bfloat16)
            forward_full_normed, forward_full_state = (
                lax.all_gather(normed, "tensor", axis=1, tiled=True),
                lax.all_gather(state_normed, "tensor", axis=2, tiled=True),
            )
            forward_query = matmul(forward_full_normed, forward_full_query).astype(jnp.bfloat16)
            forward_key = matmul(forward_full_normed, forward_full_key).astype(jnp.bfloat16)
            forward_value = matmul(forward_full_normed, forward_full_value).astype(jnp.bfloat16)
            forward_state_query = matmul(forward_full_state, forward_full_state_query).astype(
                jnp.bfloat16
            )
            forward_state_key = matmul(forward_full_state, forward_full_state_key).astype(
                jnp.bfloat16
            )
            forward_state_value = matmul(forward_full_state, forward_full_state_value).astype(
                jnp.bfloat16
            )
            gate_pre = matmul(forward_full_state, forward_full_gate) + forward_bias_columns
            forward_allowed = token_mask(forward_labels, forward_block)
            forward_token_keys = jnp.concatenate(
                [forward_earlier_key, forward_key, forward_state_key], axis=1
            )
            forward_token_values = jnp.concatenate(
                [forward_earlier_value, forward_value, forward_state_value], axis=1
            )
            forward_token_mixed, forward_token_total = attend(
                forward_query, forward_token_keys, forward_token_values, forward_allowed
            )
            forward_cross_keys = jnp.concatenate([forward_key, forward_state_key], axis=1)
            forward_cross_values = jnp.concatenate([forward_value, forward_state_value], axis=1)
            forward_state_mixed, forward_state_total = attend(
                forward_state_query, forward_cross_keys, forward_cross_values, True
            )
            forward_row_part = matmul(forward_token_mixed, forward_full_out)
            forward_state_part = matmul(forward_state_mixed, forward_full_state_out)
            row_sum, forward_state_sum = (
                lax.psum_scatter(
                    forward_row_part.astype(jnp.bfloat16), "tensor", scatter_dimension=1, tiled=True
                ).astype(jnp.float32),
                lax.psum_scatter(
                    forward_state_part.astype(jnp.bfloat16),
                    "tensor",
                    scatter_dimension=2,
                    tiled=True,
                ).astype(jnp.float32),
            )
            forward_forget = jax.nn.sigmoid(gate_pre)
            forward_kept.append(
                (
                    forward_full_normed,
                    forward_full_state,
                    forward_query,
                    forward_key,
                    forward_value,
                    forward_state_query,
                    forward_state_key,
                    forward_state_value,
                    forward_token_mixed,
                    forward_state_mixed,
                    forward_token_total,
                    forward_state_total,
                    forward_state,
                    forward_scaled,
                    forward_inverse,
                    forward_forget,
                    forward_state_sum,
                    forward_earlier_key,
                    forward_earlier_value,
                )
            )
            middle_block = forward_rows + row_sum
            middles.append(middle_block)
            forward_state = (
                forward_forget * forward_state + (1.0 - forward_forget) * forward_state_sum
            )
            forward_earlier_key, forward_earlier_value = (forward_key, forward_value)
        forward_middle = jnp.stack(middles, axis=1)
        mlp_in = normed_rows(forward_middle, forward_mlp_gain).astype(jnp.bfloat16)
        forward_full_mlp_in = lax.all_gather(mlp_in, "tensor", axis=2, tiled=True)
        forward_hidden, forward_active, mlp_partial = mlp_local(
            forward_full_mlp_in, forward_full_up, forward_full_down
        )
        mlp_sum = lax.psum_scatter(
            mlp_partial.astype(jnp.bfloat16), "tensor", scatter_dimension=2, tiled=True
        ).astype(jnp.float32)
        output = (forward_middle + mlp_sum).astype(jnp.bfloat16)
        output, saved = (
            output,
            (
                forward_kept,
                forward_middle,
                forward_full_mlp_in,
                forward_hidden,
                forward_active,
                forward_labels,
            ),
        )
        outputs.append(output)
        backward_weights = collect()
        rows_in = tokens_in[micro]
        grad_rows_out = cotangent[micro]
        (
            full_query,
            full_key,
            full_value,
            full_state_query,
            full_state_key,
            full_state_value,
            full_gate,
            full_up,
            full_init,
            full_out,
            full_state_out,
            full_down,
        ) = backward_weights[:12]
        backward_token_gain, backward_mlp_gain, backward_state_gain, backward_bias_columns = (
            unpack_gains(backward_weights)
        )
        kept, middle, full_mlp_in, hidden, active, labels = saved
        batch = rows_in.shape[0]
        full_grad = lax.all_gather(grad_rows_out, "tensor", axis=2, tiled=True)
        grad_down_w, grad_up_w, mlp_part = mlp_back_local(
            full_grad, active, hidden, full_mlp_in, full_down, full_up
        )
        grad_mlp_in = lax.psum_scatter(
            mlp_part.astype(jnp.bfloat16), "tensor", scatter_dimension=2, tiled=True
        ).astype(jnp.float32)
        unused_norm, mlp_norm_back = jax.vjp(normed_rows, middle, backward_mlp_gain)
        grad_middle_norm, grad_mlp_gain = mlp_norm_back(grad_mlp_in)
        grad_middle = grad_rows_out.astype(jnp.float32) + grad_middle_norm
        grad_state = jnp.zeros((batch, S, width_local), jnp.float32)
        carry_key = jnp.zeros((batch, W, width_local), jnp.float32)
        carry_value = jnp.zeros((batch, W, width_local), jnp.float32)
        square_zero = jnp.zeros((D, width_local), jnp.float32)
        grad_query_w = square_zero
        grad_key_w = square_zero
        grad_value_w = square_zero
        grad_state_query_w = square_zero
        grad_state_key_w = square_zero
        grad_state_value_w = square_zero
        grad_gate_w = square_zero
        grad_out_w = jnp.zeros((width_local, D), jnp.float32)
        grad_state_out_w = jnp.zeros((width_local, D), jnp.float32)
        grad_token_gain = jnp.zeros((D,), jnp.float32)
        grad_state_gain = jnp.zeros((width_local,), jnp.float32)
        grad_bias = jnp.zeros((width_local,), jnp.float32)
        grad_rows = [None] * NB
        for block in reversed(range(NB)):
            (
                full_normed,
                full_state,
                query,
                key,
                value,
                state_query,
                state_key,
                state_value,
                token_mixed,
                state_mixed,
                token_total,
                state_total,
                state,
                scaled,
                inverse,
                forget,
                state_sum,
                earlier_key,
                earlier_value,
            ) = kept[block]
            grad_row_block = grad_middle[:, block]
            grad_branch_state = ((1.0 - forget) * grad_state).astype(jnp.bfloat16)
            grad_gate = (grad_state * (state - state_sum) * forget * (1.0 - forget)).astype(
                jnp.bfloat16
            )
            carried_state = grad_state * forget
            full_grad_rows, full_grad_state = (
                lax.all_gather(grad_row_block.astype(jnp.bfloat16), "tensor", axis=1, tiled=True),
                lax.all_gather(grad_branch_state, "tensor", axis=2, tiled=True),
            )
            grad_out_w = grad_out_w + jnp.einsum(
                "bwc,bwd->cd", token_mixed, full_grad_rows, preferred_element_type=jnp.float32
            )
            grad_state_out_w = grad_state_out_w + jnp.einsum(
                "bsc,bsd->cd", state_mixed, full_grad_state, preferred_element_type=jnp.float32
            )
            grad_token_mixed = jnp.einsum(
                "bwd,cd->bwc", full_grad_rows, full_out, preferred_element_type=jnp.float32
            ).astype(jnp.bfloat16)
            grad_state_mixed = jnp.einsum(
                "bsd,cd->bsc", full_grad_state, full_state_out, preferred_element_type=jnp.float32
            ).astype(jnp.bfloat16)
            allowed = token_mask(labels, block)
            token_keys = jnp.concatenate([earlier_key, key, state_key], axis=1)
            token_values = jnp.concatenate([earlier_value, value, state_value], axis=1)
            cross_keys = jnp.concatenate([key, state_key], axis=1)
            cross_values = jnp.concatenate([value, state_value], axis=1)
            token_grad_query, token_grad_keys, token_grad_values = attend_back(
                query, token_keys, token_values, allowed, token_total, grad_token_mixed
            )
            state_grad_query, cross_grad_keys, cross_grad_values = attend_back(
                state_query, cross_keys, cross_values, True, state_total, grad_state_mixed
            )
            grad_key = (token_grad_keys[:, W : 2 * W] + cross_grad_keys[:, :W] + carry_key).astype(
                jnp.bfloat16
            )
            grad_value = (
                token_grad_values[:, W : 2 * W] + cross_grad_values[:, :W] + carry_value
            ).astype(jnp.bfloat16)
            carry_key = token_grad_keys[:, :W]
            carry_value = token_grad_values[:, :W]
            grad_state_key = (token_grad_keys[:, 2 * W :] + cross_grad_keys[:, W:]).astype(
                jnp.bfloat16
            )
            grad_state_value = (token_grad_values[:, 2 * W :] + cross_grad_values[:, W:]).astype(
                jnp.bfloat16
            )
            grad_query = token_grad_query.astype(jnp.bfloat16)
            grad_state_query = state_grad_query.astype(jnp.bfloat16)
            grad_query_w = grad_query_w + jnp.einsum(
                "bwd,bwc->dc", full_normed, grad_query, preferred_element_type=jnp.float32
            )
            grad_key_w = grad_key_w + jnp.einsum(
                "bwd,bwc->dc", full_normed, grad_key, preferred_element_type=jnp.float32
            )
            grad_value_w = grad_value_w + jnp.einsum(
                "bwd,bwc->dc", full_normed, grad_value, preferred_element_type=jnp.float32
            )
            grad_state_query_w = grad_state_query_w + jnp.einsum(
                "bsd,bsc->dc", full_state, grad_state_query, preferred_element_type=jnp.float32
            )
            grad_state_key_w = grad_state_key_w + jnp.einsum(
                "bsd,bsc->dc", full_state, grad_state_key, preferred_element_type=jnp.float32
            )
            grad_state_value_w = grad_state_value_w + jnp.einsum(
                "bsd,bsc->dc", full_state, grad_state_value, preferred_element_type=jnp.float32
            )
            grad_gate_w = grad_gate_w + jnp.einsum(
                "bsd,bsc->dc", full_state, grad_gate, preferred_element_type=jnp.float32
            )
            grad_bias = grad_bias + jnp.sum(grad_gate.astype(jnp.float32), axis=(0, 1))
            row_part = jnp.einsum(
                "bwc,dc->bwd", grad_query, full_query, preferred_element_type=jnp.float32
            )
            row_part = row_part + jnp.einsum(
                "bwc,dc->bwd", grad_key, full_key, preferred_element_type=jnp.float32
            )
            row_part = row_part + jnp.einsum(
                "bwc,dc->bwd", grad_value, full_value, preferred_element_type=jnp.float32
            )
            state_part = jnp.einsum(
                "bsc,dc->bsd",
                grad_state_query,
                full_state_query,
                preferred_element_type=jnp.float32,
            )
            state_part = state_part + jnp.einsum(
                "bsc,dc->bsd", grad_state_key, full_state_key, preferred_element_type=jnp.float32
            )
            state_part = state_part + jnp.einsum(
                "bsc,dc->bsd",
                grad_state_value,
                full_state_value,
                preferred_element_type=jnp.float32,
            )
            state_part = state_part + jnp.einsum(
                "bsc,dc->bsd", grad_gate, full_gate, preferred_element_type=jnp.float32
            )
            grad_normed, grad_state_normed = (
                lax.psum_scatter(
                    row_part.astype(jnp.bfloat16), "tensor", scatter_dimension=1, tiled=True
                ).astype(jnp.float32),
                lax.psum_scatter(
                    state_part.astype(jnp.bfloat16), "tensor", scatter_dimension=2, tiled=True
                ).astype(jnp.float32),
            )
            rows = rows_in[:, block].astype(jnp.float32)
            unused_rows, token_norm_back = jax.vjp(normed_rows, rows, backward_token_gain)
            grad_rows_norm, grad_gain_part = token_norm_back(grad_normed)
            grad_token_gain = grad_token_gain + grad_gain_part
            grad_rows[block] = (grad_row_block + grad_rows_norm).astype(jnp.bfloat16)
            grad_scaled = grad_state_normed * backward_state_gain
            grad_state_gain = grad_state_gain + jnp.sum(grad_state_normed * scaled, axis=(0, 1))
            dot_sum = lax.psum(jnp.sum(grad_scaled * scaled, axis=-1), "tensor")
            grad_state = carried_state + inverse * (grad_scaled - scaled * (dot_sum / D)[..., None])
        grad_init = jnp.sum(grad_state, axis=0)
        state_gain_full = lax.dynamic_update_slice_in_dim(
            jnp.zeros((D,), jnp.float32), grad_state_gain, column_start, 0
        )
        bias_full = lax.dynamic_update_slice_in_dim(
            jnp.zeros((D,), jnp.float32), grad_bias, column_start, 0
        )
        grads = (
            grad_query_w,
            grad_key_w,
            grad_value_w,
            grad_state_query_w,
            grad_state_key_w,
            grad_state_value_w,
            grad_gate_w,
            grad_up_w,
            grad_init,
            grad_out_w,
            grad_state_out_w,
            grad_down_w,
            grad_token_gain,
            grad_mlp_gain,
            state_gain_full,
            bias_full,
        )
        grads, grad_in = (grads, jnp.stack(grad_rows, axis=1))
        input_grads.append(grad_in)
        if totals is None:
            totals = grads
        else:
            totals = tuple((first + second for first, second in zip(totals, grads)))
    reduced = (
        lax.psum_scatter(
            totals[0].astype(jnp.bfloat16), "dp", scatter_dimension=0, tiled=True
        ).astype(jnp.float32),
        lax.psum_scatter(
            totals[1].astype(jnp.bfloat16), "dp", scatter_dimension=0, tiled=True
        ).astype(jnp.float32),
        lax.psum_scatter(
            totals[2].astype(jnp.bfloat16), "dp", scatter_dimension=0, tiled=True
        ).astype(jnp.float32),
        lax.psum_scatter(
            totals[3].astype(jnp.bfloat16), "dp", scatter_dimension=0, tiled=True
        ).astype(jnp.float32),
        lax.psum_scatter(
            totals[4].astype(jnp.bfloat16), "dp", scatter_dimension=0, tiled=True
        ).astype(jnp.float32),
        lax.psum_scatter(
            totals[5].astype(jnp.bfloat16), "dp", scatter_dimension=0, tiled=True
        ).astype(jnp.float32),
        lax.psum_scatter(
            totals[6].astype(jnp.bfloat16), "dp", scatter_dimension=0, tiled=True
        ).astype(jnp.float32),
        lax.psum_scatter(
            totals[7].astype(jnp.bfloat16), "dp", scatter_dimension=0, tiled=True
        ).astype(jnp.float32),
        lax.psum_scatter(
            totals[8].astype(jnp.bfloat16), "dp", scatter_dimension=0, tiled=True
        ).astype(jnp.float32),
        lax.psum_scatter(
            totals[9].astype(jnp.bfloat16), "dp", scatter_dimension=1, tiled=True
        ).astype(jnp.float32),
        lax.psum_scatter(
            totals[10].astype(jnp.bfloat16), "dp", scatter_dimension=1, tiled=True
        ).astype(jnp.float32),
        lax.psum_scatter(
            totals[11].astype(jnp.bfloat16), "dp", scatter_dimension=1, tiled=True
        ).astype(jnp.float32),
        lax.psum_scatter(
            totals[12].astype(jnp.bfloat16), "dp", scatter_dimension=0, tiled=True
        ).astype(jnp.float32),
        lax.psum_scatter(
            totals[13].astype(jnp.bfloat16), "dp", scatter_dimension=0, tiled=True
        ).astype(jnp.float32),
        lax.psum_scatter(
            totals[14].astype(jnp.bfloat16), "dp", scatter_dimension=0, tiled=True
        ).astype(jnp.float32),
        lax.psum_scatter(
            totals[15].astype(jnp.bfloat16), "dp", scatter_dimension=0, tiled=True
        ).astype(jnp.float32),
    )
    gain_totals = lax.psum((reduced[12], reduced[13], reduced[14], reduced[15]), "tensor")
    return (
        jnp.stack(outputs, axis=0),
        jnp.stack(input_grads, axis=0),
        gain_totals[0],
        gain_totals[1],
        gain_totals[2],
        gain_totals[3],
        reduced[0],
        reduced[1],
        reduced[2],
        reduced[9],
        reduced[3],
        reduced[4],
        reduced[5],
        reduced[10],
        reduced[6],
        reduced[7],
        reduced[11],
        reduced[8],
    )


BF = jnp.bfloat16
F32 = jnp.float32
HALF = 256
VMEM_BYTES = 60 * 1024 * 1024
EXP2_SCALE = math.log2(math.e) / math.sqrt(HEAD)
SCORE_SCALE = 1.0 / math.sqrt(HEAD)


def nn(left, right):
    return lax.dot_general(left, right, (((1,), (0,)), ((), ())), preferred_element_type=F32)


def nt(left, right):
    return lax.dot_general(left, right, (((1,), (1,)), ((), ())), preferred_element_type=F32)


def tn(left, right):
    return lax.dot_general(left, right, (((0,), (0,)), ((), ())), preferred_element_type=F32)


def inverse_rms(values):
    return lax.rsqrt(jnp.mean(values * values, axis=-1, keepdims=True) + epsilon)


def rms_back(scaled, inverse, grad):
    return (grad - scaled * jnp.mean(grad * scaled, axis=-1, keepdims=True)) * inverse


def params(semantics=("arbitrary",)):
    return pltpu.CompilerParams(dimension_semantics=semantics, vmem_limit_bytes=VMEM_BYTES)


def cost(flops, moved, transcendentals=0):
    return pl.CostEstimate(
        flops=int(flops), bytes_accessed=int(moved), transcendentals=int(transcendentals)
    )


def once(shape, index):
    return pl.BlockSpec(shape, index, pipeline_mode=pl.Buffered(1))


def project_kernel(rows, gain, w0, w1, turned, query, key, value):
    width = w0.shape[1] // 3
    wide = rows[...].astype(F32)
    normed = (wide * inverse_rms(wide) * gain[...]).astype(BF)
    turned[...] = normed.T
    for half, weight in enumerate((w0, w1)):
        for which, out in enumerate((query, key, value)):
            out[:, half * width : (half + 1) * width] = nn(
                normed, weight[:, which * width : (which + 1) * width]
            ).astype(BF)


def project(rows, gain, weights):
    tokens = rows.shape[0]
    width = 3 * D // 2
    out = jax.ShapeDtypeStruct((tokens, D), BF)
    block = pl.BlockSpec((W, D), lambda b: (b, 0))
    return pl.pallas_call(
        project_kernel,
        grid=(tokens // W,),
        in_specs=[
            block,
            once((1, D), lambda b: (0, 0)),
            once((D, width), lambda b: (0, 0)),
            once((D, width), lambda b: (1, 0)),
        ],
        out_specs=[pl.BlockSpec((D, W), lambda b: (0, b))] + [block] * 3,
        out_shape=[jax.ShapeDtypeStruct((D, tokens), BF)] + [out] * 3,
        compiler_params=params(),
        cost_estimate=cost(2 * tokens * D * 3 * D, 2 * (5 * tokens * D + 3 * D * D)),
        name="project",
    )(rows, gain, weights, weights)


def softmax_parts(parts):
    top = parts[0][0].max(axis=1, keepdims=True)
    for scores, unused in parts[1:]:
        top = jnp.maximum(top, scores.max(axis=1, keepdims=True))
    mixed = None
    for scores, values in parts:
        weights = jnp.exp2((scores - top) * EXP2_SCALE)
        wide_values = jnp.concatenate([values, jnp.ones_like(values)], axis=1)
        part_mixed = nn(weights.astype(BF), wide_values)
        mixed = part_mixed if mixed is None else mixed + part_mixed
    total = mixed[:, HEAD:]
    return (mixed[:, :HEAD] / total).astype(BF), top * EXP2_SCALE + jnp.log2(total)


def forward_kernel(
    flags,
    query,
    key,
    value,
    key_before,
    value_before,
    init,
    gain,
    bias,
    query0,
    query1,
    key0,
    key1,
    second0,
    second1,
    token_mixed,
    state_mixed,
    turned,
    state_query,
    state_key,
    state_value,
    state_in,
    forget,
    apart,
    totals,
    state,
    token_totals,
    state_totals,
):
    block = pl.program_id(0)
    width = query0.shape[1]

    @pl.when(block == 0)
    def start():
        state[...] = init[...].astype(F32)

    now = state[...]
    state_in[...] = now
    state_normed = (now * inverse_rms(now) * gain[...]).astype(BF)
    turned[...] = state_normed.T
    for half, (one, other, two) in enumerate(((query0, key0, second0), (query1, key1, second1))):
        columns = slice(half * width, (half + 1) * width)
        state_query[:, columns] = nn(state_normed, one[...]).astype(BF)
        state_key[:, columns] = nn(state_normed, other[...]).astype(BF)
        state_value[:, columns] = nn(state_normed, two[:, :width]).astype(BF)
        gate = nn(state_normed, two[:, width : 2 * width]) + bias[:, columns]
        forget[:, columns] = jax.nn.sigmoid(gate)

    def heads(with_before):
        def head(index, carry):
            columns = pl.ds(pl.multiple_of(index * HEAD, HEAD), HEAD)
            lane = lax.broadcasted_iota(jnp.int32, (W, HEAD), 1) == index
            row = lax.broadcasted_iota(jnp.int32, (W, W), 0)
            column = lax.broadcasted_iota(jnp.int32, (W, W), 1)
            lead = jnp.where(row < HALF, flags[2 * block] * (HALF - 1 - row), flags[2 * block + 1] * (W - 1 - row))
            reach = column <= row + lead
            own = query[:, columns]
            parts = []
            if with_before:
                parts.append((nt(own, key_before[:, columns]), value_before[:, columns]))
            near = jnp.where(reach, nt(own, key[:, columns]), masked_score)
            parts.append((near, value[:, columns]))
            parts.append((nt(own, state_key[:, columns]), state_value[:, columns]))
            mixed, total = softmax_parts(parts)
            token_mixed[:, columns] = mixed
            token_totals[...] = jnp.where(lane, total, token_totals[...])
            own = state_query[:, columns]
            mixed, total = softmax_parts(
                [
                    (nt(own, key[:, columns]), value[:, columns]),
                    (nt(own, state_key[:, columns]), state_value[:, columns]),
                ]
            )
            state_mixed[:, columns] = mixed
            state_totals[...] = jnp.where(lane, total, state_totals[...])
            return carry

        lax.fori_loop(0, D // HEAD, head, 0, unroll=2)

    @pl.when(block == 0)
    def first():
        heads(False)

    @pl.when(block > 0)
    def later():
        heads(True)

    count = D // HEAD
    totals[0, :count, :] = token_totals[...].T[:count]
    totals[0, count:, :] = state_totals[...].T[:count]
    new = nt(state_mixed[:, :width], second0[:, 2 * width :]) + nt(
        state_mixed[:, width:], second1[:, 2 * width :]
    )
    apart[...] = (now - new).astype(BF)
    state[...] = new + forget[...] * (now - new)


def forward(flags, query, key, value, init, gain, bias, weights, more_weights):
    blocks = query.shape[0] // W
    heads = D // HEAD
    own = pl.BlockSpec((W, D), lambda b, s: (b, 0))
    before = pl.BlockSpec((W, D), lambda b, s: (jnp.maximum(b - 1, 0), 0))
    low = jax.ShapeDtypeStruct((blocks * W, D), BF)
    wide = jax.ShapeDtypeStruct((blocks * W, D), F32)
    return pl.pallas_call(
        forward_kernel,
        grid_spec=pltpu.PrefetchScalarGridSpec(
            num_scalar_prefetch=1,
            grid=(blocks,),
            in_specs=[
                own,
                own,
                own,
                before,
                before,
                once((S, D), lambda b, s: (0, 0)),
                once((1, D), lambda b, s: (0, 0)),
                once((1, D), lambda b, s: (0, 0)),
                once((D, D // 2), lambda b, s: (0, 3)),
                once((D, D // 2), lambda b, s: (1, 3)),
                once((D, D // 2), lambda b, s: (0, 4)),
                once((D, D // 2), lambda b, s: (1, 4)),
                once((D, more_weights.shape[1]), lambda b, s: (0, 0)),
                once((D, more_weights.shape[1]), lambda b, s: (1, 0)),
            ],
            out_specs=[own] * 2
            + [pl.BlockSpec((D, S), lambda b, s: (0, b))]
            + [own] * 6
            + [pl.BlockSpec((1, 2 * heads, W), lambda b, s: (b, 0, 0))],
            scratch_shapes=[
                pltpu.VMEM((S, D), F32),
                pltpu.VMEM((W, HEAD), F32),
                pltpu.VMEM((S, HEAD), F32),
            ],
        ),
        out_shape=[low] * 2
        + [jax.ShapeDtypeStruct((D, blocks * S), BF)]
        + [low] * 3
        + [wide, wide, low, jax.ShapeDtypeStruct((blocks, 2 * heads, W), F32)],
        compiler_params=params(),
        cost_estimate=cost(42e9, 100e6, 40e6),
        name="forward",
    )(
        flags,
        query,
        key,
        value,
        key,
        value,
        init,
        gain,
        bias,
        weights,
        weights,
        weights,
        weights,
        more_weights,
        more_weights,
    )


def middle_kernel(rows, mixed, w0, w1, gain, cotangent, middle, mlp_in, mlp_turned, cot_turned):
    width = w0.shape[1]
    here = (
        rows[...].astype(F32) + nt(mixed[:, :width], w0[...]) + nt(mixed[:, width:], w1[...])
    )
    middle[...] = here
    low = (here * inverse_rms(here) * gain[...]).astype(BF)
    mlp_in[...] = low
    mlp_turned[...] = low.T
    cot_turned[...] = cotangent[...].T


def middle_rows(rows, mixed, weights, gain, cotangent):
    tokens = rows.shape[0]
    width = D // 2
    last = weights.shape[1] // width - 1
    block = pl.BlockSpec((W, D), lambda b: (b, 0))
    turned = pl.BlockSpec((D, W), lambda b: (0, b))
    low = jax.ShapeDtypeStruct((tokens, D), BF)
    return pl.pallas_call(
        middle_kernel,
        grid=(tokens // W,),
        in_specs=[
            block,
            block,
            once((D, width), lambda b: (0, last)),
            once((D, width), lambda b: (1, last)),
            once((1, D), lambda b: (0, 0)),
            block,
        ],
        out_specs=[block, block, turned, turned],
        out_shape=[
            jax.ShapeDtypeStruct((tokens, D), F32),
            low,
            jax.ShapeDtypeStruct((D, tokens), BF),
            jax.ShapeDtypeStruct((D, tokens), BF),
        ],
        compiler_params=params(),
        cost_estimate=cost(2 * tokens * D * D, 2 * 8 * tokens * D),
        name="middle",
    )(rows, mixed, weights, weights, gain, cotangent)


def mlp_kernel(
    mlp_in, mlp_turned, cot, cot_turned, weights, out, grad_in, grads, out_sum, grad_sum, act, gh
):
    step = pl.program_id(0)
    units = weights.shape[1] // 2
    tokens = mlp_in.shape[0]

    @pl.when(step == 0)
    def start():
        out_sum[...] = jnp.zeros_like(out_sum)
        grad_sum[...] = jnp.zeros_like(grad_sum)

    slope = math.sqrt(2.0 / math.pi)

    def chunk(index, carry):
        rows = pl.ds(pl.multiple_of(index * W, W), W)
        hidden = nn(mlp_in[rows, :], weights[:, :units])
        back = nn(cot[rows, :], weights[:, units:])
        square = hidden * hidden
        bent = jnp.tanh(slope * hidden * (1.0 + 0.044715 * square))
        open_part = 0.5 * (1.0 + bent)
        active = (hidden * open_part).astype(BF)
        steep = open_part + (0.5 * slope) * hidden * (1.0 - bent * bent) * (
            1.0 + (3 * 0.044715) * square
        )
        grad = (steep * back).astype(BF)
        act[rows, :] = active
        gh[rows, :] = grad
        out_sum[rows, :] += nt(active, weights[:, units:])
        grad_sum[rows, :] += nt(grad, weights[:, :units])
        return carry

    lax.fori_loop(0, tokens // W, chunk, 0)
    grads[:, :units] = nn(mlp_turned[...], gh[...]).astype(BF)
    grads[:, units:] = nn(cot_turned[...], act[...]).astype(BF)

    @pl.when(step == pl.num_programs(0) - 1)
    def end():
        out[...] = out_sum[...].astype(BF)
        grad_in[...] = grad_sum[...].astype(BF)


def mlp(mlp_in, mlp_turned, cot, cot_turned, weights):
    tokens = mlp_in.shape[0]
    units = 512
    across = (weights.shape[1] - D // 2) // (2 * units)
    low = jax.ShapeDtypeStruct((tokens, D), BF)
    rows = once((tokens, D), lambda f: (0, 0))
    turned = once((D, tokens), lambda f: (0, 0))
    tile = pl.BlockSpec((D, 2 * units), lambda f: (f // across, f % across))
    return pl.pallas_call(
        mlp_kernel,
        grid=(2 * across,),
        in_specs=[rows, turned, rows, turned, tile],
        out_specs=[rows, rows, tile],
        out_shape=[low, low, jax.ShapeDtypeStruct(weights.shape, BF)],
        scratch_shapes=[
            pltpu.VMEM((tokens, D), F32),
            pltpu.VMEM((tokens, D), F32),
            pltpu.VMEM((tokens, units), BF),
            pltpu.VMEM((tokens, units), BF),
        ],
        compiler_params=params(),
        cost_estimate=cost(103e9, 60e6, 8e6),
        name="mlp",
    )(mlp_in, mlp_turned, cot, cot_turned, weights)


def after_mlp_kernel(
    middle, mlp_out, grad_in, cot, gain, w0, w1, output, grad_middle, turned, grad_mixed, grad_gain
):
    width = w0.shape[1]
    here = middle[...]
    inverse = inverse_rms(here)
    scaled = here * inverse
    grad = grad_in[...].astype(F32)
    output[...] = (here + mlp_out[...].astype(F32)).astype(BF)
    low = (cot[...].astype(F32) + rms_back(scaled, inverse, gain[...] * grad)).astype(BF)
    grad_middle[...] = low
    turned[...] = low.T
    grad_mixed[:, :width] = nn(low, w0[...]).astype(BF)
    grad_mixed[:, width:] = nn(low, w1[...]).astype(BF)
    part = jnp.sum(grad * scaled, axis=0, keepdims=True)

    @pl.when(pl.program_id(0) == 0)
    def first():
        grad_gain[...] = part

    @pl.when(pl.program_id(0) > 0)
    def later():
        grad_gain[...] += part


def after_mlp(middle, mlp_out, grad_in, cot, gain, weights):
    tokens = middle.shape[0]
    width = D // 2
    last = weights.shape[1] // width - 1
    block = pl.BlockSpec((W, D), lambda b: (b, 0))
    low = jax.ShapeDtypeStruct((tokens, D), BF)
    return pl.pallas_call(
        after_mlp_kernel,
        grid=(tokens // W,),
        in_specs=[
            block,
            block,
            block,
            block,
            once((1, D), lambda b: (0, 0)),
            once((D, width), lambda b: (0, last)),
            once((D, width), lambda b: (1, last)),
        ],
        out_specs=[
            block,
            block,
            pl.BlockSpec((D, W), lambda b: (0, b)),
            block,
            pl.BlockSpec((1, D), lambda b: (0, 0)),
        ],
        out_shape=[
            low,
            low,
            jax.ShapeDtypeStruct((D, tokens), BF),
            low,
            jax.ShapeDtypeStruct((1, D), F32),
        ],
        compiler_params=params(),
        cost_estimate=cost(2 * tokens * D * D, 2 * 8 * tokens * D),
        name="after_mlp",
    )(middle, mlp_out, grad_in, cot, gain, weights, weights)


def backward_kernel(
    flags,
    query,
    key,
    value,
    key_before,
    value_before,
    state_query,
    state_key,
    state_value,
    token_mixed,
    state_mixed,
    grad_mixed,
    totals,
    forget,
    state_in,
    apart,
    gain,
    weight_query,
    weight_key,
    more_weight,
    wso0,
    wso1,
    grad_tokens,
    grad_states,
    branch,
    grad_init,
    grad_gain,
    grad_bias,
    grad_state,
    grad_state_mixed,
    grad_normed,
    gate_part,
    carry_key,
    carry_value,
):
    step = pl.program_id(0)
    half = pl.program_id(1)
    block = pl.num_programs(0) - 1 - step
    width = wso0.shape[1]
    local = width // HEAD
    count = D // HEAD

    @pl.when((step == 0) & (half == 0))
    def start():
        grad_state[...] = jnp.zeros_like(grad_state)
        carry_key[...] = jnp.zeros_like(carry_key)
        carry_value[...] = jnp.zeros_like(carry_value)
        grad_gain[...] = jnp.zeros_like(grad_gain)
        grad_bias[...] = jnp.zeros_like(grad_bias)

    @pl.when(half == 0)
    def begin():
        coming = grad_state[...]
        keep = forget[...]
        low = ((1.0 - keep) * coming).astype(BF)
        branch[...] = low.T
        gate = (coming * apart[...].astype(F32) * keep * (1.0 - keep)).astype(BF)
        gate_part[0] = gate[:, :width]
        gate_part[1] = gate[:, width:]
        grad_bias[...] += jnp.sum(gate.astype(F32), axis=0, keepdims=True)
        grad_state_mixed[0] = nn(low, wso0[...]).astype(BF)
        grad_state_mixed[1] = nn(low, wso1[...]).astype(BF)
        grad_normed[...] = jnp.zeros_like(grad_normed)

    grad_states[3] = gate_part[half]

    def heads(with_before):
        def head(index, carry):
            columns = pl.ds(pl.multiple_of(index * HEAD, HEAD), HEAD)
            at = half * local + index
            queries = jnp.concatenate([query[:, columns], state_query[:, columns]], axis=0)
            grads_out = jnp.concatenate(
                [grad_mixed[:, columns], grad_state_mixed[half, :, columns]], axis=0
            )
            mixed = jnp.concatenate([token_mixed[:, columns], state_mixed[:, columns]], axis=0)
            product = grads_out.astype(F32) * mixed.astype(F32)
            delta = jnp.sum(product.T, axis=0, keepdims=True)
            token_total = totals[0, pl.ds(at, 1), :]
            state_total = totals[0, pl.ds(count + at, 1), :]
            total = jnp.concatenate([token_total, state_total], axis=1)

            def chunk(keys, values, first, last, mask):
                some = queries[first:last]
                some_grads = grads_out[first:last]
                scores = nt(keys, some)
                if mask is not None:
                    size = mask.shape[1]
                    scores = jnp.concatenate(
                        [jnp.where(mask, scores[:, :size], masked_score), scores[:, size:]], axis=1
                    )
                weights = jnp.exp2(scores * EXP2_SCALE - total[:, first:last])
                back = nt(values, some_grads) - delta[:, first:last]
                grad_scores = (weights * back).astype(BF)
                grad_values = nn(weights.astype(BF), some_grads)
                grad_keys = nn(grad_scores, some)
                return grad_keys * SCORE_SCALE, grad_values, tn(keys, grad_scores)

            turned = None
            for first in range(0, S, HALF):
                rows = slice(first, first + HALF)
                grad_keys, grad_values, part = chunk(
                    state_key[rows, columns], state_value[rows, columns], 0, W + S, None
                )
                grad_states[1, rows, columns] = grad_keys.astype(BF)
                grad_states[2, rows, columns] = grad_values.astype(BF)
                turned = part if turned is None else turned + part
            for part in range(2):
                rows = slice(part * HALF, (part + 1) * HALF)
                row = lax.broadcasted_iota(jnp.int32, (HALF, HALF), 0)
                column = lax.broadcasted_iota(jnp.int32, (HALF, HALF), 1)
                mask = row <= column + flags[2 * block + part] * HALF
                grad_keys, grad_values, more = chunk(
                    key[rows, columns], value[rows, columns], part * HALF, W + S, mask
                )
                grad_tokens[1, rows, columns] = (grad_keys + carry_key[half, rows, columns]).astype(
                    BF
                )
                grad_tokens[2, rows, columns] = (
                    grad_values + carry_value[half, rows, columns]
                ).astype(BF)
                if part:
                    more = jnp.concatenate([jnp.zeros((HEAD, HALF), F32), more], axis=1)
                turned = turned + more
            turned_tokens = turned[:, :W]
            if with_before:
                for first in range(0, W, HALF):
                    rows = slice(first, first + HALF)
                    grad_keys, grad_values, part = chunk(
                        key_before[rows, columns], value_before[rows, columns], 0, W, None
                    )
                    carry_key[half, rows, columns] = grad_keys
                    carry_value[half, rows, columns] = grad_values
                    turned_tokens = turned_tokens + part
            grad_tokens[0, :, columns] = (turned_tokens * SCORE_SCALE).T.astype(BF)
            grad_states[0, :, columns] = (turned[:, W:] * SCORE_SCALE).T.astype(BF)
            return carry

        lax.fori_loop(0, local, head, 0, unroll=2)

    @pl.when(block > 0)
    def later():
        heads(True)

    @pl.when(block == 0)
    def first():
        heads(False)

    grad_normed[...] += (
        nt(grad_states[0], weight_query[...])
        + nt(grad_states[1], weight_key[...])
        + nt(grad_states[2], more_weight[:, :width])
        + nt(grad_states[3], more_weight[:, width:])
    )

    @pl.when(half == 1)
    def finish():
        here = state_in[...]
        inverse = inverse_rms(here)
        scaled = here * inverse
        grad = grad_normed[...]
        grad_gain[...] += jnp.sum(grad * scaled, axis=0, keepdims=True)
        grad_state[...] = forget[...] * grad_state[...] + rms_back(
            scaled, inverse, gain[...] * grad
        )

    @pl.when((half == 1) & (block == 0))
    def end():
        grad_init[...] = grad_state[...].astype(BF)


def backward(
    flags,
    query,
    key,
    value,
    state_query,
    state_key,
    state_value,
    token_mixed,
    state_mixed,
    grad_mixed,
    totals,
    forget,
    state_in,
    apart,
    gain,
    weights,
    more_weights,
):
    blocks = query.shape[0] // W
    heads = D // HEAD
    half_width = D // 2

    def rev(b):
        return blocks - 1 - b

    own = pl.BlockSpec((W, half_width), lambda b, t, s: (rev(b), t))
    before = pl.BlockSpec((W, half_width), lambda b, t, s: (jnp.maximum(rev(b) - 1, 0), t))
    whole = pl.BlockSpec((S, D), lambda b, t, s: (rev(b), 0))
    fixed_row = pl.BlockSpec((1, D), lambda b, t, s: (0, 0))
    return pl.pallas_call(
        backward_kernel,
        grid_spec=pltpu.PrefetchScalarGridSpec(
            num_scalar_prefetch=1,
            grid=(blocks, 2),
            in_specs=[own, own, own, before, before]
            + [own] * 6
            + [pl.BlockSpec((1, 2 * heads, W), lambda b, t, s: (rev(b), 0, 0))]
            + [whole] * 3
            + [
                once((1, D), lambda b, t, s: (0, 0)),
                pl.BlockSpec((D, half_width), lambda b, t, s: (t, 3)),
                pl.BlockSpec((D, half_width), lambda b, t, s: (t, 4)),
                pl.BlockSpec((D, 2 * half_width), lambda b, t, s: (t, 0)),
                once((D, half_width), lambda b, t, s: (0, 2)),
                once((D, half_width), lambda b, t, s: (1, 2)),
            ],
            out_specs=[
                pl.BlockSpec((3, W, half_width), lambda b, t, s: (0, rev(b), t)),
                pl.BlockSpec((4, S, half_width), lambda b, t, s: (0, rev(b), t)),
                pl.BlockSpec((D, S), lambda b, t, s: (0, rev(b))),
                pl.BlockSpec((S, D), lambda b, t, s: (0, 0)),
                fixed_row,
                fixed_row,
            ],
            scratch_shapes=[
                pltpu.VMEM((S, D), F32),
                pltpu.VMEM((2, S, half_width), BF),
                pltpu.VMEM((S, D), F32),
                pltpu.VMEM((2, S, half_width), BF),
                pltpu.VMEM((2, W, half_width), F32),
                pltpu.VMEM((2, W, half_width), F32),
            ],
        ),
        out_shape=[
            jax.ShapeDtypeStruct((3, blocks * W, D), BF),
            jax.ShapeDtypeStruct((4, blocks * W, D), BF),
            jax.ShapeDtypeStruct((D, blocks * W), BF),
            jax.ShapeDtypeStruct((S, D), BF),
            jax.ShapeDtypeStruct((1, D), F32),
            jax.ShapeDtypeStruct((1, D), F32),
        ],
        compiler_params=params(("arbitrary", "arbitrary")),
        cost_estimate=cost(70e9, 100e6, 40e6),
        name="backward",
    )(
        flags,
        query,
        key,
        value,
        key,
        value,
        state_query,
        state_key,
        state_value,
        token_mixed,
        state_mixed,
        grad_mixed,
        totals,
        forget,
        state_in,
        apart,
        gain,
        weights,
        weights,
        more_weights,
        more_weights,
        more_weights,
    )


def whole_grad_kernel(turned, right, into, out):
    out[...] = nn(turned[...], right[...]).astype(BF)


def whole_weight_grad(turned, right, into):
    tokens = right.shape[0]
    width = D // 2
    last = into.shape[1] // width - 1
    return pl.pallas_call(
        whole_grad_kernel,
        grid=(2,),
        in_specs=[
            once((D, tokens), lambda g: (0, 0)),
            pl.BlockSpec((tokens, width), lambda g: (0, g)),
            pl.BlockSpec(memory_space=pl.ANY),
        ],
        out_specs=pl.BlockSpec((D, width), lambda g: (g, last)),
        out_shape=jax.ShapeDtypeStruct(into.shape, BF),
        input_output_aliases={2: 0},
        compiler_params=params(),
        cost_estimate=cost(2 * tokens * D * D, 2 * (tokens * D + 2 * D * D)),
        name="whole_weight_grad",
    )(turned, right, into)


def weight_grad_kernel(groups, core, turned, right, *rest):
    keep, send = rest[-2:]
    grads = nn(turned[...], right[0]).astype(BF)
    group = turned.shape[0] // groups
    grads = grads.reshape(groups // 2, 2, group, grads.shape[1])
    shape = keep.shape
    low = grads[:, 0].reshape(shape)
    high = grads[:, 1].reshape(shape)
    mine = core[0] == 0
    keep[...] = jnp.where(mine, low, high)
    send[...] = jnp.where(mine, high, low)


def weight_grads(dp, core, turned, rights, first=0, many=1, across=0, at=0, into=None):
    tokens = rights.shape[1]
    width = D // 2
    across = across or many
    out = jax.ShapeDtypeStruct((D, across * width), BF)
    tile = pl.BlockSpec((D // 2, width), lambda g, s: (g % 2, at + g // 2))
    into = into or ()
    return pl.pallas_call(
        functools.partial(weight_grad_kernel, dp),
        grid_spec=pltpu.PrefetchScalarGridSpec(
            num_scalar_prefetch=1,
            grid=(2 * many,),
            in_specs=[
                once((D, tokens), lambda g, s: (0, 0)),
                pl.BlockSpec((1, tokens, width), lambda g, s: (first + g // 2, 0, g % 2)),
            ]
            + [pl.BlockSpec(memory_space=pl.ANY)] * len(into),
            out_specs=[tile, tile],
        ),
        out_shape=[out, out],
        input_output_aliases={3 + i: i for i in range(len(into))},
        compiler_params=params(),
        cost_estimate=cost(2 * tokens * D * D * many, 2 * (tokens * D + 2 * many * D * D)),
        name="weight_grads",
    )(core, turned, rights, *into)


def token_grad_kernel(grads, w0, w1, rows, grad_middle, gain, out, grad_gain):
    width = w0.shape[1] // 3
    total = None
    for which in range(3):
        for half, weight in enumerate((w0, w1)):
            part = nt(
                grads[which, :, half * width : (half + 1) * width],
                weight[:, which * width : (which + 1) * width],
            )
            total = part if total is None else total + part
    here = rows[...].astype(F32)
    inverse = inverse_rms(here)
    scaled = here * inverse
    out[...] = (
        grad_middle[...].astype(F32) + rms_back(scaled, inverse, gain[...] * total)
    ).astype(BF)
    part = jnp.sum(total * scaled, axis=0, keepdims=True)

    @pl.when(pl.program_id(0) == 0)
    def first():
        grad_gain[...] = part

    @pl.when(pl.program_id(0) > 0)
    def later():
        grad_gain[...] += part


def token_grad(grads, weights, rows, grad_middle, gain):
    tokens = rows.shape[0]
    width = 3 * D // 2
    block = pl.BlockSpec((W, D), lambda b: (b, 0))
    return pl.pallas_call(
        token_grad_kernel,
        grid=(tokens // W,),
        in_specs=[
            pl.BlockSpec((3, W, D), lambda b: (0, b, 0)),
            once((D, width), lambda b: (0, 0)),
            once((D, width), lambda b: (1, 0)),
            block,
            block,
            once((1, D), lambda b: (0, 0)),
        ],
        out_specs=[block, pl.BlockSpec((1, D), lambda b: (0, 0))],
        out_shape=[jax.ShapeDtypeStruct((tokens, D), BF), jax.ShapeDtypeStruct((1, D), F32)],
        compiler_params=params(),
        cost_estimate=cost(2 * tokens * 3 * D * D, 2 * 6 * tokens * D),
        name="token_grad",
    )(grads, weights, weights, rows, grad_middle, gain)


def gather(local):
    return lax.all_gather(local, ("tensor", "dp"), axis=0, tiled=True)


def scatter(total):
    return lax.psum_scatter(total, ("tensor", "dp"), scatter_dimension=0, tiled=True)


def axes_of(dp):
    return ["tensor"] + list(reversed(range(dp.bit_length() - 1)))


def side_of(axis):
    if axis == "tensor":
        return lax.axis_index("tensor")
    return (lax.axis_index("dp") >> axis) & 1


def trade(values, axis, dp):
    if axis == "tensor":
        return lax.ppermute(values, "tensor", [(0, 1), (1, 0)])
    return lax.ppermute(values, "dp", [(i, i ^ (1 << axis)) for i in range(dp)])


def order_of(dp, turn):
    bits = dp.bit_length() - 1
    middle = ["tensor"] + ([1] if bits > 1 else [])
    if turn:
        middle = middle[::-1]
    return ([0] if bits else []) + middle + list(reversed(range(2, bits)))


class Halving:
    def __init__(self, keep, send, dp, turn):
        self.dp = dp
        self.axes = axes_of(dp)
        self.left = order_of(dp, turn)
        self.rest = 2 * keep.shape[0] >> len(self.axes)
        self.keep = keep
        self.sent = send

    def send(self):
        axis = self.left[0]
        where = self.axes.index(axis)
        columns = self.part.shape[1]
        many = len(self.axes) - where - 1
        pairs = self.part.reshape(1 << where, 2, self.rest << many, columns)
        side = side_of(axis)
        self.sent = lax.dynamic_index_in_dim(pairs, 1 - side, 1, keepdims=False)
        self.keep = lax.dynamic_index_in_dim(pairs, side, 1, keepdims=False)
        return self.sent

    def go(self):
        self.come = trade(self.sent, self.left[0], self.dp)

    def add(self, earlier=None):
        come = self.come if earlier is None else after(self.come, earlier)
        total = (self.keep.astype(F32) + come.astype(F32)).astype(BF)
        self.part = total.reshape(-1, total.shape[-1])
        self.axes.remove(self.left.pop(0))
        if self.left:
            self.send()


def finish(many):
    while any(one.left for one in many):
        active = [one for one in many if one.left]
        for one in active:
            one.go()
        for one, come in zip(active, lax.optimization_barrier([one.come for one in active])):
            one.come = come
            one.add()
    return [one.part for one in many]


def split_core(total, dp):
    groups = total.reshape(dp, 2, total.shape[0] // (2 * dp), total.shape[1])
    side = side_of(0)
    keep = lax.dynamic_index_in_dim(groups, side, 1, keepdims=False)
    send = lax.dynamic_index_in_dim(groups, 1 - side, 1, keepdims=False)
    return [one.reshape(total.shape[0] // 2, total.shape[1]) for one in (keep, send)]


def gather_steps(local, dp, turn, earlier):
    axes = axes_of(dp)
    done = []
    part = local
    for axis in reversed(order_of(dp, turn)):
        if axis == "tensor":
            part = after(part, earlier)
        come = trade(part, axis, dp)
        low = side_of(axis) == 0
        done = [one for one in axes if one == axis or one in done]
        lead = 1 << done.index(axis)
        pair = [jnp.where(low, part, come), jnp.where(low, come, part)]
        pair = [one.reshape(lead, part.shape[0] // lead, part.shape[1]) for one in pair]
        part = jnp.stack(pair, axis=1).reshape(2 * part.shape[0], part.shape[1])
    return part


def after(values, earlier):
    return lax.optimization_barrier((values, earlier))[0]


def whole_sequence_body(
    tokens_in,
    piece_starts,
    cotangent,
    gain_tokens,
    gain_mlp,
    gain_state,
    gate_bias,
    w_query,
    w_key,
    w_value,
    w_out,
    w_state_query,
    w_state_key,
    w_state_value,
    w_state_out,
    w_gate,
    w_up,
    w_down,
    state_init,
):
    mine = lax.axis_index("tensor")
    first = mine == 0
    local_rows = w_query.shape[0]
    dp = D // local_rows
    width = w_query.shape[1]
    units = 512
    across = w_up.shape[1] // units
    swap = [(0, 1), (1, 0)]

    def other_half(pair):
        return lax.ppermute(jnp.where(first, pair[1, 0], pair[0, 0]), "tensor", swap)

    def bring(pair, come):
        keep = jnp.where(first, pair[0, 0], pair[1, 0])
        top = jnp.where(first, keep, come)
        low = jnp.where(first, come, keep)
        return jnp.concatenate([top, low], axis=1).reshape(NB * W, D)

    def give(rows, later=None):
        halves = rows.reshape(NB, 2, HALF, D)
        keep = jnp.where(first, halves[:, 0], halves[:, 1])
        send = jnp.where(first, halves[:, 1], halves[:, 0])
        come = lax.ppermute(send, "tensor", swap)
        if later is not None:
            come = after(come, later)
        return jnp.stack([jnp.where(first, keep, come), jnp.where(first, come, keep)])[:, None]

    def split_init(values):
        side = values.shape[1] // 2
        return jnp.concatenate([values[:, :side], values[:, side:]], axis=0)

    gains = jnp.stack([gain_tokens, gain_mlp, gain_state, gate_bias])
    small = jnp.concatenate(
        [split_init(state_init), jnp.pad(gains, ((0, local_rows - 4), (0, 128 - local_rows)))],
        axis=1,
    )
    full_qkv = gather(
        jnp.concatenate([w_query, w_key, w_value, w_state_query, w_state_key, small], axis=1)
    )
    full_small = full_qkv[:, 5 * width :]
    turned_down = w_down.T
    late = []
    for unit in range(0, across * units, units):
        late += [w_up[:, unit : unit + units], turned_down[:, unit : unit + units]]
    late = jnp.concatenate(late + [w_out.T], axis=1)
    rows = bring(tokens_in, other_half(tokens_in))
    full_state1 = gather_steps(
        jnp.concatenate([w_state_value, w_gate, w_state_out.T], axis=1), dp, False, (rows, late)
    )
    full_late = gather(after(late, (full_qkv, full_state1)))
    side = width // 2
    init = full_small[:, :side].reshape(2, dp, 2, local_rows // 2, side)
    init = jnp.transpose(init, (1, 3, 0, 2, 4)).reshape(S, D)
    gains = full_small[:D, side:].reshape(dp, local_rows, 128)[:, :4, :local_rows]
    gains = jnp.transpose(gains, (1, 0, 2)).reshape(4, 1, D).astype(F32)

    cot_half = other_half(after(cotangent, rows))
    starts = jnp.where(first, piece_starts[0, 0], piece_starts[1, 0])
    flags = jnp.any(
        starts[:, None] == PIECE * jnp.arange(NB * W // PIECE, dtype=jnp.int32)[None], axis=0
    ).astype(jnp.int32)

    turned, query, key, value = project(rows, gains[0], full_qkv)
    (
        token_mixed,
        state_mixed,
        state_turned,
        state_query,
        state_key,
        state_value,
        state_in,
        forget,
        apart,
        totals,
    ) = forward(flags, query, key, value, init, gains[2], gains[3], full_qkv, full_state1)
    cot = bring(cotangent, after(cot_half, token_mixed))
    middle, mlp_in, mlp_turned, cot_turned = middle_rows(
        rows, token_mixed, full_late, gains[1], cot
    )
    mlp_out, grad_mlp_in, grad_mlp_w = mlp(mlp_in, mlp_turned, cot, cot_turned, full_late)
    output, grad_middle, middle_turned, grad_mixed, grad_gain_mlp = after_mlp(
        middle, mlp_out, grad_mlp_in, cot, gains[1], full_late
    )
    grads_late = whole_weight_grad(middle_turned, token_mixed, grad_mlp_w)
    part_late = scatter(grads_late)
    core = (side_of(0) & 1).astype(jnp.int32).reshape(1)
    grad_tok, grad_sta, branch, grad_init, grad_gain_state, grad_bias = backward(
        flags,
        query,
        key,
        value,
        state_query,
        state_key,
        state_value,
        token_mixed,
        state_mixed,
        after(grad_mixed, grads_late),
        totals,
        forget,
        state_in,
        apart,
        gains[2],
        full_qkv,
        full_state1,
    )
    given_output = give(output, grad_tok)

    a = Halving(*weight_grads(dp, core, state_turned, after(grad_sta, given_output), 0, 2), dp, False)
    a.go()
    b = Halving(*weight_grads(dp, core, state_turned, after(grad_sta, a.sent), 2, 2), dp, True)
    a.add(b.keep)
    a.go()
    b.go()
    c = Halving(*weight_grads(dp, core, turned, after(grad_tok, (a.sent, b.sent)), 1, 2), dp, False)
    b.add(c.keep)
    b.go()
    c.go()
    grads_q = weight_grads(dp, core, turned, after(grad_tok, (b.sent, c.sent)), 0, 1, 2, 0)
    c.add(grads_q)
    c.go()
    d = Halving(
        *weight_grads(dp, core, after(branch, c.sent), state_mixed[None], 0, 1, 2, 1, grads_q),
        dp,
        True,
    )
    d.go()
    grad_in, grad_gain_tokens = token_grad(
        after(grad_tok, (d.sent, part_late)), full_qkv, rows, grad_middle, gains[0]
    )
    a.add(grad_in)
    d.add(grad_in)
    b.add(grad_in)
    init_parts = jnp.transpose(
        grad_init.reshape(dp, local_rows // 2, 2, 2, side), (2, 0, 3, 1, 4)
    ).reshape(2 * D, side)
    gain_parts = jnp.stack(
        [grad_gain_tokens[0], grad_gain_mlp[0], grad_gain_state[0], grad_bias[0]]
    ).reshape(4, dp, local_rows)
    gain_parts = jnp.pad(
        jnp.transpose(gain_parts, (1, 0, 2)),
        ((0, 0), (0, local_rows - 4), (0, 128 - local_rows)),
    ).reshape(D, 128)
    gain_parts = jnp.concatenate([gain_parts, gain_parts], axis=0).astype(BF)
    e = Halving(*split_core(jnp.concatenate([init_parts, gain_parts], axis=1), dp), dp, True)
    given_grad = give(grad_in)
    part_rest, part_kv, part_sqk, part_svg, part_small = [
        one.astype(F32) for one in finish([d, c, a, b, e])
    ]
    part_so = part_rest[:, width:]
    part_init = part_small[:, :side]
    part_init = jnp.concatenate(
        [part_init[: local_rows // 2], part_init[local_rows // 2 :]], axis=1
    )
    part_gains = part_small[:4, side : side + local_rows]
    part_late = part_late.astype(F32)
    part_up = [part_late[:, 2 * i * units : (2 * i + 1) * units] for i in range(across)]
    part_down = [part_late[:, (2 * i + 1) * units : (2 * i + 2) * units] for i in range(across)]
    part_sqk = part_sqk.astype(F32)
    part_svg = part_svg.astype(F32)
    return (
        given_output,
        given_grad,
        part_gains[0],
        part_gains[1],
        part_gains[2],
        part_gains[3],
        part_rest[:, :width],
        part_kv[:, :width],
        part_kv[:, width:],
        part_late[:, 2 * across * units :].T,
        part_sqk[:, :width],
        part_sqk[:, width:],
        part_svg[:, :width],
        part_so.T,
        part_svg[:, width:],
        jnp.concatenate(part_up, axis=1),
        jnp.concatenate([one.T for one in part_down], axis=0),
        part_init,
    )


def solution(mesh):
    dp = mesh.shape["dp"]
    one_each = mesh.shape["tensor"] == MICRO and dp > 1 and dp & (dp - 1) == 0
    return jax.shard_map(
        whole_sequence_body if one_each else generic_body,
        mesh=mesh,
        in_specs=(
            P(None, "dp", None, "tensor", None),
            P(None, "dp", None),
            P(None, "dp", None, "tensor", None),
            P("dp"),
            P("dp"),
            P("dp"),
            P("dp"),
            P("dp", "tensor"),
            P("dp", "tensor"),
            P("dp", "tensor"),
            P("tensor", "dp"),
            P("dp", "tensor"),
            P("dp", "tensor"),
            P("dp", "tensor"),
            P("tensor", "dp"),
            P("dp", "tensor"),
            P("dp", "tensor"),
            P("tensor", "dp"),
            P("dp", "tensor"),
        ),
        out_specs=(
            P(None, "dp", None, "tensor", None),
            P(None, "dp", None, "tensor", None),
            P("dp"),
            P("dp"),
            P("dp"),
            P("dp"),
            P("dp", "tensor"),
            P("dp", "tensor"),
            P("dp", "tensor"),
            P("tensor", "dp"),
            P("dp", "tensor"),
            P("dp", "tensor"),
            P("dp", "tensor"),
            P("tensor", "dp"),
            P("dp", "tensor"),
            P("dp", "tensor"),
            P("tensor", "dp"),
            P("dp", "tensor"),
        ),
        check_vma=False,
    )
```

```python
import functools
import math

import jax
import jax.numpy as jnp
from jax import lax
from jax.experimental import pallas as pl
from jax.experimental.pallas import tpu as pltpu
from jax.sharding import PartitionSpec as P

D = 1024
HEAD = 128
W = 512
S = 512
PIECE = 256
MICRO = 2
NB = 4


epsilon = 1e-06
masked_score = -1e30


def rms_scale(values):
    return values * lax.rsqrt(jnp.mean(values * values, axis=-1, keepdims=True) + epsilon)


def normed_rows(values, gain):
    return rms_scale(values) * gain


def matmul(left, right):
    return jnp.dot(left, right, preferred_element_type=jnp.float32)


def mlp_local(full_in, full_up, full_down):
    hidden = matmul(full_in, full_up)
    active = jax.nn.gelu(hidden).astype(jnp.bfloat16)
    return (hidden, active, matmul(active, full_down))


def mlp_back_local(full_grad, active, hidden, full_in, full_down, full_up):
    grad_down_w = jnp.einsum("...f,...d->fd", active, full_grad, preferred_element_type=jnp.float32)
    grad_active = jnp.einsum(
        "...d,fd->...f", full_grad, full_down, preferred_element_type=jnp.float32
    )
    unused_value, gelu_back = jax.vjp(jax.nn.gelu, hidden)
    grad_hidden = gelu_back(grad_active)[0].astype(jnp.bfloat16)
    grad_up_w = jnp.einsum(
        "...d,...f->df", full_in, grad_hidden, preferred_element_type=jnp.float32
    )
    mlp_part = jnp.einsum("...f,df->...d", grad_hidden, full_up, preferred_element_type=jnp.float32)
    return (grad_down_w, grad_up_w, mlp_part)


def piece_labels(starts):
    positions = jnp.arange(NB * W, dtype=jnp.int32)
    inside = (positions[None, None, :] >= starts[:, :, None]) & (
        positions[None, None, :] < starts[:, :, None] + PIECE
    )
    numbers = jnp.arange(1, starts.shape[1] + 1, dtype=jnp.int32)
    return jnp.sum(jnp.where(inside, numbers[None, :, None], 0), axis=1)


def token_mask(labels, block):
    batch = labels.shape[0]
    own = labels[:, block * W : (block + 1) * W]
    local = jnp.arange(W, dtype=jnp.int32)
    causal = (local[None, :] <= local[:, None])[None]
    together = (own[:, :, None] == own[:, None, :]) & (own[:, :, None] > 0)
    current = causal | together
    earlier = jnp.full((batch, W, W), block > 0)
    state_part = jnp.ones((batch, W, S), dtype=bool)
    return jnp.concatenate([earlier, current, state_part], axis=2)[:, None]


def split_heads(values):
    return values.reshape(values.shape[0], values.shape[1], values.shape[2] // HEAD, HEAD)


def scores_of(query, keys, allowed):
    scores = jnp.einsum(
        "brhe,bkhe->bhrk", split_heads(query), split_heads(keys), preferred_element_type=jnp.float32
    ) * (1.0 / math.sqrt(HEAD))
    return jnp.where(allowed, scores, masked_score)


def attend(query, keys, values, allowed):
    scores = scores_of(query, keys, allowed)
    top = jnp.max(scores, axis=-1, keepdims=True)
    total = top + jnp.log(jnp.sum(jnp.exp(scores - top), axis=-1, keepdims=True))
    weights = jnp.exp(scores - total).astype(jnp.bfloat16)
    mixed = jnp.einsum(
        "bhrk,bkhe->brhe", weights, split_heads(values), preferred_element_type=jnp.float32
    )
    return (mixed.reshape(query.shape).astype(jnp.bfloat16), total)


def attend_back(query, keys, values, allowed, total, grad_mixed):
    scale = 1.0 / math.sqrt(HEAD)
    weights = jnp.exp(scores_of(query, keys, allowed) - total)
    grad_heads = split_heads(grad_mixed)
    grad_weights = jnp.einsum(
        "brhe,bkhe->bhrk", grad_heads, split_heads(values), preferred_element_type=jnp.float32
    )
    grad_scores = (
        weights * (grad_weights - jnp.sum(weights * grad_weights, axis=-1, keepdims=True))
    ).astype(jnp.bfloat16)
    grad_query = (
        jnp.einsum(
            "bhrk,bkhe->brhe", grad_scores, split_heads(keys), preferred_element_type=jnp.float32
        )
        * scale
    )
    grad_keys = (
        jnp.einsum(
            "bhrk,brhe->bkhe", grad_scores, split_heads(query), preferred_element_type=jnp.float32
        )
        * scale
    )
    grad_values = jnp.einsum(
        "bhrk,brhe->bkhe",
        weights.astype(jnp.bfloat16),
        grad_heads,
        preferred_element_type=jnp.float32,
    )
    return (
        grad_query.reshape(query.shape),
        grad_keys.reshape(keys.shape),
        grad_values.reshape(values.shape),
    )


def generic_body(
    tokens_in,
    piece_starts,
    cotangent,
    gain_tokens,
    gain_mlp,
    gain_state,
    gate_bias,
    w_query,
    w_key,
    w_value,
    w_out,
    w_state_query,
    w_state_key,
    w_state_value,
    w_state_out,
    w_gate,
    w_up,
    w_down,
    state_init,
):
    width_local = w_query.shape[1]
    column_start = lax.axis_index("tensor") * width_local

    def collect():
        return (
            lax.all_gather(w_query, "dp", axis=0, tiled=True),
            lax.all_gather(w_key, "dp", axis=0, tiled=True),
            lax.all_gather(w_value, "dp", axis=0, tiled=True),
            lax.all_gather(w_state_query, "dp", axis=0, tiled=True),
            lax.all_gather(w_state_key, "dp", axis=0, tiled=True),
            lax.all_gather(w_state_value, "dp", axis=0, tiled=True),
            lax.all_gather(w_gate, "dp", axis=0, tiled=True),
            lax.all_gather(w_up, "dp", axis=0, tiled=True),
            lax.all_gather(state_init, "dp", axis=0, tiled=True),
            lax.all_gather(w_out, "dp", axis=1, tiled=True),
            lax.all_gather(w_state_out, "dp", axis=1, tiled=True),
            lax.all_gather(w_down, "dp", axis=1, tiled=True),
            lax.all_gather(gain_tokens, "dp", axis=0, tiled=True),
            lax.all_gather(gain_mlp, "dp", axis=0, tiled=True),
            lax.all_gather(gain_state, "dp", axis=0, tiled=True),
            lax.all_gather(gate_bias, "dp", axis=0, tiled=True),
        )

    def unpack_gains(weights):
        token_gain = weights[12].astype(jnp.float32)
        mlp_gain = weights[13].astype(jnp.float32)
        state_gain = lax.dynamic_slice_in_dim(
            weights[14].astype(jnp.float32), column_start, width_local
        )
        bias_columns = lax.dynamic_slice_in_dim(
            weights[15].astype(jnp.float32), column_start, width_local
        )
        return (token_gain, mlp_gain, state_gain, bias_columns)

    outputs = []
    input_grads = []
    totals = None
    for micro in range(MICRO):
        forward_weights = collect()
        forward_rows_in = tokens_in[micro]
        (
            forward_full_query,
            forward_full_key,
            forward_full_value,
            forward_full_state_query,
            forward_full_state_key,
            forward_full_state_value,
            forward_full_gate,
            forward_full_up,
            forward_full_init,
            forward_full_out,
            forward_full_state_out,
            forward_full_down,
        ) = forward_weights[:12]
        forward_token_gain, forward_mlp_gain, forward_state_gain, forward_bias_columns = (
            unpack_gains(forward_weights)
        )
        forward_batch = forward_rows_in.shape[0]
        forward_labels = piece_labels(piece_starts[micro])
        forward_state = jnp.broadcast_to(
            forward_full_init.astype(jnp.float32), (forward_batch, S, width_local)
        )
        zero_keys = jnp.zeros((forward_batch, W, width_local), jnp.bfloat16)
        forward_earlier_key = zero_keys
        forward_earlier_value = zero_keys
        forward_kept = []
        middles = []
        for forward_block in range(NB):
            forward_rows = forward_rows_in[:, forward_block].astype(jnp.float32)
            normed = normed_rows(forward_rows, forward_token_gain).astype(jnp.bfloat16)
            square_sum = lax.psum(jnp.sum(forward_state * forward_state, axis=-1), "tensor")
            forward_inverse = lax.rsqrt(square_sum / D + epsilon)[..., None]
            forward_scaled = forward_state * forward_inverse
            state_normed = (forward_scaled * forward_state_gain).astype(jnp.bfloat16)
            forward_full_normed, forward_full_state = (
                lax.all_gather(normed, "tensor", axis=1, tiled=True),
                lax.all_gather(state_normed, "tensor", axis=2, tiled=True),
            )
            forward_query = matmul(forward_full_normed, forward_full_query).astype(jnp.bfloat16)
            forward_key = matmul(forward_full_normed, forward_full_key).astype(jnp.bfloat16)
            forward_value = matmul(forward_full_normed, forward_full_value).astype(jnp.bfloat16)
            forward_state_query = matmul(forward_full_state, forward_full_state_query).astype(
                jnp.bfloat16
            )
            forward_state_key = matmul(forward_full_state, forward_full_state_key).astype(
                jnp.bfloat16
            )
            forward_state_value = matmul(forward_full_state, forward_full_state_value).astype(
                jnp.bfloat16
            )
            gate_pre = matmul(forward_full_state, forward_full_gate) + forward_bias_columns
            forward_allowed = token_mask(forward_labels, forward_block)
            forward_token_keys = jnp.concatenate(
                [forward_earlier_key, forward_key, forward_state_key], axis=1
            )
            forward_token_values = jnp.concatenate(
                [forward_earlier_value, forward_value, forward_state_value], axis=1
            )
            forward_token_mixed, forward_token_total = attend(
                forward_query, forward_token_keys, forward_token_values, forward_allowed
            )
            forward_cross_keys = jnp.concatenate([forward_key, forward_state_key], axis=1)
            forward_cross_values = jnp.concatenate([forward_value, forward_state_value], axis=1)
            forward_state_mixed, forward_state_total = attend(
                forward_state_query, forward_cross_keys, forward_cross_values, True
            )
            forward_row_part = matmul(forward_token_mixed, forward_full_out)
            forward_state_part = matmul(forward_state_mixed, forward_full_state_out)
            row_sum, forward_state_sum = (
                lax.psum_scatter(
                    forward_row_part.astype(jnp.bfloat16), "tensor", scatter_dimension=1, tiled=True
                ).astype(jnp.float32),
                lax.psum_scatter(
                    forward_state_part.astype(jnp.bfloat16),
                    "tensor",
                    scatter_dimension=2,
                    tiled=True,
                ).astype(jnp.float32),
            )
            forward_forget = jax.nn.sigmoid(gate_pre)
            forward_kept.append(
                (
                    forward_full_normed,
                    forward_full_state,
                    forward_query,
                    forward_key,
                    forward_value,
                    forward_state_query,
                    forward_state_key,
                    forward_state_value,
                    forward_token_mixed,
                    forward_state_mixed,
                    forward_token_total,
                    forward_state_total,
                    forward_state,
                    forward_scaled,
                    forward_inverse,
                    forward_forget,
                    forward_state_sum,
                    forward_earlier_key,
                    forward_earlier_value,
                )
            )
            middle_block = forward_rows + row_sum
            middles.append(middle_block)
            forward_state = (
                forward_forget * forward_state + (1.0 - forward_forget) * forward_state_sum
            )
            forward_earlier_key, forward_earlier_value = (forward_key, forward_value)
        forward_middle = jnp.stack(middles, axis=1)
        mlp_in = normed_rows(forward_middle, forward_mlp_gain).astype(jnp.bfloat16)
        forward_full_mlp_in = lax.all_gather(mlp_in, "tensor", axis=2, tiled=True)
        forward_hidden, forward_active, mlp_partial = mlp_local(
            forward_full_mlp_in, forward_full_up, forward_full_down
        )
        mlp_sum = lax.psum_scatter(
            mlp_partial.astype(jnp.bfloat16), "tensor", scatter_dimension=2, tiled=True
        ).astype(jnp.float32)
        output = (forward_middle + mlp_sum).astype(jnp.bfloat16)
        output, saved = (
            output,
            (
                forward_kept,
                forward_middle,
                forward_full_mlp_in,
                forward_hidden,
                forward_active,
                forward_labels,
            ),
        )
        outputs.append(output)
        backward_weights = collect()
        rows_in = tokens_in[micro]
        grad_rows_out = cotangent[micro]
        (
            full_query,
            full_key,
            full_value,
            full_state_query,
            full_state_key,
            full_state_value,
            full_gate,
            full_up,
            full_init,
            full_out,
            full_state_out,
            full_down,
        ) = backward_weights[:12]
        backward_token_gain, backward_mlp_gain, backward_state_gain, backward_bias_columns = (
            unpack_gains(backward_weights)
        )
        kept, middle, full_mlp_in, hidden, active, labels = saved
        batch = rows_in.shape[0]
        full_grad = lax.all_gather(grad_rows_out, "tensor", axis=2, tiled=True)
        grad_down_w, grad_up_w, mlp_part = mlp_back_local(
            full_grad, active, hidden, full_mlp_in, full_down, full_up
        )
        grad_mlp_in = lax.psum_scatter(
            mlp_part.astype(jnp.bfloat16), "tensor", scatter_dimension=2, tiled=True
        ).astype(jnp.float32)
        unused_norm, mlp_norm_back = jax.vjp(normed_rows, middle, backward_mlp_gain)
        grad_middle_norm, grad_mlp_gain = mlp_norm_back(grad_mlp_in)
        grad_middle = grad_rows_out.astype(jnp.float32) + grad_middle_norm
        grad_state = jnp.zeros((batch, S, width_local), jnp.float32)
        carry_key = jnp.zeros((batch, W, width_local), jnp.float32)
        carry_value = jnp.zeros((batch, W, width_local), jnp.float32)
        square_zero = jnp.zeros((D, width_local), jnp.float32)
        grad_query_w = square_zero
        grad_key_w = square_zero
        grad_value_w = square_zero
        grad_state_query_w = square_zero
        grad_state_key_w = square_zero
        grad_state_value_w = square_zero
        grad_gate_w = square_zero
        grad_out_w = jnp.zeros((width_local, D), jnp.float32)
        grad_state_out_w = jnp.zeros((width_local, D), jnp.float32)
        grad_token_gain = jnp.zeros((D,), jnp.float32)
        grad_state_gain = jnp.zeros((width_local,), jnp.float32)
        grad_bias = jnp.zeros((width_local,), jnp.float32)
        grad_rows = [None] * NB
        for block in reversed(range(NB)):
            (
                full_normed,
                full_state,
                query,
                key,
                value,
                state_query,
                state_key,
                state_value,
                token_mixed,
                state_mixed,
                token_total,
                state_total,
                state,
                scaled,
                inverse,
                forget,
                state_sum,
                earlier_key,
                earlier_value,
            ) = kept[block]
            grad_row_block = grad_middle[:, block]
            grad_branch_state = ((1.0 - forget) * grad_state).astype(jnp.bfloat16)
            grad_gate = (grad_state * (state - state_sum) * forget * (1.0 - forget)).astype(
                jnp.bfloat16
            )
            carried_state = grad_state * forget
            full_grad_rows, full_grad_state = (
                lax.all_gather(grad_row_block.astype(jnp.bfloat16), "tensor", axis=1, tiled=True),
                lax.all_gather(grad_branch_state, "tensor", axis=2, tiled=True),
            )
            grad_out_w = grad_out_w + jnp.einsum(
                "bwc,bwd->cd", token_mixed, full_grad_rows, preferred_element_type=jnp.float32
            )
            grad_state_out_w = grad_state_out_w + jnp.einsum(
                "bsc,bsd->cd", state_mixed, full_grad_state, preferred_element_type=jnp.float32
            )
            grad_token_mixed = jnp.einsum(
                "bwd,cd->bwc", full_grad_rows, full_out, preferred_element_type=jnp.float32
            ).astype(jnp.bfloat16)
            grad_state_mixed = jnp.einsum(
                "bsd,cd->bsc", full_grad_state, full_state_out, preferred_element_type=jnp.float32
            ).astype(jnp.bfloat16)
            allowed = token_mask(labels, block)
            token_keys = jnp.concatenate([earlier_key, key, state_key], axis=1)
            token_values = jnp.concatenate([earlier_value, value, state_value], axis=1)
            cross_keys = jnp.concatenate([key, state_key], axis=1)
            cross_values = jnp.concatenate([value, state_value], axis=1)
            token_grad_query, token_grad_keys, token_grad_values = attend_back(
                query, token_keys, token_values, allowed, token_total, grad_token_mixed
            )
            state_grad_query, cross_grad_keys, cross_grad_values = attend_back(
                state_query, cross_keys, cross_values, True, state_total, grad_state_mixed
            )
            grad_key = (token_grad_keys[:, W : 2 * W] + cross_grad_keys[:, :W] + carry_key).astype(
                jnp.bfloat16
            )
            grad_value = (
                token_grad_values[:, W : 2 * W] + cross_grad_values[:, :W] + carry_value
            ).astype(jnp.bfloat16)
            carry_key = token_grad_keys[:, :W]
            carry_value = token_grad_values[:, :W]
            grad_state_key = (token_grad_keys[:, 2 * W :] + cross_grad_keys[:, W:]).astype(
                jnp.bfloat16
            )
            grad_state_value = (token_grad_values[:, 2 * W :] + cross_grad_values[:, W:]).astype(
                jnp.bfloat16
            )
            grad_query = token_grad_query.astype(jnp.bfloat16)
            grad_state_query = state_grad_query.astype(jnp.bfloat16)
            grad_query_w = grad_query_w + jnp.einsum(
                "bwd,bwc->dc", full_normed, grad_query, preferred_element_type=jnp.float32
            )
            grad_key_w = grad_key_w + jnp.einsum(
                "bwd,bwc->dc", full_normed, grad_key, preferred_element_type=jnp.float32
            )
            grad_value_w = grad_value_w + jnp.einsum(
                "bwd,bwc->dc", full_normed, grad_value, preferred_element_type=jnp.float32
            )
            grad_state_query_w = grad_state_query_w + jnp.einsum(
                "bsd,bsc->dc", full_state, grad_state_query, preferred_element_type=jnp.float32
            )
            grad_state_key_w = grad_state_key_w + jnp.einsum(
                "bsd,bsc->dc", full_state, grad_state_key, preferred_element_type=jnp.float32
            )
            grad_state_value_w = grad_state_value_w + jnp.einsum(
                "bsd,bsc->dc", full_state, grad_state_value, preferred_element_type=jnp.float32
            )
            grad_gate_w = grad_gate_w + jnp.einsum(
                "bsd,bsc->dc", full_state, grad_gate, preferred_element_type=jnp.float32
            )
            grad_bias = grad_bias + jnp.sum(grad_gate.astype(jnp.float32), axis=(0, 1))
            row_part = jnp.einsum(
                "bwc,dc->bwd", grad_query, full_query, preferred_element_type=jnp.float32
            )
            row_part = row_part + jnp.einsum(
                "bwc,dc->bwd", grad_key, full_key, preferred_element_type=jnp.float32
            )
            row_part = row_part + jnp.einsum(
                "bwc,dc->bwd", grad_value, full_value, preferred_element_type=jnp.float32
            )
            state_part = jnp.einsum(
                "bsc,dc->bsd",
                grad_state_query,
                full_state_query,
                preferred_element_type=jnp.float32,
            )
            state_part = state_part + jnp.einsum(
                "bsc,dc->bsd", grad_state_key, full_state_key, preferred_element_type=jnp.float32
            )
            state_part = state_part + jnp.einsum(
                "bsc,dc->bsd",
                grad_state_value,
                full_state_value,
                preferred_element_type=jnp.float32,
            )
            state_part = state_part + jnp.einsum(
                "bsc,dc->bsd", grad_gate, full_gate, preferred_element_type=jnp.float32
            )
            grad_normed, grad_state_normed = (
                lax.psum_scatter(
                    row_part.astype(jnp.bfloat16), "tensor", scatter_dimension=1, tiled=True
                ).astype(jnp.float32),
                lax.psum_scatter(
                    state_part.astype(jnp.bfloat16), "tensor", scatter_dimension=2, tiled=True
                ).astype(jnp.float32),
            )
            rows = rows_in[:, block].astype(jnp.float32)
            unused_rows, token_norm_back = jax.vjp(normed_rows, rows, backward_token_gain)
            grad_rows_norm, grad_gain_part = token_norm_back(grad_normed)
            grad_token_gain = grad_token_gain + grad_gain_part
            grad_rows[block] = (grad_row_block + grad_rows_norm).astype(jnp.bfloat16)
            grad_scaled = grad_state_normed * backward_state_gain
            grad_state_gain = grad_state_gain + jnp.sum(grad_state_normed * scaled, axis=(0, 1))
            dot_sum = lax.psum(jnp.sum(grad_scaled * scaled, axis=-1), "tensor")
            grad_state = carried_state + inverse * (grad_scaled - scaled * (dot_sum / D)[..., None])
        grad_init = jnp.sum(grad_state, axis=0)
        state_gain_full = lax.dynamic_update_slice_in_dim(
            jnp.zeros((D,), jnp.float32), grad_state_gain, column_start, 0
        )
        bias_full = lax.dynamic_update_slice_in_dim(
            jnp.zeros((D,), jnp.float32), grad_bias, column_start, 0
        )
        grads = (
            grad_query_w,
            grad_key_w,
            grad_value_w,
            grad_state_query_w,
            grad_state_key_w,
            grad_state_value_w,
            grad_gate_w,
            grad_up_w,
            grad_init,
            grad_out_w,
            grad_state_out_w,
            grad_down_w,
            grad_token_gain,
            grad_mlp_gain,
            state_gain_full,
            bias_full,
        )
        grads, grad_in = (grads, jnp.stack(grad_rows, axis=1))
        input_grads.append(grad_in)
        if totals is None:
            totals = grads
        else:
            totals = tuple((first + second for first, second in zip(totals, grads)))
    reduced = (
        lax.psum_scatter(
            totals[0].astype(jnp.bfloat16), "dp", scatter_dimension=0, tiled=True
        ).astype(jnp.float32),
        lax.psum_scatter(
            totals[1].astype(jnp.bfloat16), "dp", scatter_dimension=0, tiled=True
        ).astype(jnp.float32),
        lax.psum_scatter(
            totals[2].astype(jnp.bfloat16), "dp", scatter_dimension=0, tiled=True
        ).astype(jnp.float32),
        lax.psum_scatter(
            totals[3].astype(jnp.bfloat16), "dp", scatter_dimension=0, tiled=True
        ).astype(jnp.float32),
        lax.psum_scatter(
            totals[4].astype(jnp.bfloat16), "dp", scatter_dimension=0, tiled=True
        ).astype(jnp.float32),
        lax.psum_scatter(
            totals[5].astype(jnp.bfloat16), "dp", scatter_dimension=0, tiled=True
        ).astype(jnp.float32),
        lax.psum_scatter(
            totals[6].astype(jnp.bfloat16), "dp", scatter_dimension=0, tiled=True
        ).astype(jnp.float32),
        lax.psum_scatter(
            totals[7].astype(jnp.bfloat16), "dp", scatter_dimension=0, tiled=True
        ).astype(jnp.float32),
        lax.psum_scatter(
            totals[8].astype(jnp.bfloat16), "dp", scatter_dimension=0, tiled=True
        ).astype(jnp.float32),
        lax.psum_scatter(
            totals[9].astype(jnp.bfloat16), "dp", scatter_dimension=1, tiled=True
        ).astype(jnp.float32),
        lax.psum_scatter(
            totals[10].astype(jnp.bfloat16), "dp", scatter_dimension=1, tiled=True
        ).astype(jnp.float32),
        lax.psum_scatter(
            totals[11].astype(jnp.bfloat16), "dp", scatter_dimension=1, tiled=True
        ).astype(jnp.float32),
        lax.psum_scatter(
            totals[12].astype(jnp.bfloat16), "dp", scatter_dimension=0, tiled=True
        ).astype(jnp.float32),
        lax.psum_scatter(
            totals[13].astype(jnp.bfloat16), "dp", scatter_dimension=0, tiled=True
        ).astype(jnp.float32),
        lax.psum_scatter(
            totals[14].astype(jnp.bfloat16), "dp", scatter_dimension=0, tiled=True
        ).astype(jnp.float32),
        lax.psum_scatter(
            totals[15].astype(jnp.bfloat16), "dp", scatter_dimension=0, tiled=True
        ).astype(jnp.float32),
    )
    gain_totals = lax.psum((reduced[12], reduced[13], reduced[14], reduced[15]), "tensor")
    return (
        jnp.stack(outputs, axis=0),
        jnp.stack(input_grads, axis=0),
        gain_totals[0],
        gain_totals[1],
        gain_totals[2],
        gain_totals[3],
        reduced[0],
        reduced[1],
        reduced[2],
        reduced[9],
        reduced[3],
        reduced[4],
        reduced[5],
        reduced[10],
        reduced[6],
        reduced[7],
        reduced[11],
        reduced[8],
    )


BF = jnp.bfloat16
F32 = jnp.float32
HALF = 256
VMEM_BYTES = 60 * 1024 * 1024
EXP2_SCALE = math.log2(math.e) / math.sqrt(HEAD)
SCORE_SCALE = 1.0 / math.sqrt(HEAD)


def nn(left, right):
    return lax.dot_general(left, right, (((1,), (0,)), ((), ())), preferred_element_type=F32)


def nt(left, right):
    return lax.dot_general(left, right, (((1,), (1,)), ((), ())), preferred_element_type=F32)


def tn(left, right):
    return lax.dot_general(left, right, (((0,), (0,)), ((), ())), preferred_element_type=F32)


def inverse_rms(values):
    return lax.rsqrt(jnp.mean(values * values, axis=-1, keepdims=True) + epsilon)


def rms_back(scaled, inverse, grad):
    return (grad - scaled * jnp.mean(grad * scaled, axis=-1, keepdims=True)) * inverse


def params(semantics=("arbitrary",)):
    return pltpu.CompilerParams(dimension_semantics=semantics, vmem_limit_bytes=VMEM_BYTES)


def cost(flops, moved, transcendentals=0):
    return pl.CostEstimate(
        flops=int(flops), bytes_accessed=int(moved), transcendentals=int(transcendentals)
    )


def once(shape, index):
    return pl.BlockSpec(shape, index, pipeline_mode=pl.Buffered(1))


def project_kernel(rows, gain, w0, w1, turned, query, key, value):
    width = w0.shape[1] // 3
    wide = rows[...].astype(F32)
    normed = (wide * inverse_rms(wide) * gain[...]).astype(BF)
    turned[...] = normed.T
    for half, weight in enumerate((w0, w1)):
        for which, out in enumerate((query, key, value)):
            out[:, half * width : (half + 1) * width] = nn(
                normed, weight[:, which * width : (which + 1) * width]
            ).astype(BF)


def project(rows, gain, weights):
    tokens = rows.shape[0]
    width = 3 * D // 2
    out = jax.ShapeDtypeStruct((tokens, D), BF)
    block = pl.BlockSpec((W, D), lambda b: (b, 0))
    return pl.pallas_call(
        project_kernel,
        grid=(tokens // W,),
        in_specs=[
            block,
            once((1, D), lambda b: (0, 0)),
            once((D, width), lambda b: (0, 0)),
            once((D, width), lambda b: (1, 0)),
        ],
        out_specs=[pl.BlockSpec((D, W), lambda b: (0, b))] + [block] * 3,
        out_shape=[jax.ShapeDtypeStruct((D, tokens), BF)] + [out] * 3,
        compiler_params=params(),
        cost_estimate=cost(2 * tokens * D * 3 * D, 2 * (5 * tokens * D + 3 * D * D)),
        name="project",
    )(rows, gain, weights, weights)


def softmax_parts(parts):
    top = parts[0][0].max(axis=1, keepdims=True)
    for scores, unused in parts[1:]:
        top = jnp.maximum(top, scores.max(axis=1, keepdims=True))
    mixed = None
    for scores, values in parts:
        weights = jnp.exp2((scores - top) * EXP2_SCALE)
        wide_values = jnp.concatenate([values, jnp.ones_like(values)], axis=1)
        part_mixed = nn(weights.astype(BF), wide_values)
        mixed = part_mixed if mixed is None else mixed + part_mixed
    total = mixed[:, HEAD:]
    return (mixed[:, :HEAD] / total).astype(BF), top * EXP2_SCALE + jnp.log2(total)


def forward_kernel(
    flags,
    query,
    key,
    value,
    key_before,
    value_before,
    init,
    gain,
    bias,
    query0,
    query1,
    key0,
    key1,
    second0,
    second1,
    token_mixed,
    state_mixed,
    turned,
    state_query,
    state_key,
    state_value,
    state_in,
    forget,
    apart,
    totals,
    state,
    token_totals,
    state_totals,
):
    block = pl.program_id(0)
    width = query0.shape[1]

    @pl.when(block == 0)
    def start():
        state[...] = init[...].astype(F32)

    now = state[...]
    state_in[...] = now
    state_normed = (now * inverse_rms(now) * gain[...]).astype(BF)
    turned[...] = state_normed.T
    for half, (one, other, two) in enumerate(((query0, key0, second0), (query1, key1, second1))):
        columns = slice(half * width, (half + 1) * width)
        state_query[:, columns] = nn(state_normed, one[...]).astype(BF)
        state_key[:, columns] = nn(state_normed, other[...]).astype(BF)
        state_value[:, columns] = nn(state_normed, two[:, :width]).astype(BF)
        gate = nn(state_normed, two[:, width : 2 * width]) + bias[:, columns]
        forget[:, columns] = jax.nn.sigmoid(gate)

    def heads(with_before):
        def head(index, carry):
            columns = pl.ds(pl.multiple_of(index * HEAD, HEAD), HEAD)
            lane = lax.broadcasted_iota(jnp.int32, (W, HEAD), 1) == index
            row = lax.broadcasted_iota(jnp.int32, (W, W), 0)
            column = lax.broadcasted_iota(jnp.int32, (W, W), 1)
            lead = jnp.where(row < HALF, flags[2 * block] * (HALF - 1 - row), flags[2 * block + 1] * (W - 1 - row))
            reach = column <= row + lead
            own = query[:, columns]
            parts = []
            if with_before:
                parts.append((nt(own, key_before[:, columns]), value_before[:, columns]))
            near = jnp.where(reach, nt(own, key[:, columns]), masked_score)
            parts.append((near, value[:, columns]))
            parts.append((nt(own, state_key[:, columns]), state_value[:, columns]))
            mixed, total = softmax_parts(parts)
            token_mixed[:, columns] = mixed
            token_totals[...] = jnp.where(lane, total, token_totals[...])
            own = state_query[:, columns]
            mixed, total = softmax_parts(
                [
                    (nt(own, key[:, columns]), value[:, columns]),
                    (nt(own, state_key[:, columns]), state_value[:, columns]),
                ]
            )
            state_mixed[:, columns] = mixed
            state_totals[...] = jnp.where(lane, total, state_totals[...])
            return carry

        lax.fori_loop(0, D // HEAD, head, 0, unroll=2)

    @pl.when(block == 0)
    def first():
        heads(False)

    @pl.when(block > 0)
    def later():
        heads(True)

    count = D // HEAD
    totals[0, :count, :] = token_totals[...].T[:count]
    totals[0, count:, :] = state_totals[...].T[:count]
    new = nt(state_mixed[:, :width], second0[:, 2 * width :]) + nt(
        state_mixed[:, width:], second1[:, 2 * width :]
    )
    apart[...] = (now - new).astype(BF)
    state[...] = new + forget[...] * (now - new)


def forward(flags, query, key, value, init, gain, bias, weights, more_weights):
    blocks = query.shape[0] // W
    heads = D // HEAD
    own = pl.BlockSpec((W, D), lambda b, s: (b, 0))
    before = pl.BlockSpec((W, D), lambda b, s: (jnp.maximum(b - 1, 0), 0))
    low = jax.ShapeDtypeStruct((blocks * W, D), BF)
    wide = jax.ShapeDtypeStruct((blocks * W, D), F32)
    return pl.pallas_call(
        forward_kernel,
        grid_spec=pltpu.PrefetchScalarGridSpec(
            num_scalar_prefetch=1,
            grid=(blocks,),
            in_specs=[
                own,
                own,
                own,
                before,
                before,
                once((S, D), lambda b, s: (0, 0)),
                once((1, D), lambda b, s: (0, 0)),
                once((1, D), lambda b, s: (0, 0)),
                once((D, D // 2), lambda b, s: (0, 3)),
                once((D, D // 2), lambda b, s: (1, 3)),
                once((D, D // 2), lambda b, s: (0, 4)),
                once((D, D // 2), lambda b, s: (1, 4)),
                once((D, more_weights.shape[1]), lambda b, s: (0, 0)),
                once((D, more_weights.shape[1]), lambda b, s: (1, 0)),
            ],
            out_specs=[own] * 2
            + [pl.BlockSpec((D, S), lambda b, s: (0, b))]
            + [own] * 6
            + [pl.BlockSpec((1, 2 * heads, W), lambda b, s: (b, 0, 0))],
            scratch_shapes=[
                pltpu.VMEM((S, D), F32),
                pltpu.VMEM((W, HEAD), F32),
                pltpu.VMEM((S, HEAD), F32),
            ],
        ),
        out_shape=[low] * 2
        + [jax.ShapeDtypeStruct((D, blocks * S), BF)]
        + [low] * 3
        + [wide, wide, low, jax.ShapeDtypeStruct((blocks, 2 * heads, W), F32)],
        compiler_params=params(),
        cost_estimate=cost(42e9, 100e6, 40e6),
        name="forward",
    )(
        flags,
        query,
        key,
        value,
        key,
        value,
        init,
        gain,
        bias,
        weights,
        weights,
        weights,
        weights,
        more_weights,
        more_weights,
    )


def middle_kernel(rows, mixed, w0, w1, gain, cotangent, middle, mlp_in, mlp_turned, cot_turned):
    width = w0.shape[1]
    here = (
        rows[...].astype(F32) + nt(mixed[:, :width], w0[...]) + nt(mixed[:, width:], w1[...])
    )
    middle[...] = here
    low = (here * inverse_rms(here) * gain[...]).astype(BF)
    mlp_in[...] = low
    mlp_turned[...] = low.T
    cot_turned[...] = cotangent[...].T


def middle_rows(rows, mixed, weights, gain, cotangent):
    tokens = rows.shape[0]
    width = D // 2
    last = weights.shape[1] // width - 1
    block = pl.BlockSpec((W, D), lambda b: (b, 0))
    turned = pl.BlockSpec((D, W), lambda b: (0, b))
    low = jax.ShapeDtypeStruct((tokens, D), BF)
    return pl.pallas_call(
        middle_kernel,
        grid=(tokens // W,),
        in_specs=[
            block,
            block,
            once((D, width), lambda b: (0, last)),
            once((D, width), lambda b: (1, last)),
            once((1, D), lambda b: (0, 0)),
            block,
        ],
        out_specs=[block, block, turned, turned],
        out_shape=[
            jax.ShapeDtypeStruct((tokens, D), F32),
            low,
            jax.ShapeDtypeStruct((D, tokens), BF),
            jax.ShapeDtypeStruct((D, tokens), BF),
        ],
        compiler_params=params(),
        cost_estimate=cost(2 * tokens * D * D, 2 * 8 * tokens * D),
        name="middle",
    )(rows, mixed, weights, weights, gain, cotangent)


def mlp_kernel(
    mlp_in, mlp_turned, cot, cot_turned, weights, out, grad_in, grads, out_sum, grad_sum, act, gh
):
    step = pl.program_id(0)
    units = weights.shape[1] // 2
    tokens = mlp_in.shape[0]

    @pl.when(step == 0)
    def start():
        out_sum[...] = jnp.zeros_like(out_sum)
        grad_sum[...] = jnp.zeros_like(grad_sum)

    slope = math.sqrt(2.0 / math.pi)

    def chunk(index, carry):
        rows = pl.ds(pl.multiple_of(index * W, W), W)
        hidden = nn(mlp_in[rows, :], weights[:, :units])
        back = nn(cot[rows, :], weights[:, units:])
        square = hidden * hidden
        bent = jnp.tanh(slope * hidden * (1.0 + 0.044715 * square))
        open_part = 0.5 * (1.0 + bent)
        active = (hidden * open_part).astype(BF)
        steep = open_part + (0.5 * slope) * hidden * (1.0 - bent * bent) * (
            1.0 + (3 * 0.044715) * square
        )
        grad = (steep * back).astype(BF)
        act[rows, :] = active
        gh[rows, :] = grad
        out_sum[rows, :] += nt(active, weights[:, units:])
        grad_sum[rows, :] += nt(grad, weights[:, :units])
        return carry

    lax.fori_loop(0, tokens // W, chunk, 0)
    grads[:, :units] = nn(mlp_turned[...], gh[...]).astype(BF)
    grads[:, units:] = nn(cot_turned[...], act[...]).astype(BF)

    @pl.when(step == pl.num_programs(0) - 1)
    def end():
        out[...] = out_sum[...].astype(BF)
        grad_in[...] = grad_sum[...].astype(BF)


def mlp(mlp_in, mlp_turned, cot, cot_turned, weights):
    tokens = mlp_in.shape[0]
    units = 512
    across = (weights.shape[1] - D // 2) // (2 * units)
    low = jax.ShapeDtypeStruct((tokens, D), BF)
    rows = once((tokens, D), lambda f: (0, 0))
    turned = once((D, tokens), lambda f: (0, 0))
    tile = pl.BlockSpec((D, 2 * units), lambda f: (f // across, f % across))
    return pl.pallas_call(
        mlp_kernel,
        grid=(2 * across,),
        in_specs=[rows, turned, rows, turned, tile],
        out_specs=[rows, rows, tile],
        out_shape=[low, low, jax.ShapeDtypeStruct(weights.shape, BF)],
        scratch_shapes=[
            pltpu.VMEM((tokens, D), F32),
            pltpu.VMEM((tokens, D), F32),
            pltpu.VMEM((tokens, units), BF),
            pltpu.VMEM((tokens, units), BF),
        ],
        compiler_params=params(),
        cost_estimate=cost(103e9, 60e6, 8e6),
        name="mlp",
    )(mlp_in, mlp_turned, cot, cot_turned, weights)


def after_mlp_kernel(
    middle, mlp_out, grad_in, cot, gain, w0, w1, output, grad_middle, turned, grad_mixed, grad_gain
):
    width = w0.shape[1]
    here = middle[...]
    inverse = inverse_rms(here)
    scaled = here * inverse
    grad = grad_in[...].astype(F32)
    output[...] = (here + mlp_out[...].astype(F32)).astype(BF)
    low = (cot[...].astype(F32) + rms_back(scaled, inverse, gain[...] * grad)).astype(BF)
    grad_middle[...] = low
    turned[...] = low.T
    grad_mixed[:, :width] = nn(low, w0[...]).astype(BF)
    grad_mixed[:, width:] = nn(low, w1[...]).astype(BF)
    part = jnp.sum(grad * scaled, axis=0, keepdims=True)

    @pl.when(pl.program_id(0) == 0)
    def first():
        grad_gain[...] = part

    @pl.when(pl.program_id(0) > 0)
    def later():
        grad_gain[...] += part


def after_mlp(middle, mlp_out, grad_in, cot, gain, weights):
    tokens = middle.shape[0]
    width = D // 2
    last = weights.shape[1] // width - 1
    block = pl.BlockSpec((W, D), lambda b: (b, 0))
    low = jax.ShapeDtypeStruct((tokens, D), BF)
    return pl.pallas_call(
        after_mlp_kernel,
        grid=(tokens // W,),
        in_specs=[
            block,
            block,
            block,
            block,
            once((1, D), lambda b: (0, 0)),
            once((D, width), lambda b: (0, last)),
            once((D, width), lambda b: (1, last)),
        ],
        out_specs=[
            block,
            block,
            pl.BlockSpec((D, W), lambda b: (0, b)),
            block,
            pl.BlockSpec((1, D), lambda b: (0, 0)),
        ],
        out_shape=[
            low,
            low,
            jax.ShapeDtypeStruct((D, tokens), BF),
            low,
            jax.ShapeDtypeStruct((1, D), F32),
        ],
        compiler_params=params(),
        cost_estimate=cost(2 * tokens * D * D, 2 * 8 * tokens * D),
        name="after_mlp",
    )(middle, mlp_out, grad_in, cot, gain, weights, weights)


def backward_kernel(
    flags,
    query,
    key,
    value,
    key_before,
    value_before,
    state_query,
    state_key,
    state_value,
    token_mixed,
    state_mixed,
    grad_mixed,
    totals,
    forget,
    state_in,
    apart,
    gain,
    weight_query,
    weight_key,
    more_weight,
    wso0,
    wso1,
    grad_tokens,
    grad_states,
    branch,
    grad_init,
    grad_gain,
    grad_bias,
    grad_state,
    grad_state_mixed,
    grad_normed,
    gate_part,
    carry_key,
    carry_value,
):
    step = pl.program_id(0)
    half = pl.program_id(1)
    block = pl.num_programs(0) - 1 - step
    width = wso0.shape[1]
    local = width // HEAD
    count = D // HEAD

    @pl.when((step == 0) & (half == 0))
    def start():
        grad_state[...] = jnp.zeros_like(grad_state)
        carry_key[...] = jnp.zeros_like(carry_key)
        carry_value[...] = jnp.zeros_like(carry_value)
        grad_gain[...] = jnp.zeros_like(grad_gain)
        grad_bias[...] = jnp.zeros_like(grad_bias)

    @pl.when(half == 0)
    def begin():
        coming = grad_state[...]
        keep = forget[...]
        low = ((1.0 - keep) * coming).astype(BF)
        branch[...] = low.T
        gate = (coming * apart[...].astype(F32) * keep * (1.0 - keep)).astype(BF)
        gate_part[0] = gate[:, :width]
        gate_part[1] = gate[:, width:]
        grad_bias[...] += jnp.sum(gate.astype(F32), axis=0, keepdims=True)
        grad_state_mixed[0] = nn(low, wso0[...]).astype(BF)
        grad_state_mixed[1] = nn(low, wso1[...]).astype(BF)
        grad_normed[...] = jnp.zeros_like(grad_normed)

    grad_states[3] = gate_part[half]

    def heads(with_before):
        def head(index, carry):
            columns = pl.ds(pl.multiple_of(index * HEAD, HEAD), HEAD)
            at = half * local + index
            queries = jnp.concatenate([query[:, columns], state_query[:, columns]], axis=0)
            grads_out = jnp.concatenate(
                [grad_mixed[:, columns], grad_state_mixed[half, :, columns]], axis=0
            )
            mixed = jnp.concatenate([token_mixed[:, columns], state_mixed[:, columns]], axis=0)
            product = grads_out.astype(F32) * mixed.astype(F32)
            delta = jnp.sum(product.T, axis=0, keepdims=True)
            token_total = totals[0, pl.ds(at, 1), :]
            state_total = totals[0, pl.ds(count + at, 1), :]
            total = jnp.concatenate([token_total, state_total], axis=1)

            def chunk(keys, values, first, last, mask):
                some = queries[first:last]
                some_grads = grads_out[first:last]
                scores = nt(keys, some)
                if mask is not None:
                    size = mask.shape[1]
                    scores = jnp.concatenate(
                        [jnp.where(mask, scores[:, :size], masked_score), scores[:, size:]], axis=1
                    )
                weights = jnp.exp2(scores * EXP2_SCALE - total[:, first:last])
                back = nt(values, some_grads) - delta[:, first:last]
                grad_scores = (weights * back).astype(BF)
                grad_values = nn(weights.astype(BF), some_grads)
                grad_keys = nn(grad_scores, some)
                return grad_keys * SCORE_SCALE, grad_values, tn(keys, grad_scores)

            turned = None
            for first in range(0, S, HALF):
                rows = slice(first, first + HALF)
                grad_keys, grad_values, part = chunk(
                    state_key[rows, columns], state_value[rows, columns], 0, W + S, None
                )
                grad_states[1, rows, columns] = grad_keys.astype(BF)
                grad_states[2, rows, columns] = grad_values.astype(BF)
                turned = part if turned is None else turned + part
            for part in range(2):
                rows = slice(part * HALF, (part + 1) * HALF)
                row = lax.broadcasted_iota(jnp.int32, (HALF, HALF), 0)
                column = lax.broadcasted_iota(jnp.int32, (HALF, HALF), 1)
                mask = row <= column + flags[2 * block + part] * HALF
                grad_keys, grad_values, more = chunk(
                    key[rows, columns], value[rows, columns], part * HALF, W + S, mask
                )
                grad_tokens[1, rows, columns] = (grad_keys + carry_key[half, rows, columns]).astype(
                    BF
                )
                grad_tokens[2, rows, columns] = (
                    grad_values + carry_value[half, rows, columns]
                ).astype(BF)
                if part:
                    more = jnp.concatenate([jnp.zeros((HEAD, HALF), F32), more], axis=1)
                turned = turned + more
            turned_tokens = turned[:, :W]
            if with_before:
                for first in range(0, W, HALF):
                    rows = slice(first, first + HALF)
                    grad_keys, grad_values, part = chunk(
                        key_before[rows, columns], value_before[rows, columns], 0, W, None
                    )
                    carry_key[half, rows, columns] = grad_keys
                    carry_value[half, rows, columns] = grad_values
                    turned_tokens = turned_tokens + part
            grad_tokens[0, :, columns] = (turned_tokens * SCORE_SCALE).T.astype(BF)
            grad_states[0, :, columns] = (turned[:, W:] * SCORE_SCALE).T.astype(BF)
            return carry

        lax.fori_loop(0, local, head, 0, unroll=2)

    @pl.when(block > 0)
    def later():
        heads(True)

    @pl.when(block == 0)
    def first():
        heads(False)

    grad_normed[...] += (
        nt(grad_states[0], weight_query[...])
        + nt(grad_states[1], weight_key[...])
        + nt(grad_states[2], more_weight[:, :width])
        + nt(grad_states[3], more_weight[:, width:])
    )

    @pl.when(half == 1)
    def finish():
        here = state_in[...]
        inverse = inverse_rms(here)
        scaled = here * inverse
        grad = grad_normed[...]
        grad_gain[...] += jnp.sum(grad * scaled, axis=0, keepdims=True)
        grad_state[...] = forget[...] * grad_state[...] + rms_back(
            scaled, inverse, gain[...] * grad
        )

    @pl.when((half == 1) & (block == 0))
    def end():
        grad_init[...] = grad_state[...].astype(BF)


def backward(
    flags,
    query,
    key,
    value,
    state_query,
    state_key,
    state_value,
    token_mixed,
    state_mixed,
    grad_mixed,
    totals,
    forget,
    state_in,
    apart,
    gain,
    weights,
    more_weights,
):
    blocks = query.shape[0] // W
    heads = D // HEAD
    half_width = D // 2

    def rev(b):
        return blocks - 1 - b

    own = pl.BlockSpec((W, half_width), lambda b, t, s: (rev(b), t))
    before = pl.BlockSpec((W, half_width), lambda b, t, s: (jnp.maximum(rev(b) - 1, 0), t))
    whole = pl.BlockSpec((S, D), lambda b, t, s: (rev(b), 0))
    fixed_row = pl.BlockSpec((1, D), lambda b, t, s: (0, 0))
    return pl.pallas_call(
        backward_kernel,
        grid_spec=pltpu.PrefetchScalarGridSpec(
            num_scalar_prefetch=1,
            grid=(blocks, 2),
            in_specs=[own, own, own, before, before]
            + [own] * 6
            + [pl.BlockSpec((1, 2 * heads, W), lambda b, t, s: (rev(b), 0, 0))]
            + [whole] * 3
            + [
                once((1, D), lambda b, t, s: (0, 0)),
                pl.BlockSpec((D, half_width), lambda b, t, s: (t, 3)),
                pl.BlockSpec((D, half_width), lambda b, t, s: (t, 4)),
                pl.BlockSpec((D, 2 * half_width), lambda b, t, s: (t, 0)),
                once((D, half_width), lambda b, t, s: (0, 2)),
                once((D, half_width), lambda b, t, s: (1, 2)),
            ],
            out_specs=[
                pl.BlockSpec((3, W, half_width), lambda b, t, s: (0, rev(b), t)),
                pl.BlockSpec((4, S, half_width), lambda b, t, s: (0, rev(b), t)),
                pl.BlockSpec((D, S), lambda b, t, s: (0, rev(b))),
                pl.BlockSpec((S, D), lambda b, t, s: (0, 0)),
                fixed_row,
                fixed_row,
            ],
            scratch_shapes=[
                pltpu.VMEM((S, D), F32),
                pltpu.VMEM((2, S, half_width), BF),
                pltpu.VMEM((S, D), F32),
                pltpu.VMEM((2, S, half_width), BF),
                pltpu.VMEM((2, W, half_width), F32),
                pltpu.VMEM((2, W, half_width), F32),
            ],
        ),
        out_shape=[
            jax.ShapeDtypeStruct((3, blocks * W, D), BF),
            jax.ShapeDtypeStruct((4, blocks * W, D), BF),
            jax.ShapeDtypeStruct((D, blocks * W), BF),
            jax.ShapeDtypeStruct((S, D), BF),
            jax.ShapeDtypeStruct((1, D), F32),
            jax.ShapeDtypeStruct((1, D), F32),
        ],
        compiler_params=params(("arbitrary", "arbitrary")),
        cost_estimate=cost(70e9, 100e6, 40e6),
        name="backward",
    )(
        flags,
        query,
        key,
        value,
        key,
        value,
        state_query,
        state_key,
        state_value,
        token_mixed,
        state_mixed,
        grad_mixed,
        totals,
        forget,
        state_in,
        apart,
        gain,
        weights,
        weights,
        more_weights,
        more_weights,
        more_weights,
    )


def whole_grad_kernel(turned, right, into, out):
    out[...] = nn(turned[...], right[...]).astype(BF)


def whole_weight_grad(turned, right, into):
    tokens = right.shape[0]
    width = D // 2
    last = into.shape[1] // width - 1
    return pl.pallas_call(
        whole_grad_kernel,
        grid=(2,),
        in_specs=[
            once((D, tokens), lambda g: (0, 0)),
            pl.BlockSpec((tokens, width), lambda g: (0, g)),
            pl.BlockSpec(memory_space=pl.ANY),
        ],
        out_specs=pl.BlockSpec((D, width), lambda g: (g, last)),
        out_shape=jax.ShapeDtypeStruct(into.shape, BF),
        input_output_aliases={2: 0},
        compiler_params=params(),
        cost_estimate=cost(2 * tokens * D * D, 2 * (tokens * D + 2 * D * D)),
        name="whole_weight_grad",
    )(turned, right, into)


def weight_grad_kernel(groups, core, turned, right, *rest):
    keep, send = rest[-2:]
    grads = nn(turned[...], right[0]).astype(BF)
    group = turned.shape[0] // groups
    grads = grads.reshape(groups // 2, 2, group, grads.shape[1])
    shape = keep.shape
    low = grads[:, 0].reshape(shape)
    high = grads[:, 1].reshape(shape)
    mine = core[0] == 0
    keep[...] = jnp.where(mine, low, high)
    send[...] = jnp.where(mine, high, low)


def weight_grads(dp, core, turned, rights, first=0, many=1, across=0, at=0, into=None):
    tokens = rights.shape[1]
    width = D // 2
    across = across or many
    out = jax.ShapeDtypeStruct((D, across * width), BF)
    tile = pl.BlockSpec((D // 2, width), lambda g, s: (g % 2, at + g // 2))
    into = into or ()
    return pl.pallas_call(
        functools.partial(weight_grad_kernel, dp),
        grid_spec=pltpu.PrefetchScalarGridSpec(
            num_scalar_prefetch=1,
            grid=(2 * many,),
            in_specs=[
                once((D, tokens), lambda g, s: (0, 0)),
                pl.BlockSpec((1, tokens, width), lambda g, s: (first + g // 2, 0, g % 2)),
            ]
            + [pl.BlockSpec(memory_space=pl.ANY)] * len(into),
            out_specs=[tile, tile],
        ),
        out_shape=[out, out],
        input_output_aliases={3 + i: i for i in range(len(into))},
        compiler_params=params(),
        cost_estimate=cost(2 * tokens * D * D * many, 2 * (tokens * D + 2 * many * D * D)),
        name="weight_grads",
    )(core, turned, rights, *into)


def token_grad_kernel(grads, w0, w1, rows, grad_middle, gain, out, grad_gain):
    width = w0.shape[1] // 3
    total = None
    for which in range(3):
        for half, weight in enumerate((w0, w1)):
            part = nt(
                grads[which, :, half * width : (half + 1) * width],
                weight[:, which * width : (which + 1) * width],
            )
            total = part if total is None else total + part
    here = rows[...].astype(F32)
    inverse = inverse_rms(here)
    scaled = here * inverse
    out[...] = (
        grad_middle[...].astype(F32) + rms_back(scaled, inverse, gain[...] * total)
    ).astype(BF)
    part = jnp.sum(total * scaled, axis=0, keepdims=True)

    @pl.when(pl.program_id(0) == 0)
    def first():
        grad_gain[...] = part

    @pl.when(pl.program_id(0) > 0)
    def later():
        grad_gain[...] += part


def token_grad(grads, weights, rows, grad_middle, gain):
    tokens = rows.shape[0]
    width = 3 * D // 2
    block = pl.BlockSpec((W, D), lambda b: (b, 0))
    return pl.pallas_call(
        token_grad_kernel,
        grid=(tokens // W,),
        in_specs=[
            pl.BlockSpec((3, W, D), lambda b: (0, b, 0)),
            once((D, width), lambda b: (0, 0)),
            once((D, width), lambda b: (1, 0)),
            block,
            block,
            once((1, D), lambda b: (0, 0)),
        ],
        out_specs=[block, pl.BlockSpec((1, D), lambda b: (0, 0))],
        out_shape=[jax.ShapeDtypeStruct((tokens, D), BF), jax.ShapeDtypeStruct((1, D), F32)],
        compiler_params=params(),
        cost_estimate=cost(2 * tokens * 3 * D * D, 2 * 6 * tokens * D),
        name="token_grad",
    )(grads, weights, weights, rows, grad_middle, gain)


def gather(local):
    return lax.all_gather(local, ("tensor", "dp"), axis=0, tiled=True)


def scatter(total):
    return lax.psum_scatter(total, ("tensor", "dp"), scatter_dimension=0, tiled=True)


def axes_of(dp):
    return ["tensor"] + list(reversed(range(dp.bit_length() - 1)))


def side_of(axis):
    if axis == "tensor":
        return lax.axis_index("tensor")
    return (lax.axis_index("dp") >> axis) & 1


def trade(values, axis, dp):
    if axis == "tensor":
        return lax.ppermute(values, "tensor", [(0, 1), (1, 0)])
    return lax.ppermute(values, "dp", [(i, i ^ (1 << axis)) for i in range(dp)])


def order_of(dp, turn):
    bits = dp.bit_length() - 1
    middle = ["tensor"] + ([1] if bits > 1 else [])
    if turn:
        middle = middle[::-1]
    return ([0] if bits else []) + middle + list(range(2, bits))


class Halving:
    def __init__(self, keep, send, dp, turn):
        self.dp = dp
        self.axes = axes_of(dp)
        self.left = order_of(dp, turn)
        self.rest = 2 * keep.shape[0] >> len(self.axes)
        self.keep = keep
        self.sent = send

    def send(self):
        axis = self.left[0]
        where = self.axes.index(axis)
        columns = self.part.shape[1]
        many = len(self.axes) - where - 1
        pairs = self.part.reshape(1 << where, 2, self.rest << many, columns)
        side = side_of(axis)
        self.sent = lax.dynamic_index_in_dim(pairs, 1 - side, 1, keepdims=False)
        self.keep = lax.dynamic_index_in_dim(pairs, side, 1, keepdims=False)
        return self.sent

    def go(self):
        self.come = trade(self.sent, self.left[0], self.dp)

    def add(self, earlier=None):
        come = self.come if earlier is None else after(self.come, earlier)
        total = (self.keep.astype(F32) + come.astype(F32)).astype(BF)
        self.part = total.reshape(-1, total.shape[-1])
        self.axes.remove(self.left.pop(0))
        if self.left:
            self.send()


def finish(many):
    while any(one.left for one in many):
        active = [one for one in many if one.left]
        for one in active:
            one.go()
        for one, come in zip(active, lax.optimization_barrier([one.come for one in active])):
            one.come = come
            one.add()
    return [one.part for one in many]


def split_core(total, dp):
    groups = total.reshape(dp, 2, total.shape[0] // (2 * dp), total.shape[1])
    side = side_of(0)
    keep = lax.dynamic_index_in_dim(groups, side, 1, keepdims=False)
    send = lax.dynamic_index_in_dim(groups, 1 - side, 1, keepdims=False)
    return [one.reshape(total.shape[0] // 2, total.shape[1]) for one in (keep, send)]


def gather_steps(local, dp, turn, earlier):
    axes = axes_of(dp)
    done = []
    part = local
    for axis in reversed(order_of(dp, turn)):
        if axis == "tensor":
            part = after(part, earlier)
        come = trade(part, axis, dp)
        low = side_of(axis) == 0
        done = [one for one in axes if one == axis or one in done]
        lead = 1 << done.index(axis)
        pair = [jnp.where(low, part, come), jnp.where(low, come, part)]
        pair = [one.reshape(lead, part.shape[0] // lead, part.shape[1]) for one in pair]
        part = jnp.stack(pair, axis=1).reshape(2 * part.shape[0], part.shape[1])
    return part


def after(values, earlier):
    return lax.optimization_barrier((values, earlier))[0]


def whole_sequence_body(
    tokens_in,
    piece_starts,
    cotangent,
    gain_tokens,
    gain_mlp,
    gain_state,
    gate_bias,
    w_query,
    w_key,
    w_value,
    w_out,
    w_state_query,
    w_state_key,
    w_state_value,
    w_state_out,
    w_gate,
    w_up,
    w_down,
    state_init,
):
    mine = lax.axis_index("tensor")
    first = mine == 0
    local_rows = w_query.shape[0]
    dp = D // local_rows
    width = w_query.shape[1]
    units = 512
    across = w_up.shape[1] // units
    swap = [(0, 1), (1, 0)]

    def other_half(pair):
        return lax.ppermute(jnp.where(first, pair[1, 0], pair[0, 0]), "tensor", swap)

    def bring(pair, come):
        keep = jnp.where(first, pair[0, 0], pair[1, 0])
        top = jnp.where(first, keep, come)
        low = jnp.where(first, come, keep)
        return jnp.concatenate([top, low], axis=1).reshape(NB * W, D)

    def give(rows, later=None):
        halves = rows.reshape(NB, 2, HALF, D)
        keep = jnp.where(first, halves[:, 0], halves[:, 1])
        send = jnp.where(first, halves[:, 1], halves[:, 0])
        come = lax.ppermute(send, "tensor", swap)
        if later is not None:
            come = after(come, later)
        return jnp.stack([jnp.where(first, keep, come), jnp.where(first, come, keep)])[:, None]

    def split_init(values):
        side = values.shape[1] // 2
        return jnp.concatenate([values[:, :side], values[:, side:]], axis=0)

    gains = jnp.stack([gain_tokens, gain_mlp, gain_state, gate_bias])
    small = jnp.concatenate(
        [split_init(state_init), jnp.pad(gains, ((0, local_rows - 4), (0, 128 - local_rows)))],
        axis=1,
    )
    full_qkv = gather(
        jnp.concatenate([w_query, w_key, w_value, w_state_query, w_state_key, small], axis=1)
    )
    full_small = full_qkv[:, 5 * width :]
    turned_down = w_down.T
    late = []
    for unit in range(0, across * units, units):
        late += [w_up[:, unit : unit + units], turned_down[:, unit : unit + units]]
    late = jnp.concatenate(late + [w_out.T], axis=1)
    rows = bring(tokens_in, other_half(tokens_in))
    full_state1 = gather_steps(
        jnp.concatenate([w_state_value, w_gate, w_state_out.T], axis=1), dp, False, (rows, late)
    )
    full_late = gather(after(late, (full_qkv, full_state1)))
    side = width // 2
    init = full_small[:, :side].reshape(2, dp, 2, local_rows // 2, side)
    init = jnp.transpose(init, (1, 3, 0, 2, 4)).reshape(S, D)
    gains = full_small[:D, side:].reshape(dp, local_rows, 128)[:, :4, :local_rows]
    gains = jnp.transpose(gains, (1, 0, 2)).reshape(4, 1, D).astype(F32)

    cot_half = other_half(after(cotangent, rows))
    starts = jnp.where(first, piece_starts[0, 0], piece_starts[1, 0])
    flags = jnp.any(
        starts[:, None] == PIECE * jnp.arange(NB * W // PIECE, dtype=jnp.int32)[None], axis=0
    ).astype(jnp.int32)

    turned, query, key, value = project(rows, gains[0], full_qkv)
    (
        token_mixed,
        state_mixed,
        state_turned,
        state_query,
        state_key,
        state_value,
        state_in,
        forget,
        apart,
        totals,
    ) = forward(flags, query, key, value, init, gains[2], gains[3], full_qkv, full_state1)
    cot = bring(cotangent, after(cot_half, token_mixed))
    middle, mlp_in, mlp_turned, cot_turned = middle_rows(
        rows, token_mixed, full_late, gains[1], cot
    )
    mlp_out, grad_mlp_in, grad_mlp_w = mlp(mlp_in, mlp_turned, cot, cot_turned, full_late)
    output, grad_middle, middle_turned, grad_mixed, grad_gain_mlp = after_mlp(
        middle, mlp_out, grad_mlp_in, cot, gains[1], full_late
    )
    grads_late = whole_weight_grad(middle_turned, token_mixed, grad_mlp_w)
    part_late = scatter(grads_late)
    core = (side_of(0) & 1).astype(jnp.int32).reshape(1)
    grad_tok, grad_sta, branch, grad_init, grad_gain_state, grad_bias = backward(
        flags,
        query,
        key,
        value,
        state_query,
        state_key,
        state_value,
        token_mixed,
        state_mixed,
        after(grad_mixed, grads_late),
        totals,
        forget,
        state_in,
        apart,
        gains[2],
        full_qkv,
        full_state1,
    )
    given_output = give(output, grad_tok)

    a = Halving(*weight_grads(dp, core, state_turned, after(grad_sta, given_output), 0, 2), dp, False)
    a.go()
    b = Halving(*weight_grads(dp, core, state_turned, after(grad_sta, a.sent), 2, 2), dp, True)
    a.add(b.keep)
    a.go()
    b.go()
    c = Halving(*weight_grads(dp, core, turned, after(grad_tok, (a.sent, b.sent)), 1, 2), dp, False)
    b.add(c.keep)
    b.go()
    c.go()
    grads_q = weight_grads(dp, core, turned, after(grad_tok, (b.sent, c.sent)), 0, 1, 2, 0)
    c.add(grads_q)
    c.go()
    d = Halving(
        *weight_grads(dp, core, after(branch, c.sent), state_mixed[None], 0, 1, 2, 1, grads_q),
        dp,
        True,
    )
    d.go()
    grad_in, grad_gain_tokens = token_grad(
        after(grad_tok, (d.sent, part_late)), full_qkv, rows, grad_middle, gains[0]
    )
    a.add(grad_in)
    d.add(grad_in)
    b.add(grad_in)
    init_parts = jnp.transpose(
        grad_init.reshape(dp, local_rows // 2, 2, 2, side), (2, 0, 3, 1, 4)
    ).reshape(2 * D, side)
    gain_parts = jnp.stack(
        [grad_gain_tokens[0], grad_gain_mlp[0], grad_gain_state[0], grad_bias[0]]
    ).reshape(4, dp, local_rows)
    gain_parts = jnp.pad(
        jnp.transpose(gain_parts, (1, 0, 2)),
        ((0, 0), (0, local_rows - 4), (0, 128 - local_rows)),
    ).reshape(D, 128)
    gain_parts = jnp.concatenate([gain_parts, gain_parts], axis=0).astype(BF)
    e = Halving(*split_core(jnp.concatenate([init_parts, gain_parts], axis=1), dp), dp, True)
    given_grad = give(grad_in)
    part_rest, part_kv, part_sqk, part_svg, part_small = [
        one.astype(F32) for one in finish([d, c, a, b, e])
    ]
    part_so = part_rest[:, width:]
    part_init = part_small[:, :side]
    part_init = jnp.concatenate(
        [part_init[: local_rows // 2], part_init[local_rows // 2 :]], axis=1
    )
    part_gains = part_small[:4, side : side + local_rows]
    part_late = part_late.astype(F32)
    part_up = [part_late[:, 2 * i * units : (2 * i + 1) * units] for i in range(across)]
    part_down = [part_late[:, (2 * i + 1) * units : (2 * i + 2) * units] for i in range(across)]
    part_sqk = part_sqk.astype(F32)
    part_svg = part_svg.astype(F32)
    return (
        given_output,
        given_grad,
        part_gains[0],
        part_gains[1],
        part_gains[2],
        part_gains[3],
        part_rest[:, :width],
        part_kv[:, :width],
        part_kv[:, width:],
        part_late[:, 2 * across * units :].T,
        part_sqk[:, :width],
        part_sqk[:, width:],
        part_svg[:, :width],
        part_so.T,
        part_svg[:, width:],
        jnp.concatenate(part_up, axis=1),
        jnp.concatenate([one.T for one in part_down], axis=0),
        part_init,
    )


def solution(mesh):
    dp = mesh.shape["dp"]
    one_each = mesh.shape["tensor"] == MICRO and dp > 1 and dp & (dp - 1) == 0
    return jax.shard_map(
        whole_sequence_body if one_each else generic_body,
        mesh=mesh,
        in_specs=(
            P(None, "dp", None, "tensor", None),
            P(None, "dp", None),
            P(None, "dp", None, "tensor", None),
            P("dp"),
            P("dp"),
            P("dp"),
            P("dp"),
            P("dp", "tensor"),
            P("dp", "tensor"),
            P("dp", "tensor"),
            P("tensor", "dp"),
            P("dp", "tensor"),
            P("dp", "tensor"),
            P("dp", "tensor"),
            P("tensor", "dp"),
            P("dp", "tensor"),
            P("dp", "tensor"),
            P("tensor", "dp"),
            P("dp", "tensor"),
        ),
        out_specs=(
            P(None, "dp", None, "tensor", None),
            P(None, "dp", None, "tensor", None),
            P("dp"),
            P("dp"),
            P("dp"),
            P("dp"),
            P("dp", "tensor"),
            P("dp", "tensor"),
            P("dp", "tensor"),
            P("tensor", "dp"),
            P("dp", "tensor"),
            P("dp", "tensor"),
            P("dp", "tensor"),
            P("tensor", "dp"),
            P("dp", "tensor"),
            P("dp", "tensor"),
            P("tensor", "dp"),
            P("dp", "tensor"),
        ),
        check_vma=False,
    )
```

```python
import functools
import math

import jax
import jax.numpy as jnp
from jax import lax
from jax.experimental import pallas as pl
from jax.experimental.pallas import tpu as pltpu
from jax.sharding import PartitionSpec as P

D = 1024
HEAD = 128
W = 512
S = 512
PIECE = 256
MICRO = 2
NB = 4


epsilon = 1e-06
masked_score = -1e30


def rms_scale(values):
    return values * lax.rsqrt(jnp.mean(values * values, axis=-1, keepdims=True) + epsilon)


def normed_rows(values, gain):
    return rms_scale(values) * gain


def matmul(left, right):
    return jnp.dot(left, right, preferred_element_type=jnp.float32)


def mlp_local(full_in, full_up, full_down):
    hidden = matmul(full_in, full_up)
    active = jax.nn.gelu(hidden).astype(jnp.bfloat16)
    return (hidden, active, matmul(active, full_down))


def mlp_back_local(full_grad, active, hidden, full_in, full_down, full_up):
    grad_down_w = jnp.einsum("...f,...d->fd", active, full_grad, preferred_element_type=jnp.float32)
    grad_active = jnp.einsum(
        "...d,fd->...f", full_grad, full_down, preferred_element_type=jnp.float32
    )
    unused_value, gelu_back = jax.vjp(jax.nn.gelu, hidden)
    grad_hidden = gelu_back(grad_active)[0].astype(jnp.bfloat16)
    grad_up_w = jnp.einsum(
        "...d,...f->df", full_in, grad_hidden, preferred_element_type=jnp.float32
    )
    mlp_part = jnp.einsum("...f,df->...d", grad_hidden, full_up, preferred_element_type=jnp.float32)
    return (grad_down_w, grad_up_w, mlp_part)


def piece_labels(starts):
    positions = jnp.arange(NB * W, dtype=jnp.int32)
    inside = (positions[None, None, :] >= starts[:, :, None]) & (
        positions[None, None, :] < starts[:, :, None] + PIECE
    )
    numbers = jnp.arange(1, starts.shape[1] + 1, dtype=jnp.int32)
    return jnp.sum(jnp.where(inside, numbers[None, :, None], 0), axis=1)


def token_mask(labels, block):
    batch = labels.shape[0]
    own = labels[:, block * W : (block + 1) * W]
    local = jnp.arange(W, dtype=jnp.int32)
    causal = (local[None, :] <= local[:, None])[None]
    together = (own[:, :, None] == own[:, None, :]) & (own[:, :, None] > 0)
    current = causal | together
    earlier = jnp.full((batch, W, W), block > 0)
    state_part = jnp.ones((batch, W, S), dtype=bool)
    return jnp.concatenate([earlier, current, state_part], axis=2)[:, None]


def split_heads(values):
    return values.reshape(values.shape[0], values.shape[1], values.shape[2] // HEAD, HEAD)


def scores_of(query, keys, allowed):
    scores = jnp.einsum(
        "brhe,bkhe->bhrk", split_heads(query), split_heads(keys), preferred_element_type=jnp.float32
    ) * (1.0 / math.sqrt(HEAD))
    return jnp.where(allowed, scores, masked_score)


def attend(query, keys, values, allowed):
    scores = scores_of(query, keys, allowed)
    top = jnp.max(scores, axis=-1, keepdims=True)
    total = top + jnp.log(jnp.sum(jnp.exp(scores - top), axis=-1, keepdims=True))
    weights = jnp.exp(scores - total).astype(jnp.bfloat16)
    mixed = jnp.einsum(
        "bhrk,bkhe->brhe", weights, split_heads(values), preferred_element_type=jnp.float32
    )
    return (mixed.reshape(query.shape).astype(jnp.bfloat16), total)


def attend_back(query, keys, values, allowed, total, grad_mixed):
    scale = 1.0 / math.sqrt(HEAD)
    weights = jnp.exp(scores_of(query, keys, allowed) - total)
    grad_heads = split_heads(grad_mixed)
    grad_weights = jnp.einsum(
        "brhe,bkhe->bhrk", grad_heads, split_heads(values), preferred_element_type=jnp.float32
    )
    grad_scores = (
        weights * (grad_weights - jnp.sum(weights * grad_weights, axis=-1, keepdims=True))
    ).astype(jnp.bfloat16)
    grad_query = (
        jnp.einsum(
            "bhrk,bkhe->brhe", grad_scores, split_heads(keys), preferred_element_type=jnp.float32
        )
        * scale
    )
    grad_keys = (
        jnp.einsum(
            "bhrk,brhe->bkhe", grad_scores, split_heads(query), preferred_element_type=jnp.float32
        )
        * scale
    )
    grad_values = jnp.einsum(
        "bhrk,brhe->bkhe",
        weights.astype(jnp.bfloat16),
        grad_heads,
        preferred_element_type=jnp.float32,
    )
    return (
        grad_query.reshape(query.shape),
        grad_keys.reshape(keys.shape),
        grad_values.reshape(values.shape),
    )


def generic_body(
    tokens_in,
    piece_starts,
    cotangent,
    gain_tokens,
    gain_mlp,
    gain_state,
    gate_bias,
    w_query,
    w_key,
    w_value,
    w_out,
    w_state_query,
    w_state_key,
    w_state_value,
    w_state_out,
    w_gate,
    w_up,
    w_down,
    state_init,
):
    width_local = w_query.shape[1]
    column_start = lax.axis_index("tensor") * width_local

    def collect():
        return (
            lax.all_gather(w_query, "dp", axis=0, tiled=True),
            lax.all_gather(w_key, "dp", axis=0, tiled=True),
            lax.all_gather(w_value, "dp", axis=0, tiled=True),
            lax.all_gather(w_state_query, "dp", axis=0, tiled=True),
            lax.all_gather(w_state_key, "dp", axis=0, tiled=True),
            lax.all_gather(w_state_value, "dp", axis=0, tiled=True),
            lax.all_gather(w_gate, "dp", axis=0, tiled=True),
            lax.all_gather(w_up, "dp", axis=0, tiled=True),
            lax.all_gather(state_init, "dp", axis=0, tiled=True),
            lax.all_gather(w_out, "dp", axis=1, tiled=True),
            lax.all_gather(w_state_out, "dp", axis=1, tiled=True),
            lax.all_gather(w_down, "dp", axis=1, tiled=True),
            lax.all_gather(gain_tokens, "dp", axis=0, tiled=True),
            lax.all_gather(gain_mlp, "dp", axis=0, tiled=True),
            lax.all_gather(gain_state, "dp", axis=0, tiled=True),
            lax.all_gather(gate_bias, "dp", axis=0, tiled=True),
        )

    def unpack_gains(weights):
        token_gain = weights[12].astype(jnp.float32)
        mlp_gain = weights[13].astype(jnp.float32)
        state_gain = lax.dynamic_slice_in_dim(
            weights[14].astype(jnp.float32), column_start, width_local
        )
        bias_columns = lax.dynamic_slice_in_dim(
            weights[15].astype(jnp.float32), column_start, width_local
        )
        return (token_gain, mlp_gain, state_gain, bias_columns)

    outputs = []
    input_grads = []
    totals = None
    for micro in range(MICRO):
        forward_weights = collect()
        forward_rows_in = tokens_in[micro]
        (
            forward_full_query,
            forward_full_key,
            forward_full_value,
            forward_full_state_query,
            forward_full_state_key,
            forward_full_state_value,
            forward_full_gate,
            forward_full_up,
            forward_full_init,
            forward_full_out,
            forward_full_state_out,
            forward_full_down,
        ) = forward_weights[:12]
        forward_token_gain, forward_mlp_gain, forward_state_gain, forward_bias_columns = (
            unpack_gains(forward_weights)
        )
        forward_batch = forward_rows_in.shape[0]
        forward_labels = piece_labels(piece_starts[micro])
        forward_state = jnp.broadcast_to(
            forward_full_init.astype(jnp.float32), (forward_batch, S, width_local)
        )
        zero_keys = jnp.zeros((forward_batch, W, width_local), jnp.bfloat16)
        forward_earlier_key = zero_keys
        forward_earlier_value = zero_keys
        forward_kept = []
        middles = []
        for forward_block in range(NB):
            forward_rows = forward_rows_in[:, forward_block].astype(jnp.float32)
            normed = normed_rows(forward_rows, forward_token_gain).astype(jnp.bfloat16)
            square_sum = lax.psum(jnp.sum(forward_state * forward_state, axis=-1), "tensor")
            forward_inverse = lax.rsqrt(square_sum / D + epsilon)[..., None]
            forward_scaled = forward_state * forward_inverse
            state_normed = (forward_scaled * forward_state_gain).astype(jnp.bfloat16)
            forward_full_normed, forward_full_state = (
                lax.all_gather(normed, "tensor", axis=1, tiled=True),
                lax.all_gather(state_normed, "tensor", axis=2, tiled=True),
            )
            forward_query = matmul(forward_full_normed, forward_full_query).astype(jnp.bfloat16)
            forward_key = matmul(forward_full_normed, forward_full_key).astype(jnp.bfloat16)
            forward_value = matmul(forward_full_normed, forward_full_value).astype(jnp.bfloat16)
            forward_state_query = matmul(forward_full_state, forward_full_state_query).astype(
                jnp.bfloat16
            )
            forward_state_key = matmul(forward_full_state, forward_full_state_key).astype(
                jnp.bfloat16
            )
            forward_state_value = matmul(forward_full_state, forward_full_state_value).astype(
                jnp.bfloat16
            )
            gate_pre = matmul(forward_full_state, forward_full_gate) + forward_bias_columns
            forward_allowed = token_mask(forward_labels, forward_block)
            forward_token_keys = jnp.concatenate(
                [forward_earlier_key, forward_key, forward_state_key], axis=1
            )
            forward_token_values = jnp.concatenate(
                [forward_earlier_value, forward_value, forward_state_value], axis=1
            )
            forward_token_mixed, forward_token_total = attend(
                forward_query, forward_token_keys, forward_token_values, forward_allowed
            )
            forward_cross_keys = jnp.concatenate([forward_key, forward_state_key], axis=1)
            forward_cross_values = jnp.concatenate([forward_value, forward_state_value], axis=1)
            forward_state_mixed, forward_state_total = attend(
                forward_state_query, forward_cross_keys, forward_cross_values, True
            )
            forward_row_part = matmul(forward_token_mixed, forward_full_out)
            forward_state_part = matmul(forward_state_mixed, forward_full_state_out)
            row_sum, forward_state_sum = (
                lax.psum_scatter(
                    forward_row_part.astype(jnp.bfloat16), "tensor", scatter_dimension=1, tiled=True
                ).astype(jnp.float32),
                lax.psum_scatter(
                    forward_state_part.astype(jnp.bfloat16),
                    "tensor",
                    scatter_dimension=2,
                    tiled=True,
                ).astype(jnp.float32),
            )
            forward_forget = jax.nn.sigmoid(gate_pre)
            forward_kept.append(
                (
                    forward_full_normed,
                    forward_full_state,
                    forward_query,
                    forward_key,
                    forward_value,
                    forward_state_query,
                    forward_state_key,
                    forward_state_value,
                    forward_token_mixed,
                    forward_state_mixed,
                    forward_token_total,
                    forward_state_total,
                    forward_state,
                    forward_scaled,
                    forward_inverse,
                    forward_forget,
                    forward_state_sum,
                    forward_earlier_key,
                    forward_earlier_value,
                )
            )
            middle_block = forward_rows + row_sum
            middles.append(middle_block)
            forward_state = (
                forward_forget * forward_state + (1.0 - forward_forget) * forward_state_sum
            )
            forward_earlier_key, forward_earlier_value = (forward_key, forward_value)
        forward_middle = jnp.stack(middles, axis=1)
        mlp_in = normed_rows(forward_middle, forward_mlp_gain).astype(jnp.bfloat16)
        forward_full_mlp_in = lax.all_gather(mlp_in, "tensor", axis=2, tiled=True)
        forward_hidden, forward_active, mlp_partial = mlp_local(
            forward_full_mlp_in, forward_full_up, forward_full_down
        )
        mlp_sum = lax.psum_scatter(
            mlp_partial.astype(jnp.bfloat16), "tensor", scatter_dimension=2, tiled=True
        ).astype(jnp.float32)
        output = (forward_middle + mlp_sum).astype(jnp.bfloat16)
        output, saved = (
            output,
            (
                forward_kept,
                forward_middle,
                forward_full_mlp_in,
                forward_hidden,
                forward_active,
                forward_labels,
            ),
        )
        outputs.append(output)
        backward_weights = collect()
        rows_in = tokens_in[micro]
        grad_rows_out = cotangent[micro]
        (
            full_query,
            full_key,
            full_value,
            full_state_query,
            full_state_key,
            full_state_value,
            full_gate,
            full_up,
            full_init,
            full_out,
            full_state_out,
            full_down,
        ) = backward_weights[:12]
        backward_token_gain, backward_mlp_gain, backward_state_gain, backward_bias_columns = (
            unpack_gains(backward_weights)
        )
        kept, middle, full_mlp_in, hidden, active, labels = saved
        batch = rows_in.shape[0]
        full_grad = lax.all_gather(grad_rows_out, "tensor", axis=2, tiled=True)
        grad_down_w, grad_up_w, mlp_part = mlp_back_local(
            full_grad, active, hidden, full_mlp_in, full_down, full_up
        )
        grad_mlp_in = lax.psum_scatter(
            mlp_part.astype(jnp.bfloat16), "tensor", scatter_dimension=2, tiled=True
        ).astype(jnp.float32)
        unused_norm, mlp_norm_back = jax.vjp(normed_rows, middle, backward_mlp_gain)
        grad_middle_norm, grad_mlp_gain = mlp_norm_back(grad_mlp_in)
        grad_middle = grad_rows_out.astype(jnp.float32) + grad_middle_norm
        grad_state = jnp.zeros((batch, S, width_local), jnp.float32)
        carry_key = jnp.zeros((batch, W, width_local), jnp.float32)
        carry_value = jnp.zeros((batch, W, width_local), jnp.float32)
        square_zero = jnp.zeros((D, width_local), jnp.float32)
        grad_query_w = square_zero
        grad_key_w = square_zero
        grad_value_w = square_zero
        grad_state_query_w = square_zero
        grad_state_key_w = square_zero
        grad_state_value_w = square_zero
        grad_gate_w = square_zero
        grad_out_w = jnp.zeros((width_local, D), jnp.float32)
        grad_state_out_w = jnp.zeros((width_local, D), jnp.float32)
        grad_token_gain = jnp.zeros((D,), jnp.float32)
        grad_state_gain = jnp.zeros((width_local,), jnp.float32)
        grad_bias = jnp.zeros((width_local,), jnp.float32)
        grad_rows = [None] * NB
        for block in reversed(range(NB)):
            (
                full_normed,
                full_state,
                query,
                key,
                value,
                state_query,
                state_key,
                state_value,
                token_mixed,
                state_mixed,
                token_total,
                state_total,
                state,
                scaled,
                inverse,
                forget,
                state_sum,
                earlier_key,
                earlier_value,
            ) = kept[block]
            grad_row_block = grad_middle[:, block]
            grad_branch_state = ((1.0 - forget) * grad_state).astype(jnp.bfloat16)
            grad_gate = (grad_state * (state - state_sum) * forget * (1.0 - forget)).astype(
                jnp.bfloat16
            )
            carried_state = grad_state * forget
            full_grad_rows, full_grad_state = (
                lax.all_gather(grad_row_block.astype(jnp.bfloat16), "tensor", axis=1, tiled=True),
                lax.all_gather(grad_branch_state, "tensor", axis=2, tiled=True),
            )
            grad_out_w = grad_out_w + jnp.einsum(
                "bwc,bwd->cd", token_mixed, full_grad_rows, preferred_element_type=jnp.float32
            )
            grad_state_out_w = grad_state_out_w + jnp.einsum(
                "bsc,bsd->cd", state_mixed, full_grad_state, preferred_element_type=jnp.float32
            )
            grad_token_mixed = jnp.einsum(
                "bwd,cd->bwc", full_grad_rows, full_out, preferred_element_type=jnp.float32
            ).astype(jnp.bfloat16)
            grad_state_mixed = jnp.einsum(
                "bsd,cd->bsc", full_grad_state, full_state_out, preferred_element_type=jnp.float32
            ).astype(jnp.bfloat16)
            allowed = token_mask(labels, block)
            token_keys = jnp.concatenate([earlier_key, key, state_key], axis=1)
            token_values = jnp.concatenate([earlier_value, value, state_value], axis=1)
            cross_keys = jnp.concatenate([key, state_key], axis=1)
            cross_values = jnp.concatenate([value, state_value], axis=1)
            token_grad_query, token_grad_keys, token_grad_values = attend_back(
                query, token_keys, token_values, allowed, token_total, grad_token_mixed
            )
            state_grad_query, cross_grad_keys, cross_grad_values = attend_back(
                state_query, cross_keys, cross_values, True, state_total, grad_state_mixed
            )
            grad_key = (token_grad_keys[:, W : 2 * W] + cross_grad_keys[:, :W] + carry_key).astype(
                jnp.bfloat16
            )
            grad_value = (
                token_grad_values[:, W : 2 * W] + cross_grad_values[:, :W] + carry_value
            ).astype(jnp.bfloat16)
            carry_key = token_grad_keys[:, :W]
            carry_value = token_grad_values[:, :W]
            grad_state_key = (token_grad_keys[:, 2 * W :] + cross_grad_keys[:, W:]).astype(
                jnp.bfloat16
            )
            grad_state_value = (token_grad_values[:, 2 * W :] + cross_grad_values[:, W:]).astype(
                jnp.bfloat16
            )
            grad_query = token_grad_query.astype(jnp.bfloat16)
            grad_state_query = state_grad_query.astype(jnp.bfloat16)
            grad_query_w = grad_query_w + jnp.einsum(
                "bwd,bwc->dc", full_normed, grad_query, preferred_element_type=jnp.float32
            )
            grad_key_w = grad_key_w + jnp.einsum(
                "bwd,bwc->dc", full_normed, grad_key, preferred_element_type=jnp.float32
            )
            grad_value_w = grad_value_w + jnp.einsum(
                "bwd,bwc->dc", full_normed, grad_value, preferred_element_type=jnp.float32
            )
            grad_state_query_w = grad_state_query_w + jnp.einsum(
                "bsd,bsc->dc", full_state, grad_state_query, preferred_element_type=jnp.float32
            )
            grad_state_key_w = grad_state_key_w + jnp.einsum(
                "bsd,bsc->dc", full_state, grad_state_key, preferred_element_type=jnp.float32
            )
            grad_state_value_w = grad_state_value_w + jnp.einsum(
                "bsd,bsc->dc", full_state, grad_state_value, preferred_element_type=jnp.float32
            )
            grad_gate_w = grad_gate_w + jnp.einsum(
                "bsd,bsc->dc", full_state, grad_gate, preferred_element_type=jnp.float32
            )
            grad_bias = grad_bias + jnp.sum(grad_gate.astype(jnp.float32), axis=(0, 1))
            row_part = jnp.einsum(
                "bwc,dc->bwd", grad_query, full_query, preferred_element_type=jnp.float32
            )
            row_part = row_part + jnp.einsum(
                "bwc,dc->bwd", grad_key, full_key, preferred_element_type=jnp.float32
            )
            row_part = row_part + jnp.einsum(
                "bwc,dc->bwd", grad_value, full_value, preferred_element_type=jnp.float32
            )
            state_part = jnp.einsum(
                "bsc,dc->bsd",
                grad_state_query,
                full_state_query,
                preferred_element_type=jnp.float32,
            )
            state_part = state_part + jnp.einsum(
                "bsc,dc->bsd", grad_state_key, full_state_key, preferred_element_type=jnp.float32
            )
            state_part = state_part + jnp.einsum(
                "bsc,dc->bsd",
                grad_state_value,
                full_state_value,
                preferred_element_type=jnp.float32,
            )
            state_part = state_part + jnp.einsum(
                "bsc,dc->bsd", grad_gate, full_gate, preferred_element_type=jnp.float32
            )
            grad_normed, grad_state_normed = (
                lax.psum_scatter(
                    row_part.astype(jnp.bfloat16), "tensor", scatter_dimension=1, tiled=True
                ).astype(jnp.float32),
                lax.psum_scatter(
                    state_part.astype(jnp.bfloat16), "tensor", scatter_dimension=2, tiled=True
                ).astype(jnp.float32),
            )
            rows = rows_in[:, block].astype(jnp.float32)
            unused_rows, token_norm_back = jax.vjp(normed_rows, rows, backward_token_gain)
            grad_rows_norm, grad_gain_part = token_norm_back(grad_normed)
            grad_token_gain = grad_token_gain + grad_gain_part
            grad_rows[block] = (grad_row_block + grad_rows_norm).astype(jnp.bfloat16)
            grad_scaled = grad_state_normed * backward_state_gain
            grad_state_gain = grad_state_gain + jnp.sum(grad_state_normed * scaled, axis=(0, 1))
            dot_sum = lax.psum(jnp.sum(grad_scaled * scaled, axis=-1), "tensor")
            grad_state = carried_state + inverse * (grad_scaled - scaled * (dot_sum / D)[..., None])
        grad_init = jnp.sum(grad_state, axis=0)
        state_gain_full = lax.dynamic_update_slice_in_dim(
            jnp.zeros((D,), jnp.float32), grad_state_gain, column_start, 0
        )
        bias_full = lax.dynamic_update_slice_in_dim(
            jnp.zeros((D,), jnp.float32), grad_bias, column_start, 0
        )
        grads = (
            grad_query_w,
            grad_key_w,
            grad_value_w,
            grad_state_query_w,
            grad_state_key_w,
            grad_state_value_w,
            grad_gate_w,
            grad_up_w,
            grad_init,
            grad_out_w,
            grad_state_out_w,
            grad_down_w,
            grad_token_gain,
            grad_mlp_gain,
            state_gain_full,
            bias_full,
        )
        grads, grad_in = (grads, jnp.stack(grad_rows, axis=1))
        input_grads.append(grad_in)
        if totals is None:
            totals = grads
        else:
            totals = tuple((first + second for first, second in zip(totals, grads)))
    reduced = (
        lax.psum_scatter(
            totals[0].astype(jnp.bfloat16), "dp", scatter_dimension=0, tiled=True
        ).astype(jnp.float32),
        lax.psum_scatter(
            totals[1].astype(jnp.bfloat16), "dp", scatter_dimension=0, tiled=True
        ).astype(jnp.float32),
        lax.psum_scatter(
            totals[2].astype(jnp.bfloat16), "dp", scatter_dimension=0, tiled=True
        ).astype(jnp.float32),
        lax.psum_scatter(
            totals[3].astype(jnp.bfloat16), "dp", scatter_dimension=0, tiled=True
        ).astype(jnp.float32),
        lax.psum_scatter(
            totals[4].astype(jnp.bfloat16), "dp", scatter_dimension=0, tiled=True
        ).astype(jnp.float32),
        lax.psum_scatter(
            totals[5].astype(jnp.bfloat16), "dp", scatter_dimension=0, tiled=True
        ).astype(jnp.float32),
        lax.psum_scatter(
            totals[6].astype(jnp.bfloat16), "dp", scatter_dimension=0, tiled=True
        ).astype(jnp.float32),
        lax.psum_scatter(
            totals[7].astype(jnp.bfloat16), "dp", scatter_dimension=0, tiled=True
        ).astype(jnp.float32),
        lax.psum_scatter(
            totals[8].astype(jnp.bfloat16), "dp", scatter_dimension=0, tiled=True
        ).astype(jnp.float32),
        lax.psum_scatter(
            totals[9].astype(jnp.bfloat16), "dp", scatter_dimension=1, tiled=True
        ).astype(jnp.float32),
        lax.psum_scatter(
            totals[10].astype(jnp.bfloat16), "dp", scatter_dimension=1, tiled=True
        ).astype(jnp.float32),
        lax.psum_scatter(
            totals[11].astype(jnp.bfloat16), "dp", scatter_dimension=1, tiled=True
        ).astype(jnp.float32),
        lax.psum_scatter(
            totals[12].astype(jnp.bfloat16), "dp", scatter_dimension=0, tiled=True
        ).astype(jnp.float32),
        lax.psum_scatter(
            totals[13].astype(jnp.bfloat16), "dp", scatter_dimension=0, tiled=True
        ).astype(jnp.float32),
        lax.psum_scatter(
            totals[14].astype(jnp.bfloat16), "dp", scatter_dimension=0, tiled=True
        ).astype(jnp.float32),
        lax.psum_scatter(
            totals[15].astype(jnp.bfloat16), "dp", scatter_dimension=0, tiled=True
        ).astype(jnp.float32),
    )
    gain_totals = lax.psum((reduced[12], reduced[13], reduced[14], reduced[15]), "tensor")
    return (
        jnp.stack(outputs, axis=0),
        jnp.stack(input_grads, axis=0),
        gain_totals[0],
        gain_totals[1],
        gain_totals[2],
        gain_totals[3],
        reduced[0],
        reduced[1],
        reduced[2],
        reduced[9],
        reduced[3],
        reduced[4],
        reduced[5],
        reduced[10],
        reduced[6],
        reduced[7],
        reduced[11],
        reduced[8],
    )


BF = jnp.bfloat16
F32 = jnp.float32
HALF = 256
VMEM_BYTES = 60 * 1024 * 1024
EXP2_SCALE = math.log2(math.e) / math.sqrt(HEAD)
SCORE_SCALE = 1.0 / math.sqrt(HEAD)


def nn(left, right):
    return lax.dot_general(left, right, (((1,), (0,)), ((), ())), preferred_element_type=F32)


def nt(left, right):
    return lax.dot_general(left, right, (((1,), (1,)), ((), ())), preferred_element_type=F32)


def tn(left, right):
    return lax.dot_general(left, right, (((0,), (0,)), ((), ())), preferred_element_type=F32)


def inverse_rms(values):
    return lax.rsqrt(jnp.mean(values * values, axis=-1, keepdims=True) + epsilon)


def rms_back(scaled, inverse, grad):
    return (grad - scaled * jnp.mean(grad * scaled, axis=-1, keepdims=True)) * inverse


def params(semantics=("arbitrary",)):
    return pltpu.CompilerParams(dimension_semantics=semantics, vmem_limit_bytes=VMEM_BYTES)


def cost(flops, moved, transcendentals=0):
    return pl.CostEstimate(
        flops=int(flops), bytes_accessed=int(moved), transcendentals=int(transcendentals)
    )


def once(shape, index):
    return pl.BlockSpec(shape, index, pipeline_mode=pl.Buffered(1))


def project_kernel(rows, gain, w0, w1, turned, query, key, value):
    width = w0.shape[1] // 3
    wide = rows[...].astype(F32)
    normed = (wide * inverse_rms(wide) * gain[...]).astype(BF)
    turned[...] = normed.T
    for half, weight in enumerate((w0, w1)):
        for which, out in enumerate((query, key, value)):
            out[:, half * width : (half + 1) * width] = nn(
                normed, weight[:, which * width : (which + 1) * width]
            ).astype(BF)


def project(rows, gain, weights):
    tokens = rows.shape[0]
    width = 3 * D // 2
    out = jax.ShapeDtypeStruct((tokens, D), BF)
    block = pl.BlockSpec((W, D), lambda b: (b, 0))
    return pl.pallas_call(
        project_kernel,
        grid=(tokens // W,),
        in_specs=[
            block,
            once((1, D), lambda b: (0, 0)),
            once((D, width), lambda b: (0, 0)),
            once((D, width), lambda b: (1, 0)),
        ],
        out_specs=[pl.BlockSpec((D, W), lambda b: (0, b))] + [block] * 3,
        out_shape=[jax.ShapeDtypeStruct((D, tokens), BF)] + [out] * 3,
        compiler_params=params(),
        cost_estimate=cost(2 * tokens * D * 3 * D, 2 * (5 * tokens * D + 3 * D * D)),
        name="project",
    )(rows, gain, weights, weights)


def softmax_parts(parts):
    top = parts[0][0].max(axis=1, keepdims=True)
    for scores, unused in parts[1:]:
        top = jnp.maximum(top, scores.max(axis=1, keepdims=True))
    mixed = None
    for scores, values in parts:
        weights = jnp.exp2((scores - top) * EXP2_SCALE)
        wide_values = jnp.concatenate([values, jnp.ones_like(values)], axis=1)
        part_mixed = nn(weights.astype(BF), wide_values)
        mixed = part_mixed if mixed is None else mixed + part_mixed
    total = mixed[:, HEAD:]
    return (mixed[:, :HEAD] / total).astype(BF), top * EXP2_SCALE + jnp.log2(total)


def forward_kernel(
    flags,
    query,
    key,
    value,
    key_before,
    value_before,
    init,
    gain,
    bias,
    query0,
    query1,
    key0,
    key1,
    second0,
    second1,
    token_mixed,
    state_mixed,
    turned,
    state_query,
    state_key,
    state_value,
    state_in,
    forget,
    apart,
    totals,
    state,
    token_totals,
    state_totals,
):
    block = pl.program_id(0)
    width = query0.shape[1]

    @pl.when(block == 0)
    def start():
        state[...] = init[...].astype(F32)

    now = state[...]
    state_in[...] = now
    state_normed = (now * inverse_rms(now) * gain[...]).astype(BF)
    turned[...] = state_normed.T
    for half, (one, other, two) in enumerate(((query0, key0, second0), (query1, key1, second1))):
        columns = slice(half * width, (half + 1) * width)
        state_query[:, columns] = nn(state_normed, one[...]).astype(BF)
        state_key[:, columns] = nn(state_normed, other[...]).astype(BF)
        state_value[:, columns] = nn(state_normed, two[:, :width]).astype(BF)
        gate = nn(state_normed, two[:, width : 2 * width]) + bias[:, columns]
        forget[:, columns] = jax.nn.sigmoid(gate)

    def heads(with_before):
        def head(index, carry):
            columns = pl.ds(pl.multiple_of(index * HEAD, HEAD), HEAD)
            lane = lax.broadcasted_iota(jnp.int32, (W, HEAD), 1) == index
            row = lax.broadcasted_iota(jnp.int32, (W, W), 0)
            column = lax.broadcasted_iota(jnp.int32, (W, W), 1)
            lead = jnp.where(row < HALF, flags[2 * block] * (HALF - 1 - row), flags[2 * block + 1] * (W - 1 - row))
            reach = column <= row + lead
            own = query[:, columns]
            parts = []
            if with_before:
                parts.append((nt(own, key_before[:, columns]), value_before[:, columns]))
            near = jnp.where(reach, nt(own, key[:, columns]), masked_score)
            parts.append((near, value[:, columns]))
            parts.append((nt(own, state_key[:, columns]), state_value[:, columns]))
            mixed, total = softmax_parts(parts)
            token_mixed[:, columns] = mixed
            token_totals[...] = jnp.where(lane, total, token_totals[...])
            own = state_query[:, columns]
            mixed, total = softmax_parts(
                [
                    (nt(own, key[:, columns]), value[:, columns]),
                    (nt(own, state_key[:, columns]), state_value[:, columns]),
                ]
            )
            state_mixed[:, columns] = mixed
            state_totals[...] = jnp.where(lane, total, state_totals[...])
            return carry

        lax.fori_loop(0, D // HEAD, head, 0, unroll=2)

    @pl.when(block == 0)
    def first():
        heads(False)

    @pl.when(block > 0)
    def later():
        heads(True)

    count = D // HEAD
    totals[0, :count, :] = token_totals[...].T[:count]
    totals[0, count:, :] = state_totals[...].T[:count]
    new = nt(state_mixed[:, :width], second0[:, 2 * width :]) + nt(
        state_mixed[:, width:], second1[:, 2 * width :]
    )
    apart[...] = (now - new).astype(BF)
    state[...] = new + forget[...] * (now - new)


def forward(flags, query, key, value, init, gain, bias, weights, more_weights):
    blocks = query.shape[0] // W
    heads = D // HEAD
    own = pl.BlockSpec((W, D), lambda b, s: (b, 0))
    before = pl.BlockSpec((W, D), lambda b, s: (jnp.maximum(b - 1, 0), 0))
    low = jax.ShapeDtypeStruct((blocks * W, D), BF)
    wide = jax.ShapeDtypeStruct((blocks * W, D), F32)
    return pl.pallas_call(
        forward_kernel,
        grid_spec=pltpu.PrefetchScalarGridSpec(
            num_scalar_prefetch=1,
            grid=(blocks,),
            in_specs=[
                own,
                own,
                own,
                before,
                before,
                once((S, D), lambda b, s: (0, 0)),
                once((1, D), lambda b, s: (0, 0)),
                once((1, D), lambda b, s: (0, 0)),
                once((D, D // 2), lambda b, s: (0, 3)),
                once((D, D // 2), lambda b, s: (1, 3)),
                once((D, D // 2), lambda b, s: (0, 4)),
                once((D, D // 2), lambda b, s: (1, 4)),
                once((D, more_weights.shape[1]), lambda b, s: (0, 0)),
                once((D, more_weights.shape[1]), lambda b, s: (1, 0)),
            ],
            out_specs=[own] * 2
            + [pl.BlockSpec((D, S), lambda b, s: (0, b))]
            + [own] * 6
            + [pl.BlockSpec((1, 2 * heads, W), lambda b, s: (b, 0, 0))],
            scratch_shapes=[
                pltpu.VMEM((S, D), F32),
                pltpu.VMEM((W, HEAD), F32),
                pltpu.VMEM((S, HEAD), F32),
            ],
        ),
        out_shape=[low] * 2
        + [jax.ShapeDtypeStruct((D, blocks * S), BF)]
        + [low] * 3
        + [wide, wide, low, jax.ShapeDtypeStruct((blocks, 2 * heads, W), F32)],
        compiler_params=params(),
        cost_estimate=cost(42e9, 100e6, 40e6),
        name="forward",
    )(
        flags,
        query,
        key,
        value,
        key,
        value,
        init,
        gain,
        bias,
        weights,
        weights,
        weights,
        weights,
        more_weights,
        more_weights,
    )


def middle_kernel(rows, mixed, w0, w1, gain, cotangent, middle, mlp_in, mlp_turned, cot_turned):
    width = w0.shape[1]
    here = (
        rows[...].astype(F32) + nt(mixed[:, :width], w0[...]) + nt(mixed[:, width:], w1[...])
    )
    middle[...] = here.astype(BF)
    low = (here * inverse_rms(here) * gain[...]).astype(BF)
    mlp_in[...] = low
    mlp_turned[...] = low.T
    cot_turned[...] = cotangent[...].T


def middle_rows(rows, mixed, weights, gain, cotangent):
    tokens = rows.shape[0]
    width = D // 2
    last = weights.shape[1] // width - 1
    block = pl.BlockSpec((W, D), lambda b: (b, 0))
    turned = pl.BlockSpec((D, W), lambda b: (0, b))
    low = jax.ShapeDtypeStruct((tokens, D), BF)
    return pl.pallas_call(
        middle_kernel,
        grid=(tokens // W,),
        in_specs=[
            block,
            block,
            once((D, width), lambda b: (0, last)),
            once((D, width), lambda b: (1, last)),
            once((1, D), lambda b: (0, 0)),
            block,
        ],
        out_specs=[block, block, turned, turned],
        out_shape=[
            low,
            low,
            jax.ShapeDtypeStruct((D, tokens), BF),
            jax.ShapeDtypeStruct((D, tokens), BF),
        ],
        compiler_params=params(),
        cost_estimate=cost(2 * tokens * D * D, 2 * 8 * tokens * D),
        name="middle",
    )(rows, mixed, weights, weights, gain, cotangent)


def mlp_kernel(
    mlp_in, mlp_turned, cot, cot_turned, weights, out, grad_in, grads, out_sum, grad_sum, act, gh
):
    step = pl.program_id(0)
    units = weights.shape[1] // 2
    tokens = mlp_in.shape[0]

    @pl.when(step == 0)
    def start():
        out_sum[...] = jnp.zeros_like(out_sum)
        grad_sum[...] = jnp.zeros_like(grad_sum)

    slope = math.sqrt(2.0 / math.pi)

    def chunk(index, carry):
        rows = pl.ds(pl.multiple_of(index * W, W), W)
        hidden = nn(mlp_in[rows, :], weights[:, :units])
        back = nn(cot[rows, :], weights[:, units:])
        square = hidden * hidden
        bent = jnp.tanh(slope * hidden * (1.0 + 0.044715 * square))
        open_part = 0.5 * (1.0 + bent)
        active = (hidden * open_part).astype(BF)
        steep = open_part + (0.5 * slope) * hidden * (1.0 - bent * bent) * (
            1.0 + (3 * 0.044715) * square
        )
        grad = (steep * back).astype(BF)
        act[rows, :] = active
        gh[rows, :] = grad
        out_sum[rows, :] += nt(active, weights[:, units:])
        grad_sum[rows, :] += nt(grad, weights[:, :units])
        return carry

    lax.fori_loop(0, tokens // W, chunk, 0)
    grads[:, :units] = nn(mlp_turned[...], gh[...]).astype(BF)
    grads[:, units:] = nn(cot_turned[...], act[...]).astype(BF)

    @pl.when(step == pl.num_programs(0) - 1)
    def end():
        out[...] = out_sum[...].astype(BF)
        grad_in[...] = grad_sum[...].astype(BF)


def mlp(mlp_in, mlp_turned, cot, cot_turned, weights):
    tokens = mlp_in.shape[0]
    units = 512
    across = (weights.shape[1] - D // 2) // (2 * units)
    low = jax.ShapeDtypeStruct((tokens, D), BF)
    rows = once((tokens, D), lambda f: (0, 0))
    turned = once((D, tokens), lambda f: (0, 0))
    tile = pl.BlockSpec((D, 2 * units), lambda f: (f // across, f % across))
    return pl.pallas_call(
        mlp_kernel,
        grid=(2 * across,),
        in_specs=[rows, turned, rows, turned, tile],
        out_specs=[rows, rows, tile],
        out_shape=[low, low, jax.ShapeDtypeStruct(weights.shape, BF)],
        scratch_shapes=[
            pltpu.VMEM((tokens, D), F32),
            pltpu.VMEM((tokens, D), F32),
            pltpu.VMEM((tokens, units), BF),
            pltpu.VMEM((tokens, units), BF),
        ],
        compiler_params=params(),
        cost_estimate=cost(103e9, 60e6, 8e6),
        name="mlp",
    )(mlp_in, mlp_turned, cot, cot_turned, weights)


def after_mlp_kernel(
    middle, mlp_out, grad_in, cot, gain, w0, w1, output, grad_middle, turned, grad_mixed, grad_gain
):
    width = w0.shape[1]
    here = middle[...].astype(F32)
    inverse = inverse_rms(here)
    scaled = here * inverse
    grad = grad_in[...].astype(F32)
    output[...] = (here + mlp_out[...].astype(F32)).astype(BF)
    low = (cot[...].astype(F32) + rms_back(scaled, inverse, gain[...] * grad)).astype(BF)
    grad_middle[...] = low
    turned[...] = low.T
    grad_mixed[:, :width] = nn(low, w0[...]).astype(BF)
    grad_mixed[:, width:] = nn(low, w1[...]).astype(BF)
    part = jnp.sum(grad * scaled, axis=0, keepdims=True)

    @pl.when(pl.program_id(0) == 0)
    def first():
        grad_gain[...] = part

    @pl.when(pl.program_id(0) > 0)
    def later():
        grad_gain[...] += part


def after_mlp(middle, mlp_out, grad_in, cot, gain, weights):
    tokens = middle.shape[0]
    width = D // 2
    last = weights.shape[1] // width - 1
    block = pl.BlockSpec((W, D), lambda b: (b, 0))
    low = jax.ShapeDtypeStruct((tokens, D), BF)
    return pl.pallas_call(
        after_mlp_kernel,
        grid=(tokens // W,),
        in_specs=[
            block,
            block,
            block,
            block,
            once((1, D), lambda b: (0, 0)),
            once((D, width), lambda b: (0, last)),
            once((D, width), lambda b: (1, last)),
        ],
        out_specs=[
            block,
            block,
            pl.BlockSpec((D, W), lambda b: (0, b)),
            block,
            pl.BlockSpec((1, D), lambda b: (0, 0)),
        ],
        out_shape=[
            low,
            low,
            jax.ShapeDtypeStruct((D, tokens), BF),
            low,
            jax.ShapeDtypeStruct((1, D), F32),
        ],
        compiler_params=params(),
        cost_estimate=cost(2 * tokens * D * D, 2 * 8 * tokens * D),
        name="after_mlp",
    )(middle, mlp_out, grad_in, cot, gain, weights, weights)


def backward_kernel(
    flags,
    query,
    key,
    value,
    key_before,
    value_before,
    state_query,
    state_key,
    state_value,
    token_mixed,
    state_mixed,
    grad_mixed,
    totals,
    forget,
    state_in,
    apart,
    gain,
    weight_query,
    weight_key,
    more_weight,
    wso0,
    wso1,
    grad_tokens,
    grad_states,
    branch,
    grad_init,
    grad_gain,
    grad_bias,
    grad_state,
    grad_state_mixed,
    grad_normed,
    gate_part,
    carry_key,
    carry_value,
):
    step = pl.program_id(0)
    half = pl.program_id(1)
    block = pl.num_programs(0) - 1 - step
    width = wso0.shape[1]
    local = width // HEAD
    count = D // HEAD

    @pl.when((step == 0) & (half == 0))
    def start():
        grad_state[...] = jnp.zeros_like(grad_state)
        carry_key[...] = jnp.zeros_like(carry_key)
        carry_value[...] = jnp.zeros_like(carry_value)
        grad_gain[...] = jnp.zeros_like(grad_gain)
        grad_bias[...] = jnp.zeros_like(grad_bias)

    @pl.when(half == 0)
    def begin():
        coming = grad_state[...]
        keep = forget[...]
        low = ((1.0 - keep) * coming).astype(BF)
        branch[...] = low.T
        gate = (coming * apart[...].astype(F32) * keep * (1.0 - keep)).astype(BF)
        gate_part[0] = gate[:, :width]
        gate_part[1] = gate[:, width:]
        grad_bias[...] += jnp.sum(gate.astype(F32), axis=0, keepdims=True)
        grad_state_mixed[0] = nn(low, wso0[...]).astype(BF)
        grad_state_mixed[1] = nn(low, wso1[...]).astype(BF)
        grad_normed[...] = jnp.zeros_like(grad_normed)

    grad_states[3] = gate_part[half]

    def heads(with_before):
        def head(index, carry):
            columns = pl.ds(pl.multiple_of(index * HEAD, HEAD), HEAD)
            at = half * local + index
            queries = jnp.concatenate([query[:, columns], state_query[:, columns]], axis=0)
            grads_out = jnp.concatenate(
                [grad_mixed[:, columns], grad_state_mixed[half, :, columns]], axis=0
            )
            mixed = jnp.concatenate([token_mixed[:, columns], state_mixed[:, columns]], axis=0)
            product = grads_out.astype(F32) * mixed.astype(F32)
            delta = jnp.sum(product.T, axis=0, keepdims=True)
            token_total = totals[0, pl.ds(at, 1), :]
            state_total = totals[0, pl.ds(count + at, 1), :]
            total = jnp.concatenate([token_total, state_total], axis=1)

            def chunk(keys, values, first, last, mask):
                some = queries[first:last]
                some_grads = grads_out[first:last]
                scores = nt(keys, some)
                if mask is not None:
                    size = mask.shape[1]
                    scores = jnp.concatenate(
                        [jnp.where(mask, scores[:, :size], masked_score), scores[:, size:]], axis=1
                    )
                weights = jnp.exp2(scores * EXP2_SCALE - total[:, first:last])
                back = nt(values, some_grads) - delta[:, first:last]
                grad_scores = (weights * back).astype(BF)
                grad_values = nn(weights.astype(BF), some_grads)
                grad_keys = nn(grad_scores, some)
                return grad_keys * SCORE_SCALE, grad_values, tn(keys, grad_scores)

            turned = None
            for first in range(0, S, HALF):
                rows = slice(first, first + HALF)
                grad_keys, grad_values, part = chunk(
                    state_key[rows, columns], state_value[rows, columns], 0, W + S, None
                )
                grad_states[1, rows, columns] = grad_keys.astype(BF)
                grad_states[2, rows, columns] = grad_values.astype(BF)
                turned = part if turned is None else turned + part
            for part in range(2):
                rows = slice(part * HALF, (part + 1) * HALF)
                row = lax.broadcasted_iota(jnp.int32, (HALF, HALF), 0)
                column = lax.broadcasted_iota(jnp.int32, (HALF, HALF), 1)
                mask = row <= column + flags[2 * block + part] * HALF
                grad_keys, grad_values, more = chunk(
                    key[rows, columns], value[rows, columns], part * HALF, W + S, mask
                )
                grad_tokens[1, rows, columns] = (grad_keys + carry_key[half, rows, columns]).astype(
                    BF
                )
                grad_tokens[2, rows, columns] = (
                    grad_values + carry_value[half, rows, columns]
                ).astype(BF)
                if part:
                    more = jnp.concatenate([jnp.zeros((HEAD, HALF), F32), more], axis=1)
                turned = turned + more
            turned_tokens = turned[:, :W]
            if with_before:
                for first in range(0, W, HALF):
                    rows = slice(first, first + HALF)
                    grad_keys, grad_values, part = chunk(
                        key_before[rows, columns], value_before[rows, columns], 0, W, None
                    )
                    carry_key[half, rows, columns] = grad_keys
                    carry_value[half, rows, columns] = grad_values
                    turned_tokens = turned_tokens + part
            grad_tokens[0, :, columns] = (turned_tokens * SCORE_SCALE).T.astype(BF)
            grad_states[0, :, columns] = (turned[:, W:] * SCORE_SCALE).T.astype(BF)
            return carry

        lax.fori_loop(0, local, head, 0, unroll=2)

    @pl.when(block > 0)
    def later():
        heads(True)

    @pl.when(block == 0)
    def first():
        heads(False)

    grad_normed[...] += (
        nt(grad_states[0], weight_query[...])
        + nt(grad_states[1], weight_key[...])
        + nt(grad_states[2], more_weight[:, :width])
        + nt(grad_states[3], more_weight[:, width:])
    )

    @pl.when(half == 1)
    def finish():
        here = state_in[...]
        inverse = inverse_rms(here)
        scaled = here * inverse
        grad = grad_normed[...]
        grad_gain[...] += jnp.sum(grad * scaled, axis=0, keepdims=True)
        grad_state[...] = forget[...] * grad_state[...] + rms_back(
            scaled, inverse, gain[...] * grad
        )

    @pl.when((half == 1) & (block == 0))
    def end():
        grad_init[...] = grad_state[...].astype(BF)


def backward(
    flags,
    query,
    key,
    value,
    state_query,
    state_key,
    state_value,
    token_mixed,
    state_mixed,
    grad_mixed,
    totals,
    forget,
    state_in,
    apart,
    gain,
    weights,
    more_weights,
):
    blocks = query.shape[0] // W
    heads = D // HEAD
    half_width = D // 2

    def rev(b):
        return blocks - 1 - b

    own = pl.BlockSpec((W, half_width), lambda b, t, s: (rev(b), t))
    before = pl.BlockSpec((W, half_width), lambda b, t, s: (jnp.maximum(rev(b) - 1, 0), t))
    whole = pl.BlockSpec((S, D), lambda b, t, s: (rev(b), 0))
    fixed_row = pl.BlockSpec((1, D), lambda b, t, s: (0, 0))
    return pl.pallas_call(
        backward_kernel,
        grid_spec=pltpu.PrefetchScalarGridSpec(
            num_scalar_prefetch=1,
            grid=(blocks, 2),
            in_specs=[own, own, own, before, before]
            + [own] * 6
            + [pl.BlockSpec((1, 2 * heads, W), lambda b, t, s: (rev(b), 0, 0))]
            + [whole] * 3
            + [
                once((1, D), lambda b, t, s: (0, 0)),
                pl.BlockSpec((D, half_width), lambda b, t, s: (t, 3)),
                pl.BlockSpec((D, half_width), lambda b, t, s: (t, 4)),
                pl.BlockSpec((D, 2 * half_width), lambda b, t, s: (t, 0)),
                once((D, half_width), lambda b, t, s: (0, 2)),
                once((D, half_width), lambda b, t, s: (1, 2)),
            ],
            out_specs=[
                pl.BlockSpec((3, W, half_width), lambda b, t, s: (0, rev(b), t)),
                pl.BlockSpec((4, S, half_width), lambda b, t, s: (0, rev(b), t)),
                pl.BlockSpec((D, S), lambda b, t, s: (0, rev(b))),
                pl.BlockSpec((S, D), lambda b, t, s: (0, 0)),
                fixed_row,
                fixed_row,
            ],
            scratch_shapes=[
                pltpu.VMEM((S, D), F32),
                pltpu.VMEM((2, S, half_width), BF),
                pltpu.VMEM((S, D), F32),
                pltpu.VMEM((2, S, half_width), BF),
                pltpu.VMEM((2, W, half_width), F32),
                pltpu.VMEM((2, W, half_width), F32),
            ],
        ),
        out_shape=[
            jax.ShapeDtypeStruct((3, blocks * W, D), BF),
            jax.ShapeDtypeStruct((4, blocks * W, D), BF),
            jax.ShapeDtypeStruct((D, blocks * W), BF),
            jax.ShapeDtypeStruct((S, D), BF),
            jax.ShapeDtypeStruct((1, D), F32),
            jax.ShapeDtypeStruct((1, D), F32),
        ],
        compiler_params=params(("arbitrary", "arbitrary")),
        cost_estimate=cost(70e9, 100e6, 40e6),
        name="backward",
    )(
        flags,
        query,
        key,
        value,
        key,
        value,
        state_query,
        state_key,
        state_value,
        token_mixed,
        state_mixed,
        grad_mixed,
        totals,
        forget,
        state_in,
        apart,
        gain,
        weights,
        weights,
        more_weights,
        more_weights,
        more_weights,
    )


def whole_grad_kernel(turned, right, into, out):
    out[...] = nn(turned[...], right[...]).astype(BF)


def whole_weight_grad(turned, right, into):
    tokens = right.shape[0]
    width = D // 2
    last = into.shape[1] // width - 1
    return pl.pallas_call(
        whole_grad_kernel,
        grid=(2,),
        in_specs=[
            once((D, tokens), lambda g: (0, 0)),
            pl.BlockSpec((tokens, width), lambda g: (0, g)),
            pl.BlockSpec(memory_space=pl.ANY),
        ],
        out_specs=pl.BlockSpec((D, width), lambda g: (g, last)),
        out_shape=jax.ShapeDtypeStruct(into.shape, BF),
        input_output_aliases={2: 0},
        compiler_params=params(),
        cost_estimate=cost(2 * tokens * D * D, 2 * (tokens * D + 2 * D * D)),
        name="whole_weight_grad",
    )(turned, right, into)


def weight_grad_kernel(groups, core, turned, right, *rest):
    keep, send = rest[-2:]
    grads = nn(turned[...], right[0]).astype(BF)
    group = turned.shape[0] // groups
    grads = grads.reshape(groups // 2, 2, group, grads.shape[1])
    shape = keep.shape
    low = grads[:, 0].reshape(shape)
    high = grads[:, 1].reshape(shape)
    mine = core[0] == 0
    keep[...] = jnp.where(mine, low, high)
    send[...] = jnp.where(mine, high, low)


def weight_grads(dp, core, turned, rights, first=0, many=1, across=0, at=0, into=None):
    tokens = rights.shape[1]
    width = D // 2
    across = across or many
    out = jax.ShapeDtypeStruct((D, across * width), BF)
    tile = pl.BlockSpec((D // 2, width), lambda g, s: (g % 2, at + g // 2))
    into = into or ()
    return pl.pallas_call(
        functools.partial(weight_grad_kernel, dp),
        grid_spec=pltpu.PrefetchScalarGridSpec(
            num_scalar_prefetch=1,
            grid=(2 * many,),
            in_specs=[
                once((D, tokens), lambda g, s: (0, 0)),
                pl.BlockSpec((1, tokens, width), lambda g, s: (first + g // 2, 0, g % 2)),
            ]
            + [pl.BlockSpec(memory_space=pl.ANY)] * len(into),
            out_specs=[tile, tile],
        ),
        out_shape=[out, out],
        input_output_aliases={3 + i: i for i in range(len(into))},
        compiler_params=params(),
        cost_estimate=cost(2 * tokens * D * D * many, 2 * (tokens * D + 2 * many * D * D)),
        name="weight_grads",
    )(core, turned, rights, *into)


def token_grad_kernel(grads, w0, w1, rows, grad_middle, gain, out, grad_gain):
    width = w0.shape[1] // 3
    total = None
    for which in range(3):
        for half, weight in enumerate((w0, w1)):
            part = nt(
                grads[which, :, half * width : (half + 1) * width],
                weight[:, which * width : (which + 1) * width],
            )
            total = part if total is None else total + part
    here = rows[...].astype(F32)
    inverse = inverse_rms(here)
    scaled = here * inverse
    out[...] = (
        grad_middle[...].astype(F32) + rms_back(scaled, inverse, gain[...] * total)
    ).astype(BF)
    part = jnp.sum(total * scaled, axis=0, keepdims=True)

    @pl.when(pl.program_id(0) == 0)
    def first():
        grad_gain[...] = part

    @pl.when(pl.program_id(0) > 0)
    def later():
        grad_gain[...] += part


def token_grad(grads, weights, rows, grad_middle, gain):
    tokens = rows.shape[0]
    width = 3 * D // 2
    block = pl.BlockSpec((W, D), lambda b: (b, 0))
    return pl.pallas_call(
        token_grad_kernel,
        grid=(tokens // W,),
        in_specs=[
            pl.BlockSpec((3, W, D), lambda b: (0, b, 0)),
            once((D, width), lambda b: (0, 0)),
            once((D, width), lambda b: (1, 0)),
            block,
            block,
            once((1, D), lambda b: (0, 0)),
        ],
        out_specs=[block, pl.BlockSpec((1, D), lambda b: (0, 0))],
        out_shape=[jax.ShapeDtypeStruct((tokens, D), BF), jax.ShapeDtypeStruct((1, D), F32)],
        compiler_params=params(),
        cost_estimate=cost(2 * tokens * 3 * D * D, 2 * 6 * tokens * D),
        name="token_grad",
    )(grads, weights, weights, rows, grad_middle, gain)


def gather(local):
    return lax.all_gather(local, ("tensor", "dp"), axis=0, tiled=True)


def scatter(total):
    return lax.psum_scatter(total, ("tensor", "dp"), scatter_dimension=0, tiled=True)


def axes_of(dp):
    return ["tensor"] + list(reversed(range(dp.bit_length() - 1)))


def side_of(axis):
    if axis == "tensor":
        return lax.axis_index("tensor")
    return (lax.axis_index("dp") >> axis) & 1


def trade(values, axis, dp):
    if axis == "tensor":
        return lax.ppermute(values, "tensor", [(0, 1), (1, 0)])
    return lax.ppermute(values, "dp", [(i, i ^ (1 << axis)) for i in range(dp)])


def order_of(dp, turn):
    bits = dp.bit_length() - 1
    middle = ["tensor"] + ([1] if bits > 1 else [])
    if turn:
        middle = middle[::-1]
    return ([0] if bits else []) + middle + list(range(2, bits))


class Halving:
    def __init__(self, keep, send, dp, turn):
        self.dp = dp
        self.axes = axes_of(dp)
        self.left = order_of(dp, turn)
        self.rest = 2 * keep.shape[0] >> len(self.axes)
        self.keep = keep
        self.sent = send

    def send(self):
        axis = self.left[0]
        where = self.axes.index(axis)
        columns = self.part.shape[1]
        many = len(self.axes) - where - 1
        pairs = self.part.reshape(1 << where, 2, self.rest << many, columns)
        side = side_of(axis)
        self.sent = lax.dynamic_index_in_dim(pairs, 1 - side, 1, keepdims=False)
        self.keep = lax.dynamic_index_in_dim(pairs, side, 1, keepdims=False)
        return self.sent

    def go(self):
        self.come = trade(self.sent, self.left[0], self.dp)

    def add(self, earlier=None):
        come = self.come if earlier is None else after(self.come, earlier)
        total = (self.keep.astype(F32) + come.astype(F32)).astype(BF)
        self.part = total.reshape(-1, total.shape[-1])
        self.axes.remove(self.left.pop(0))
        if self.left:
            self.send()


def finish(many):
    while any(one.left for one in many):
        active = [one for one in many if one.left]
        for one in active:
            one.go()
        for one, come in zip(active, lax.optimization_barrier([one.come for one in active])):
            one.come = come
            one.add()
    return [one.part for one in many]


def split_core(total, dp):
    groups = total.reshape(dp, 2, total.shape[0] // (2 * dp), total.shape[1])
    side = side_of(0)
    keep = lax.dynamic_index_in_dim(groups, side, 1, keepdims=False)
    send = lax.dynamic_index_in_dim(groups, 1 - side, 1, keepdims=False)
    return [one.reshape(total.shape[0] // 2, total.shape[1]) for one in (keep, send)]


def gather_steps(local, dp, turn, earlier):
    axes = axes_of(dp)
    done = []
    part = local
    for axis in reversed(order_of(dp, turn)):
        if axis == "tensor":
            part = after(part, earlier)
        come = trade(part, axis, dp)
        low = side_of(axis) == 0
        done = [one for one in axes if one == axis or one in done]
        lead = 1 << done.index(axis)
        pair = [jnp.where(low, part, come), jnp.where(low, come, part)]
        pair = [one.reshape(lead, part.shape[0] // lead, part.shape[1]) for one in pair]
        part = jnp.stack(pair, axis=1).reshape(2 * part.shape[0], part.shape[1])
    return part


def after(values, earlier):
    return lax.optimization_barrier((values, earlier))[0]


def whole_sequence_body(
    tokens_in,
    piece_starts,
    cotangent,
    gain_tokens,
    gain_mlp,
    gain_state,
    gate_bias,
    w_query,
    w_key,
    w_value,
    w_out,
    w_state_query,
    w_state_key,
    w_state_value,
    w_state_out,
    w_gate,
    w_up,
    w_down,
    state_init,
):
    mine = lax.axis_index("tensor")
    first = mine == 0
    local_rows = w_query.shape[0]
    dp = D // local_rows
    width = w_query.shape[1]
    units = 512
    across = w_up.shape[1] // units
    swap = [(0, 1), (1, 0)]

    def half_of(pair):
        return jnp.where(first, pair[1, 0], pair[0, 0])

    def bring(pair, come):
        keep = jnp.where(first, pair[0, 0], pair[1, 0])
        top = jnp.where(first, keep, come)
        low = jnp.where(first, come, keep)
        return jnp.concatenate([top, low], axis=1).reshape(NB * W, D)

    def give(rows, later=None):
        halves = rows.reshape(NB, 2, HALF, D)
        keep = jnp.where(first, halves[:, 0], halves[:, 1])
        send = jnp.where(first, halves[:, 1], halves[:, 0])
        come = lax.ppermute(send, "tensor", swap)
        if later is not None:
            come = after(come, later)
        return jnp.stack([jnp.where(first, keep, come), jnp.where(first, come, keep)])[:, None]

    def split_init(values):
        side = values.shape[1] // 2
        return jnp.concatenate([values[:, :side], values[:, side:]], axis=0)

    gains = jnp.stack([gain_tokens, gain_mlp, gain_state, gate_bias])
    small = jnp.concatenate(
        [split_init(state_init), jnp.pad(gains, ((0, local_rows - 4), (0, 128 - local_rows)))],
        axis=1,
    )
    full_qkv = gather(
        jnp.concatenate([w_query, w_key, w_value, w_state_query, w_state_key, small], axis=1)
    )
    full_small = full_qkv[:, 5 * width :]
    turned_down = w_down.T
    late = []
    for unit in range(0, across * units, units):
        late += [w_up[:, unit : unit + units], turned_down[:, unit : unit + units]]
    late = jnp.concatenate(late + [w_out.T], axis=1)
    rows = bring(tokens_in, lax.ppermute(half_of(tokens_in), "tensor", swap))
    cot_send = half_of(cotangent)
    full_state1 = gather_steps(
        jnp.concatenate([w_state_value, w_gate, w_state_out.T], axis=1), dp, False, (rows, late, cot_send)
    )
    full_late = gather(after(late, (full_qkv, full_state1)))
    side = width // 2
    init = full_small[:, :side].reshape(2, dp, 2, local_rows // 2, side)
    init = jnp.transpose(init, (1, 3, 0, 2, 4)).reshape(S, D)
    gains = full_small[:D, side:].reshape(dp, local_rows, 128)[:, :4, :local_rows]
    gains = jnp.transpose(gains, (1, 0, 2)).reshape(4, 1, D).astype(F32)

    cot_half = lax.ppermute(after(cot_send, full_qkv), "tensor", swap)
    starts = jnp.where(first, piece_starts[0, 0], piece_starts[1, 0])
    flags = jnp.any(
        starts[:, None] == PIECE * jnp.arange(NB * W // PIECE, dtype=jnp.int32)[None], axis=0
    ).astype(jnp.int32)

    turned, query, key, value = project(rows, gains[0], full_qkv)
    (
        token_mixed,
        state_mixed,
        state_turned,
        state_query,
        state_key,
        state_value,
        state_in,
        forget,
        apart,
        totals,
    ) = forward(flags, query, key, value, init, gains[2], gains[3], full_qkv, full_state1)
    cot = bring(cotangent, after(cot_half, token_mixed))
    middle, mlp_in, mlp_turned, cot_turned = middle_rows(
        rows, token_mixed, full_late, gains[1], cot
    )
    mlp_out, grad_mlp_in, grad_mlp_w = mlp(mlp_in, mlp_turned, cot, cot_turned, full_late)
    output, grad_middle, middle_turned, grad_mixed, grad_gain_mlp = after_mlp(
        middle, mlp_out, grad_mlp_in, cot, gains[1], full_late
    )
    grads_late = whole_weight_grad(middle_turned, token_mixed, grad_mlp_w)
    part_late = scatter(grads_late)
    core = (side_of(0) & 1).astype(jnp.int32).reshape(1)
    grad_tok, grad_sta, branch, grad_init, grad_gain_state, grad_bias = backward(
        flags,
        query,
        key,
        value,
        state_query,
        state_key,
        state_value,
        token_mixed,
        state_mixed,
        after(grad_mixed, grads_late),
        totals,
        forget,
        state_in,
        apart,
        gains[2],
        full_qkv,
        full_state1,
    )
    given_output = give(output, grad_tok)

    a = Halving(*weight_grads(dp, core, state_turned, after(grad_sta, given_output), 0, 2), dp, False)
    a.go()
    b = Halving(*weight_grads(dp, core, state_turned, after(grad_sta, a.sent), 2, 2), dp, True)
    a.add(b.keep)
    a.go()
    b.go()
    c = Halving(*weight_grads(dp, core, turned, after(grad_tok, (a.sent, b.sent)), 1, 2), dp, False)
    b.add(c.keep)
    b.go()
    c.go()
    grads_q = weight_grads(dp, core, turned, after(grad_tok, (b.sent, c.sent)), 0, 1, 2, 0)
    c.add(grads_q)
    c.go()
    d = Halving(
        *weight_grads(dp, core, after(branch, c.sent), state_mixed[None], 0, 1, 2, 1, grads_q),
        dp,
        True,
    )
    d.go()
    grad_in, grad_gain_tokens = token_grad(
        after(grad_tok, (d.sent, part_late)), full_qkv, rows, grad_middle, gains[0]
    )
    a.add(grad_in)
    d.add(grad_in)
    b.add(grad_in)
    init_parts = jnp.transpose(
        grad_init.reshape(dp, local_rows // 2, 2, 2, side), (2, 0, 3, 1, 4)
    ).reshape(2 * D, side)
    gain_parts = jnp.stack(
        [grad_gain_tokens[0], grad_gain_mlp[0], grad_gain_state[0], grad_bias[0]]
    ).reshape(4, dp, local_rows)
    gain_parts = jnp.pad(
        jnp.transpose(gain_parts, (1, 0, 2)),
        ((0, 0), (0, local_rows - 4), (0, 128 - local_rows)),
    ).reshape(D, 128)
    gain_parts = jnp.concatenate([gain_parts, gain_parts], axis=0).astype(BF)
    e = Halving(*split_core(jnp.concatenate([init_parts, gain_parts], axis=1), dp), dp, True)
    given_grad = give(grad_in)
    part_rest, part_kv, part_sqk, part_svg, part_small = [
        one.astype(F32) for one in finish([d, c, a, b, e])
    ]
    part_so = part_rest[:, width:]
    part_init = part_small[:, :side]
    part_init = jnp.concatenate(
        [part_init[: local_rows // 2], part_init[local_rows // 2 :]], axis=1
    )
    part_gains = part_small[:4, side : side + local_rows]
    part_late = part_late.astype(F32)
    part_up = [part_late[:, 2 * i * units : (2 * i + 1) * units] for i in range(across)]
    part_down = [part_late[:, (2 * i + 1) * units : (2 * i + 2) * units] for i in range(across)]
    part_sqk = part_sqk.astype(F32)
    part_svg = part_svg.astype(F32)
    return (
        given_output,
        given_grad,
        part_gains[0],
        part_gains[1],
        part_gains[2],
        part_gains[3],
        part_rest[:, :width],
        part_kv[:, :width],
        part_kv[:, width:],
        part_late[:, 2 * across * units :].T,
        part_sqk[:, :width],
        part_sqk[:, width:],
        part_svg[:, :width],
        part_so.T,
        part_svg[:, width:],
        jnp.concatenate(part_up, axis=1),
        jnp.concatenate([one.T for one in part_down], axis=0),
        part_init,
    )


def solution(mesh):
    dp = mesh.shape["dp"]
    one_each = mesh.shape["tensor"] == MICRO and dp > 1 and dp & (dp - 1) == 0
    return jax.shard_map(
        whole_sequence_body if one_each else generic_body,
        mesh=mesh,
        in_specs=(
            P(None, "dp", None, "tensor", None),
            P(None, "dp", None),
            P(None, "dp", None, "tensor", None),
            P("dp"),
            P("dp"),
            P("dp"),
            P("dp"),
            P("dp", "tensor"),
            P("dp", "tensor"),
            P("dp", "tensor"),
            P("tensor", "dp"),
            P("dp", "tensor"),
            P("dp", "tensor"),
            P("dp", "tensor"),
            P("tensor", "dp"),
            P("dp", "tensor"),
            P("dp", "tensor"),
            P("tensor", "dp"),
            P("dp", "tensor"),
        ),
        out_specs=(
            P(None, "dp", None, "tensor", None),
            P(None, "dp", None, "tensor", None),
            P("dp"),
            P("dp"),
            P("dp"),
            P("dp"),
            P("dp", "tensor"),
            P("dp", "tensor"),
            P("dp", "tensor"),
            P("tensor", "dp"),
            P("dp", "tensor"),
            P("dp", "tensor"),
            P("dp", "tensor"),
            P("tensor", "dp"),
            P("dp", "tensor"),
            P("dp", "tensor"),
            P("tensor", "dp"),
            P("dp", "tensor"),
        ),
        check_vma=False,
    )
```
